128 devices in a mesh: row: 32 (over z, y, core), col: 4 (over x).
Axes of the slice: x: 4, y: 4, z: 4, core: 2. Of those that a mesh axis runs over, the one named last changes fastest.
Arguments:
- snapshots: float32 [131072, 2048], P('row', 'col'), may hold values from -36 to 36, as said below
- tiles: int32 [256, 16], P('row', 'col'), may hold values 0 or 1
Outputs:
- factors: float32 [2, 256, 256], replicated
- reduced: float32 [131072, 2048], P('row', 'col')
The draws below stay inside these ranges and needn't reach their ends.
Inputs may be any that keep to these rules, and one draw needn't show every extreme that they name: `snapshots`: the snapshot entries lie within this range.
All inputs are finite; a program needn't handle non-finite values. No bound on the sum of `tiles` on one device may be relied on, other than what follows from the above.
Results may differ from the reference program's by a relative error of at most 0.00011.
Values sent between devices are 32-bit elements; how exact they have to be, the bound alone decides.
No kernel may reach another device: no remote copies, remote signals or barrier semaphores. Data moves between devices by JAX's collectives and lax.ppermute only.
A program may use at most 128 MiB of HBM per device.

```python
import math
import jax
import jax.numpy as jnp
from jax import lax

PW = 256
PANELS = 2
TILE_ROWS = 512
TILE_COLS = 128
ROWS = 131072
NCOL = 2048


def draw_snapshots(key, part):
    key = jax.random.fold_in(key, 11)
    key_base, key_rows, key_cols = jax.random.split(key, 3)
    row_scale = 0.3 * jnp.exp(jax.random.uniform(key_rows, (ROWS, 1), jnp.float32) * math.log(10.0))
    base = jnp.clip(jax.random.normal(key_base, (ROWS, NCOL), jnp.float32), -4.0, 4.0)
    col_scale = 0.5 * jnp.exp(jax.random.uniform(key_cols, (1, NCOL), jnp.float32) * math.log(4.0))
    return (base * row_scale * col_scale).astype(jnp.float32)


def touch_ends(array, rng, least, top_value):
    index_at = [jax.random.randint(jax.random.fold_in(rng, axis), (), 0, length) for axis, length in enumerate(array.shape)]
    widest = array.shape.index(max(array.shape))
    neighbour = index_at[:widest] + [(index_at[widest] + 1) % array.shape[widest]] + index_at[widest + 1:]
    return array.at[tuple(index_at)].set(least).at[tuple(neighbour)].set(top_value)


def setup_inputs(seed: int = 0) -> dict:
    seeds = jax.random.split(jax.random.key(seed), 3)
    snapshots = draw_snapshots(jax.random.fold_in(seeds[2], 71), 0)
    tiles = touch_ends((jax.random.randint(seeds[1], (ROWS // TILE_ROWS, NCOL // TILE_COLS), 0, 2) < 1).astype(jnp.int32), jax.random.fold_in(seeds[1], 1), 0, 1)
    return {"snapshots": snapshots, "tiles": tiles}


def chol_solve(lower, right):
    first = lax.linalg.triangular_solve(lower, right, left_side=True, lower=True)
    return lax.linalg.triangular_solve(lower, first, left_side=True, lower=True, transpose_a=True)

def right_solve(lower, panel):
    return lax.linalg.triangular_solve(lower, panel, left_side=False, lower=True, transpose_a=True)

def reference(snapshots, tiles):
    total_rows, total_cols = snapshots.shape
    occupancy = tiles.astype(jnp.float32)
    row_tiles = total_rows // TILE_ROWS
    col_tiles = total_cols // TILE_COLS
    work = (snapshots.reshape(row_tiles, TILE_ROWS, col_tiles, TILE_COLS) * occupancy[:, None, :, None]).reshape(total_rows, total_cols)
    factor_list = []
    for panel_index in range(PANELS):
        start = panel_index * PW
        panel = work[:, start:start + PW]
        gram = jnp.einsum('rp,rq->pq', panel, panel, precision=lax.Precision.HIGHEST)
        lower = jnp.linalg.cholesky(gram)
        trailing = work[:, start:]
        proj = jnp.einsum('rp,rc->pc', panel, trailing, precision=lax.Precision.HIGHEST)
        solved = chol_solve(lower, proj)
        updated = trailing - jnp.dot(panel.astype(jnp.float32), solved.astype(jnp.float32), precision=lax.Precision.HIGHEST, preferred_element_type=jnp.float32)
        q_block = right_solve(lower, panel) * jnp.float32(math.sqrt(total_rows))
        updated = updated.at[:, 0:PW].set(q_block)
        work = jnp.concatenate([work[:, :start], updated], axis=1)
        factor_list.append(lower.T)
    return (jnp.stack(factor_list), work)
```

```python
import functools
import math

import jax
import jax.numpy as jnp
from jax import lax
from jax.experimental import pallas as pl
from jax.experimental.pallas import tpu as pltpu
from jax.sharding import PartitionSpec as P

TH = 512
TW = 128
TI = 8
TJ = 4
SLOTS = TI * TJ
PAIR = 2
LAG = 2
CHUNKS = SLOTS // PAIR
W = TJ * TW
F32 = jnp.float32
CHEAP = pl.CostEstimate(flops=1024, bytes_accessed=1024, transcendentals=0)
BF16 = jnp.bfloat16


def params(limit=57):
    return pltpu.CompilerParams(vmem_limit_bytes=limit * 1024 * 1024)


def sds(shape, dtype):
    return jax.ShapeDtypeStruct(shape, dtype)


def site(r):
    return r // 8, (r // 2) % 4, r % 2


def row_of(z, y, c):
    return (z % 4) * 8 + (y % 4) * 2 + c


def row_perm(f):
    return [(r, row_of(*f(*site(r)))) for r in range(32)]


SWAP = row_perm(lambda z, y, c: (z, y, 1 - c))
SHIFT = {
    "y": [row_perm(lambda z, y, c, d=d: (z, y + d, c)) for d in range(4)],
    "z": [row_perm(lambda z, y, c, d=d: (z + d, y, c)) for d in range(4)],
}
RING = [(r * 4 + x, r * 4 + (x + (1 if r % 2 == 0 else 3)) % 4) for r in range(32) for x in range(4)]


def ring_step(x):
    return lax.ppermute(x, ("row", "col"), RING)


def scatter4(x, axis, me):
    h = x.shape[0] // 4
    total = lax.dynamic_slice_in_dim(x, me * h, h, 0)
    for d in (1, 3, 2):
        part = lax.dynamic_slice_in_dim(x, lax.rem(me + d, 4) * h, h, 0)
        total = total + lax.ppermute(part, "row", SHIFT[axis][d])
    return total


def gather4(x, axis, me):
    h = x.shape[0]
    out = jnp.zeros((4 * h, x.shape[1]), x.dtype)
    for d in range(4):
        got = x if d == 0 else lax.ppermute(x, "row", SHIFT[axis][d])
        out = lax.dynamic_update_slice_in_dim(out, got, lax.rem(me + 4 - d, 4) * h, 0)
    return out


def core_scatter(x, c):
    h = x.shape[0] // 2
    mine = lax.dynamic_slice_in_dim(x, c * h, h, 0)
    other = lax.dynamic_slice_in_dim(x, (1 - c) * h, h, 0)
    return mine + lax.ppermute(other, "row", SWAP)


def core_gather(x, c):
    got = lax.ppermute(x, "row", SWAP)
    first = jnp.where(c == 0, x, got)
    second = jnp.where(c == 0, got, x)
    return jnp.concatenate([first, second], 0)


def row_sum(x):
    z, y, c = site(lax.axis_index("row"))
    v = core_scatter(x, c)
    v = scatter4(v, "y", y)
    v = scatter4(v, "z", z)
    v = gather4(v, "z", z)
    v = gather4(v, "y", y)
    return core_gather(v, c)


def shifted(x, axis):
    if axis == "col":
        return [lax.ppermute(x, "col", [(i, (i + d) % 4) for i in range(4)]) for d in (1, 2, 3)]
    return [lax.ppermute(x, "row", SHIFT[axis][d]) for d in (1, 2, 3)]


HBM = pl.BlockSpec(memory_space=pltpu.HBM)
VMEM = pl.BlockSpec(memory_space=pltpu.VMEM)
SMEM = pl.BlockSpec(memory_space=pltpu.SMEM)
ROOT, HOP, CORE, ZPOS, COL = range(5)
UPPER = [(i, j) for i in range(TJ) for j in range(i, TJ)]
HALF = len(UPPER) // 2 * TW
QUARTER = HALF // 4


def split(x):
    high = x.astype(BF16)
    return high, (x - high.astype(F32)).astype(BF16)


def dot(a, b):
    return jnp.dot(a, b, preferred_element_type=F32)


def hdot(a, b, dims):
    return lax.dot_general(a, b, (dims, ((), ())), precision=lax.Precision.HIGHEST, preferred_element_type=F32)


def call(body, ins, outs, shapes, name, scratch=(), aliases=None):
    return pl.pallas_call(
        body,
        in_specs=ins,
        out_specs=outs,
        out_shape=shapes,
        scratch_shapes=list(scratch),
        input_output_aliases=aliases or {},
        compiler_params=params(),
        cost_estimate=CHEAP,
        name=name,
    )


def find(panel, wanted):
    seen, place, found = jnp.int32(0), jnp.int32(0), jnp.int32(0)
    for t in range(SLOTS):
        full = panel[t % TI, t // TI]
        hit = jnp.where((full > 0) & (seen == wanted), 1, 0)
        place += hit * t
        found += hit
        seen += full
    return place, found > 0


def relay_body(step, last, fresh, me, panel, x_ref, *refs):
    refs = list(refs)
    got = None if step < LAG else refs.pop(0)
    if not fresh:
        refs.pop(0)
    filed = refs.pop(0)
    send = None if last else refs.pop(0)
    sem = refs.pop(0)
    root = me[ROOT] > 0
    chunk = step - me[HOP] * LAG

    def each(act):
        for e in range(PAIR):
            place, found = find(panel, chunk * PAIR + e)
            found = found & (chunk >= 0)
            rows = pl.ds(pl.multiple_of((place % TI) * TH, TH), TH)
            cols = pl.ds(pl.multiple_of((place // TI) * TW, TW), TW)
            part = pl.ds(e * TH, TH)

            def move(src, e=e, rows=rows, cols=cols, part=part):
                act(pltpu.make_async_copy(src, filed.at[rows, cols], sem.at[2 * e]))
                if send is not None:
                    act(pltpu.make_async_copy(src, send.at[part, :], sem.at[2 * e + 1]))

            @pl.when(found & root)
            def _(move=move, rows=rows, cols=cols):
                move(x_ref.at[rows, cols])

            if got is not None:

                @pl.when(found & jnp.logical_not(root))
                def _(move=move, part=part):
                    move(got.at[part, :])

    each(lambda c: c.start())
    each(lambda c: c.wait())


def relay(step, last, me, panel, x, got, filed):
    ins, args = [SMEM, SMEM, HBM], [me, panel, x]
    if step >= LAG:
        ins.append(HBM)
        args.append(got)
    aliases = {}
    if filed is not None:
        aliases = {len(args): 0}
        ins.append(HBM)
        args.append(filed)
    shapes = [sds((TI * TH, W), F32)]
    if not last:
        shapes.append(sds((PAIR * TH, TW), F32))
    out = call(
        functools.partial(relay_body, step, last, filed is None),
        ins,
        [HBM] * len(shapes),
        shapes,
        "relay",
        [pltpu.SemaphoreType.DMA((2 * PAIR,))],
        aliases,
    )(*args)
    return out if not last else (out[0], None)


def gram_body(me, occ, x_ref, filed_in, keep, give, filed, gram_ref, cross_ref):
    i = pl.program_id(0)

    @pl.when(i == 0)
    def _():
        gram_ref[...] = jnp.zeros_like(gram_ref)
        cross_ref[...] = jnp.zeros_like(cross_ref)

    @pl.when(me[ROOT] > 0)
    def _():
        x = jnp.concatenate([x_ref[:, j * TW : (j + 1) * TW] * occ[i, j].astype(F32) for j in range(TJ)], 1)
        high, low = split(x)
        h = W // 2
        high_t, low_t = high.T, low.T
        gram_ref[:h, :] += dot(high_t[:h], high) + dot(low_t[:h], low)
        gram_ref[h:, h:] += dot(high_t[h:], high[:, h:]) + dot(low_t[h:], low[:, h:])
        cross_ref[...] += dot(high_t, low)

    @pl.when(i == TI - 1)
    def _():
        for b, (r, q) in enumerate(UPPER):
            rows, cols = slice(r * TW, (r + 1) * TW), slice(q * TW, (q + 1) * TW)
            block = gram_ref[rows, cols] + cross_ref[rows, cols] + cross_ref[cols, rows].T
            part, at = divmod(b * TW, HALF)
            mine = me[CORE] == part

            @pl.when(mine)
            def _(block=block, at=at):
                keep[at : at + TW, :] = block

            @pl.when(jnp.logical_not(mine))
            def _(block=block, at=at):
                give[at : at + TW, :] = block


def gram_part(me, occ, x, filed):
    whole = pl.BlockSpec((HALF, TW), lambda i, *_: (0, 0))
    return pl.pallas_call(
        gram_body,
        grid_spec=pltpu.PrefetchScalarGridSpec(
            num_scalar_prefetch=2,
            grid=(TI,),
            in_specs=[pl.BlockSpec((TH, W), lambda i, me, occ: (i * me[ROOT], 0)), HBM],
            out_specs=[whole, whole, HBM],
            scratch_shapes=[pltpu.VMEM((W, W), F32), pltpu.VMEM((W, W), F32)],
        ),
        out_shape=[sds((HALF, TW), F32), sds((HALF, TW), F32), sds(filed.shape, F32)],
        input_output_aliases={3: 2},
        compiler_params=params(),
        cost_estimate=CHEAP,
        name="gram_part",
    )(me, occ, x, filed)


def add_body(*refs):
    ins, (_, out, _) = refs[:-3], refs[-3:]
    total = ins[0][...]
    for r in ins[1:]:
        total = total + r[...]
    out[...] = total


def add_parts(parts, filed):
    n = len(parts)
    return call(
        add_body,
        [VMEM] * n + [HBM],
        [VMEM, HBM],
        [sds(parts[0].shape, F32), sds(filed.shape, F32)],
        "add_parts",
        aliases={n: 1},
    )(*parts, filed)


def add_cut_body(me, a, b, c, d, _, own, one, two, three, __, total):
    total[...] = a[...] + b[...] + c[...] + d[...]
    for k, out in enumerate((own, one, two, three)):
        at = lax.rem(me[ZPOS] + k, 4) * QUARTER
        out[...] = total[pl.ds(pl.multiple_of(at, 8), QUARTER), :]


def add_cut(me, parts, filed):
    return call(
        add_cut_body,
        [SMEM] + [VMEM] * 4 + [HBM],
        [VMEM] * 4 + [HBM],
        [sds((QUARTER, TW), F32)] * 4 + [sds(filed.shape, F32)],
        "add_cut",
        [pltpu.VMEM((HALF, TW), F32)],
        {5: 4},
    )(me, *parts, filed)


def choose_body(me, a, b, c, d, _, out, __):
    for k, ref in enumerate((a, b, c, d)):

        @pl.when(me[COL] == k)
        def _(ref=ref):
            out[...] = ref[...]


def choose(me, parts, filed):
    return call(
        choose_body,
        [SMEM] + [VMEM] * 4 + [HBM],
        [VMEM, HBM],
        [sds((QUARTER, TW), F32), sds(filed.shape, F32)],
        "choose",
        aliases={5: 1},
    )(me, *parts, filed)


def stack_body(me, a, b, c, d, _, out, __):
    for k, ref in enumerate((a, b, c, d)):
        at = lax.rem(me[ZPOS] + 4 - k, 4) * QUARTER
        out[pl.ds(pl.multiple_of(at, 8), QUARTER), :] = ref[...]


def stack(me, parts, filed):
    return call(
        stack_body,
        [SMEM] + [VMEM] * 4 + [HBM],
        [VMEM, HBM],
        [sds((HALF, TW), F32), sds(filed.shape, F32)],
        "stack",
        aliases={5: 1},
    )(me, *parts, filed)


def unpack_body(me, mine, other, _, s_ref, e_ref, __):
    s_ref[...] = jnp.zeros_like(s_ref)
    for b, (r, q) in enumerate(UPPER):
        part, at = divmod(b * TW, HALF)
        block = jnp.where(me[CORE] == part, mine[at : at + TW, :], other[at : at + TW, :])
        s_ref[r * TW : (r + 1) * TW, q * TW : (q + 1) * TW] = block
        if b == 0:
            e_ref[:, :TW] = block
    e_ref[:, TW:] = unit()


def unpack(me, mine, other, filed):
    return call(
        unpack_body,
        [SMEM, VMEM, VMEM, HBM],
        [VMEM, VMEM, HBM],
        [sds((W, W), F32), sds((TW, 2 * TW), F32), sds(filed.shape, F32)],
        "unpack",
        aliases={3: 2},
    )(me, mine, other, filed)


def unit():
    r = lax.broadcasted_iota(jnp.int32, (TW, TW), 0)
    c = lax.broadcasted_iota(jnp.int32, (TW, TW), 1)
    return jnp.where(r == c, 1.0, 0.0).astype(F32)


def eliminate(m_rows, v_rows, start, stop):
    groups = len(m_rows)
    full = (8, m_rows[0].shape[1])
    sub = lax.broadcasted_iota(jnp.int32, full, 0)

    def row(x, r):
        return jnp.broadcast_to(x[r : r + 1, :], full)

    for g in range(start, stop):
        lanes = [8 * g + k for k in range(8)]
        columns = [jnp.broadcast_to(m_rows[g][:, lane : lane + 1], full) for lane in lanes]
        a = {(r, k): row(columns[k], r) for k in range(8) for r in range(k, 8)}
        rm = [row(m_rows[g], r) for r in range(8)]
        rv = [row(v_rows[g], r) for r in range(8)]
        inverse = []
        for k in range(8):
            scale = lax.rsqrt(a[k, k])
            inverse.append(scale)
            for r in range(k + 1, 8):
                a[r, k] = a[r, k] * scale
            for c in range(k + 1, 8):
                for r in range(c, 8):
                    a[r, c] = a[r, c] - a[r, k] * a[c, k]
            rm[k] = rm[k] * scale
            rv[k] = rv[k] * scale
            for r in range(k + 1, 8):
                rm[r] = rm[r] - a[r, k] * rm[k]
                rv[r] = rv[r] - a[r, k] * rv[k]
        for i in range(g + 1, groups):
            factor = [jnp.broadcast_to(m_rows[i][:, lane : lane + 1], full) for lane in lanes]
            new_m, new_v = m_rows[i], v_rows[i]
            for k in range(8):
                factor[k] = factor[k] * inverse[k]
                for r in range(k + 1, 8):
                    factor[r] = factor[r] - factor[k] * a[r, k]
                new_m = new_m - factor[k] * rm[k]
                new_v = new_v - factor[k] * rv[k]
            m_rows[i], v_rows[i] = new_m, new_v
        top_m, top_v = rm[0], rv[0]
        for r in range(1, 8):
            top_m = jnp.where(sub == r, rm[r], top_m)
            top_v = jnp.where(sub == r, rv[r], top_v)
        m_rows[g], v_rows[g] = top_m, top_v
    return m_rows, v_rows


def eliminate_body(e_in, _, e_out, __):
    groups = range(TW // 8)
    m_rows = [e_in[8 * g : 8 * g + 8, :TW] for g in groups]
    v_rows = [e_in[8 * g : 8 * g + 8, TW:] for g in groups]
    m_rows, v_rows = eliminate(m_rows, v_rows, 0, TW // 8)
    r = lax.broadcasted_iota(jnp.int32, (8, TW), 0)
    c = lax.broadcasted_iota(jnp.int32, (8, TW), 1)
    for g in groups:
        e_out[8 * g : 8 * g + 8, :TW] = jnp.where(r + 8 * g <= c, m_rows[g], 0.0)
        e_out[8 * g : 8 * g + 8, TW:] = v_rows[g]


def eliminate_block(e, filed):
    return call(
        eliminate_body,
        [VMEM, HBM],
        [VMEM, HBM],
        [sds((TW, 2 * TW), F32), sds(filed.shape, F32)],
        "eliminate",
        aliases={1: 1},
    )(e, filed)


def spread_body(b, e_in, s_in, v_in, _, s_ref, v_ref, e_out, __):
    lo, hi = b * TW, (b + 1) * TW
    s_ref[...] = s_in[...]
    if b == 0:
        v_ref[...] = jnp.zeros_like(v_ref)
    else:
        v_ref[...] = v_in[...]
    inv = e_in[:, TW:]
    s_ref[lo:hi, lo:hi] = e_in[:, :TW]
    v_ref[lo:hi, lo:hi] = inv
    if b > 0:
        v_ref[lo:hi, :lo] = hdot(inv, v_in[lo:hi, :lo], ((1,), (0,)))
    if hi < W:
        right = hdot(inv, s_in[lo:hi, hi:], ((1,), (0,)))
        s_ref[lo:hi, hi:] = right
        s_ref[hi:, hi:] -= hdot(right, right, ((0,), (0,)))
        s_ref[hi:, lo:hi] = jnp.zeros((W - hi, TW), F32)
        v_ref[hi:, :hi] -= hdot(right, v_ref[lo:hi, :hi], ((0,), (0,)))
        e_out[:, :TW] = s_ref[hi : hi + TW, hi : hi + TW]
        e_out[:, TW:] = unit()
    else:
        e_out[...] = e_in[...]


def spread(b, e, s, v, filed):
    return call(
        functools.partial(spread_body, b),
        [VMEM] * 3 + [HBM],
        [VMEM] * 3 + [HBM],
        [sds((W, W), F32), sds((W, W), F32), sds((TW, 2 * TW), F32), sds(filed.shape, F32)],
        "spread",
        aliases={4 - 1: 3},
    )(e, s, v, filed)


def masked(ref, flags, i, upto=TJ):
    parts = []
    for j in range(upto):
        block = ref[:, j * TW : (j + 1) * TW]
        parts.append(jnp.where(flags[i, j] > 0, block, jnp.zeros_like(block)))
    return jnp.concatenate(parts, 1)


def project_body(me, occ, panel, x_ref, a_ref, c_ref):
    i = pl.program_id(0)

    @pl.when(i == 0)
    def _():
        c_ref[...] = jnp.zeros_like(c_ref)

    @pl.when(me[ROOT] == 0)
    def _():
        ah, al = split(masked(a_ref, panel, i))
        bh, bl = split(masked(x_ref, occ, i))
        ah_t, al_t = ah.T, al.T
        c_ref[...] += dot(ah_t, bh) + dot(al_t, bh) + dot(ah_t, bl)


def project(me, occ, panel, x, filed):
    block = pl.BlockSpec((TH, W), lambda i, *_: (i, 0))
    return pl.pallas_call(
        project_body,
        grid_spec=pltpu.PrefetchScalarGridSpec(
            num_scalar_prefetch=3,
            grid=(TI,),
            in_specs=[block, block],
            out_specs=pl.BlockSpec((W, W), lambda i, *_: (0, 0)),
        ),
        out_shape=sds((W, W), F32),
        compiler_params=params(),
        cost_estimate=CHEAP,
        name="project",
    )(me, occ, panel, x, filed)


def finish_body(me, occ, panel, x_ref, a_ref, xh, xl, out_ref):
    i = pl.program_id(0)
    keep = 1 - me[ROOT]
    ah, al = split(masked(a_ref, panel, i))
    taken = dot(ah, xh[...]) + dot(ah, xl[...]) + dot(al, xh[...])
    for j in range(TJ):
        at = slice(j * TW, (j + 1) * TW)
        out_ref[:, at] = x_ref[:, at] * (occ[i, j] * keep).astype(F32) - taken[:, at]


def finish(me, occ, panel, x, filed, xh, xl):
    rows = TI * TH
    block = pl.BlockSpec((TH, W), lambda i, *_: (i, 0))
    whole = pl.BlockSpec((W, W), lambda i, *_: (0, 0))
    return pl.pallas_call(
        finish_body,
        grid_spec=pltpu.PrefetchScalarGridSpec(
            num_scalar_prefetch=3,
            grid=(TI,),
            in_specs=[block, block, whole, whole],
            out_specs=block,
        ),
        out_shape=sds((rows, W), F32),
        compiler_params=params(),
        cost_estimate=CHEAP,
        name="finish",
    )(me, occ, panel, x, filed, xh, xl)


def shards(snapshots, tiles):
    col = lax.axis_index("col")
    z, _, core = site(lax.axis_index("row"))
    root = col == 0
    hop = jnp.where(core == 0, col, (4 - col) % 4)
    total_rows = snapshots.shape[0] * lax.axis_size("row")
    scale = jnp.float32(math.sqrt(total_rows))
    me = jnp.stack([root.astype(jnp.int32), hop, core, z, col]).astype(jnp.int32)

    steps = CHUNKS + 3 * LAG
    panels, passed = [tiles], tiles
    for h in range(1, 4):
        passed = ring_step(passed)
        panels.append(jnp.where(hop == h, passed, panels[-1]))
    panel = panels[3]

    got = [None] * LAG
    filed = None
    state = {}

    def gram_stage(name):
        nonlocal filed
        if name == "parts":
            keep, give, filed = gram_part(me, tiles, snapshots, filed)
            state["v"] = [keep, lax.ppermute(give, "row", SWAP)]
        elif name == "core":
            v, filed = add_parts(state["v"], filed)
            state["v"] = [v] + shifted(v, "y")
        elif name == "y":
            own, one, two, three, filed = add_cut(me, state["v"], filed)
            sent = [lax.ppermute(p, "row", SHIFT["z"][d]) for d, p in ((1, one), (2, two), (3, three))]
            state["v"] = [own] + sent
        elif name == "z":
            v, filed = add_parts(state["v"], filed)
            state["v"] = [v] + shifted(v, "col")
        elif name == "col":
            v, filed = choose(me, state["v"], filed)
            state["v"] = [v] + shifted(v, "z")
        elif name == "stack":
            v, filed = stack(me, state["v"], filed)
            state["v"] = [v, lax.ppermute(v, "row", SWAP)]
        elif name == "unpack":
            state["s"], state["e"], filed = unpack(me, *state["v"], filed)
            state["inv"] = state["s"]
        elif name[0] == "e":
            state["e"], filed = eliminate_block(state["e"], filed)
        else:
            state["s"], state["inv"], state["e"], filed = spread(int(name[1]), state["e"], state["s"], state["inv"], filed)

    plan = {1: ["parts"], 2: ["core"], 4: ["y"], 6: ["z"], 7: ["col"], 9: ["stack"], 10: ["unpack"]}
    for b in range(TJ):
        plan[11 + 2 * b] = [f"e{b}"]
        plan[12 + 2 * b] = [f"s{b}"]

    for s in range(steps):
        last = s >= steps - LAG
        filed, send = relay(s, last, me, panels[min(s // LAG, 3)], snapshots, got[s % LAG], filed)
        if not last:
            got[s % LAG] = ring_step(send)
        for name in plan.get(s, []):
            gram_stage(name)

    proj = row_sum(project(me, tiles, panel, snapshots, filed))
    inv = state["inv"]
    mid = jnp.dot(inv, proj, precision=lax.Precision.HIGHEST)
    coef = jnp.dot(inv.T, mid, precision=lax.Precision.HIGHEST)
    coef = jnp.where(root, -scale * inv.T, coef)
    xh = lax.reduce_precision(coef, 8, 7)
    xl = (coef - xh).astype(BF16)
    out = finish(me, tiles, panel, snapshots, filed, xh.astype(BF16), xl)
    half = W // 2
    upper = state["s"]
    factors = jnp.stack([upper[:half, :half], upper[half:, half:]])
    return factors, out


def solution(mesh):
    placed = (P("row", "col"), P("row", "col"))
    return jax.shard_map(shards, mesh=mesh, in_specs=placed, out_specs=(P(), P("row", "col")), check_vma=False)
```

```python
import functools
import math

import jax
import jax.numpy as jnp
from jax import lax
from jax.experimental import pallas as pl
from jax.experimental.pallas import tpu as pltpu
from jax.sharding import PartitionSpec as P

TH = 512
TW = 128
TI = 8
TJ = 4
SLOTS = TI * TJ
PAIR = 2
LAG = 2
CHUNKS = SLOTS // PAIR
SHORT = 12
W = TJ * TW
F32 = jnp.float32
CHEAP = pl.CostEstimate(flops=1024, bytes_accessed=1024, transcendentals=0)
BF16 = jnp.bfloat16


def params(limit=16):
    return pltpu.CompilerParams(vmem_limit_bytes=limit * 1024 * 1024)


def sds(shape, dtype):
    return jax.ShapeDtypeStruct(shape, dtype)


def site(r):
    return r // 8, (r // 2) % 4, r % 2


def row_of(z, y, c):
    return (z % 4) * 8 + (y % 4) * 2 + c


def row_perm(f):
    return [(r, row_of(*f(*site(r)))) for r in range(32)]


SWAP = row_perm(lambda z, y, c: (z, y, 1 - c))
SHIFT = {
    "y": [row_perm(lambda z, y, c, d=d: (z, y + d, c)) for d in range(4)],
    "z": [row_perm(lambda z, y, c, d=d: (z + d, y, c)) for d in range(4)],
}
RING = [(r * 4 + x, r * 4 + (x + (1 if r % 2 == 0 else 3)) % 4) for r in range(32) for x in range(4)]


def ring_step(x):
    return lax.ppermute(x, ("row", "col"), RING)


def scatter4(x, axis, me):
    h = x.shape[0] // 4
    total = lax.dynamic_slice_in_dim(x, me * h, h, 0)
    for d in (1, 3, 2):
        part = lax.dynamic_slice_in_dim(x, lax.rem(me + d, 4) * h, h, 0)
        total = total + lax.ppermute(part, "row", SHIFT[axis][d])
    return total


def gather4(x, axis, me):
    h = x.shape[0]
    out = jnp.zeros((4 * h, x.shape[1]), x.dtype)
    for d in range(4):
        got = x if d == 0 else lax.ppermute(x, "row", SHIFT[axis][d])
        out = lax.dynamic_update_slice_in_dim(out, got, lax.rem(me + 4 - d, 4) * h, 0)
    return out


def core_scatter(x, c):
    h = x.shape[0] // 2
    mine = lax.dynamic_slice_in_dim(x, c * h, h, 0)
    other = lax.dynamic_slice_in_dim(x, (1 - c) * h, h, 0)
    return mine + lax.ppermute(other, "row", SWAP)


def core_gather(x, c):
    got = lax.ppermute(x, "row", SWAP)
    first = jnp.where(c == 0, x, got)
    second = jnp.where(c == 0, got, x)
    return jnp.concatenate([first, second], 0)


def row_sum(x):
    z, y, c = site(lax.axis_index("row"))
    v = core_scatter(x, c)
    v = scatter4(v, "y", y)
    v = scatter4(v, "z", z)
    v = gather4(v, "z", z)
    v = gather4(v, "y", y)
    return core_gather(v, c)


def shifted(x, axis):
    if axis == "col":
        return [lax.ppermute(x, "col", [(i, (i + d) % 4) for i in range(4)]) for d in (1, 2, 3)]
    return [lax.ppermute(x, "row", SHIFT[axis][d]) for d in (1, 2, 3)]


HBM = pl.BlockSpec(memory_space=pltpu.HBM)
VMEM = pl.BlockSpec(memory_space=pltpu.VMEM)
SMEM = pl.BlockSpec(memory_space=pltpu.SMEM)
ROOT, HOP, CORE, ZPOS, COL = range(5)
UPPER = [(i, j) for i in range(TJ) for j in range(i, TJ)]
BLOCKS = len(UPPER) // 2 * TW
HALF = BLOCKS + 32
QUARTER = HALF // 4


def split(x):
    high = x.astype(BF16)
    return high, (x - high.astype(F32)).astype(BF16)


def dot(a, b):
    return jnp.dot(a, b, preferred_element_type=F32)


def hdot(a, b, dims):
    return lax.dot_general(a, b, (dims, ((), ())), precision=lax.Precision.HIGHEST, preferred_element_type=F32)


def call(body, ins, outs, shapes, name, scratch=(), aliases=None, limit=57):
    return pl.pallas_call(
        body,
        in_specs=ins,
        out_specs=outs,
        out_shape=shapes,
        scratch_shapes=list(scratch),
        input_output_aliases=aliases or {},
        compiler_params=params(limit),
        cost_estimate=CHEAP,
        name=name,
    )


def find(panel, wanted):
    seen, place, found = jnp.int32(0), jnp.int32(0), jnp.int32(0)
    for t in range(SLOTS):
        full = panel[t % TI, t // TI]
        hit = jnp.where((full > 0) & (seen == wanted), 1, 0)
        place += hit * t
        found += hit
        seen += full
    return place, found > 0


def relay_body(step, start, stop, fresh, me, panel, x_ref, *refs):
    refs = list(refs)
    got = None if step < LAG else refs.pop(0)
    if not fresh:
        refs.pop(0)
    filed = refs.pop(0)
    send = refs.pop(0) if len(refs) > 3 else None
    held, in_sem, out_sem = refs
    root = me[ROOT] > 0
    chunk = start + step - me[HOP] * LAG
    tiles = []
    for e in range(PAIR):
        place, found = find(panel, chunk * PAIR + e)
        rows = pl.ds(pl.multiple_of((place % TI) * TH, TH), TH)
        cols = pl.ds(pl.multiple_of((place // TI) * TW, TW), TW)
        tiles.append((e, found & (chunk >= start) & (chunk < stop), rows, cols, pl.ds(e * TH, TH)))

    def arrive(act):
        for e, found, rows, cols, part in tiles:

            @pl.when(found & root)
            def _(e=e, rows=rows, cols=cols, part=part):
                act(pltpu.make_async_copy(x_ref.at[rows, cols], held.at[part, :], in_sem.at[e]))

            if got is not None:

                @pl.when(found & jnp.logical_not(root))
                def _(e=e, part=part):
                    act(pltpu.make_async_copy(got.at[part, :], held.at[part, :], in_sem.at[e]))

    def leave(act):
        for e, found, rows, cols, part in tiles:

            @pl.when(found)
            def _(e=e, rows=rows, cols=cols, part=part):
                if send is not None:
                    act(pltpu.make_async_copy(held.at[part, :], send.at[part, :], out_sem.at[2 * e]))
                act(pltpu.make_async_copy(held.at[part, :], filed.at[rows, cols], out_sem.at[2 * e + 1]))

    arrive(lambda c: c.start())
    arrive(lambda c: c.wait())
    leave(lambda c: c.start())
    leave(lambda c: c.wait())


def relay(step, start, stop, last, me, panel, x, got, filed):
    ins, args = [SMEM, SMEM, HBM], [me, panel, x]
    if step >= LAG:
        ins.append(HBM)
        args.append(got)
    aliases = {}
    if filed is not None:
        aliases = {len(args): 0}
        ins.append(HBM)
        args.append(filed)
    shapes = [sds((TI * TH, W), F32)]
    if not last:
        shapes.append(sds((PAIR * TH, TW), F32))
    scratch = [pltpu.VMEM((PAIR * TH, TW), F32), pltpu.SemaphoreType.DMA((PAIR,)), pltpu.SemaphoreType.DMA((2 * PAIR,))]
    out = call(
        functools.partial(relay_body, step, start, stop, filed is None),
        ins,
        [HBM] * len(shapes),
        shapes,
        "relay",
        scratch,
        aliases,
    )(*args)
    return out if not last else (out[0], None)


def gram_body(me, occ, x_ref, filed_in, keep, give, filed, gram_ref, cross_ref):
    i = pl.program_id(0)

    @pl.when(i == 0)
    def _():
        gram_ref[...] = jnp.zeros_like(gram_ref)
        cross_ref[...] = jnp.zeros_like(cross_ref)

    @pl.when(me[ROOT] > 0)
    def _():
        x = jnp.concatenate([x_ref[:, j * TW : (j + 1) * TW] * occ[i, j].astype(F32) for j in range(TJ)], 1)
        high, low = split(x)
        h = W // 2
        high_t, low_t = high.T, low.T
        gram_ref[:h, :] += dot(high_t[:h], high) + dot(low_t[:h], low)
        gram_ref[h:, h:] += dot(high_t[h:], high[:, h:]) + dot(low_t[h:], low[:, h:])
        cross_ref[...] += dot(high_t, low)

    @pl.when(i == TI - 1)
    def _():
        full = jnp.int32(0)
        for t in range(SLOTS):
            full += occ[t % TI, t // TI]
        over = jnp.where(full > SHORT * PAIR, 1.0, 0.0)
        keep[BLOCKS:, :] = jnp.full((HALF - BLOCKS, TW), over, F32)
        give[BLOCKS:, :] = jnp.full((HALF - BLOCKS, TW), over, F32)
        for b, (r, q) in enumerate(UPPER):
            rows, cols = slice(r * TW, (r + 1) * TW), slice(q * TW, (q + 1) * TW)
            block = gram_ref[rows, cols] + cross_ref[rows, cols] + cross_ref[cols, rows].T
            part, at = divmod(b * TW, BLOCKS)
            mine = me[CORE] == part

            @pl.when(mine)
            def _(block=block, at=at):
                keep[at : at + TW, :] = block

            @pl.when(jnp.logical_not(mine))
            def _(block=block, at=at):
                give[at : at + TW, :] = block


def gram_part(me, occ, x, filed):
    whole = pl.BlockSpec((HALF, TW), lambda i, *_: (0, 0))
    return pl.pallas_call(
        gram_body,
        grid_spec=pltpu.PrefetchScalarGridSpec(
            num_scalar_prefetch=2,
            grid=(TI,),
            in_specs=[pl.BlockSpec((TH, W), lambda i, me, occ: (i * me[ROOT], 0)), HBM],
            out_specs=[whole, whole, HBM],
            scratch_shapes=[pltpu.VMEM((W, W), F32), pltpu.VMEM((W, W), F32)],
        ),
        out_shape=[sds((HALF, TW), F32), sds((HALF, TW), F32), sds(filed.shape, F32)],
        input_output_aliases={3: 2},
        compiler_params=params(57),
        cost_estimate=CHEAP,
        name="gram_part",
    )(me, occ, x, filed)


def add_body(*refs):
    ins, (_, out, _) = refs[:-3], refs[-3:]
    total = ins[0][...]
    for r in ins[1:]:
        total = total + r[...]
    out[...] = total


def add_parts(parts, filed):
    n = len(parts)
    return call(
        add_body,
        [VMEM] * n + [HBM],
        [VMEM, HBM],
        [sds(parts[0].shape, F32), sds(filed.shape, F32)],
        "add_parts",
        aliases={n: 1},
    )(*parts, filed)


def add_cut_body(me, a, b, c, d, _, own, one, two, three, __, total):
    total[...] = a[...] + b[...] + c[...] + d[...]
    for k, out in enumerate((own, one, two, three)):
        at = lax.rem(me[ZPOS] + k, 4) * QUARTER
        out[...] = total[pl.ds(pl.multiple_of(at, 8), QUARTER), :]


def add_cut(me, parts, filed):
    return call(
        add_cut_body,
        [SMEM] + [VMEM] * 4 + [HBM],
        [VMEM] * 4 + [HBM],
        [sds((QUARTER, TW), F32)] * 4 + [sds(filed.shape, F32)],
        "add_cut",
        [pltpu.VMEM((HALF, TW), F32)],
        {5: 4},
    )(me, *parts, filed)


def choose_body(me, a, b, c, d, _, out, __):
    for k, ref in enumerate((a, b, c, d)):

        @pl.when(me[COL] == k)
        def _(ref=ref):
            out[...] = ref[...]


def choose(me, parts, filed):
    return call(
        choose_body,
        [SMEM] + [VMEM] * 4 + [HBM],
        [VMEM, HBM],
        [sds((QUARTER, TW), F32), sds(filed.shape, F32)],
        "choose",
        aliases={5: 1},
    )(me, *parts, filed)


def stack_body(me, a, b, c, d, _, out, __):
    for k, ref in enumerate((a, b, c, d)):
        at = lax.rem(me[ZPOS] + 4 - k, 4) * QUARTER
        out[pl.ds(pl.multiple_of(at, 8), QUARTER), :] = ref[...]


def stack(me, parts, filed):
    return call(
        stack_body,
        [SMEM] + [VMEM] * 4 + [HBM],
        [VMEM, HBM],
        [sds((HALF, TW), F32), sds(filed.shape, F32)],
        "stack",
        aliases={5: 1},
    )(me, *parts, filed)


def unpack_body(me, mine, other, _, s_ref, e_ref, over_ref, __):
    over_ref[...] = mine[BLOCKS : BLOCKS + 8, :]
    s_ref[...] = jnp.zeros_like(s_ref)
    for b, (r, q) in enumerate(UPPER):
        part, at = divmod(b * TW, BLOCKS)
        block = jnp.where(me[CORE] == part, mine[at : at + TW, :], other[at : at + TW, :])
        s_ref[r * TW : (r + 1) * TW, q * TW : (q + 1) * TW] = block
        if b == 0:
            e_ref[:, :TW] = block
    e_ref[:, TW:] = unit()


def unpack(me, mine, other, filed):
    return call(
        unpack_body,
        [SMEM, VMEM, VMEM, HBM],
        [VMEM, VMEM, VMEM, HBM],
        [sds((W, W), F32), sds((TW, 2 * TW), F32), sds((8, TW), F32), sds(filed.shape, F32)],
        "unpack",
        aliases={3: 3},
    )(me, mine, other, filed)


def unit():
    r = lax.broadcasted_iota(jnp.int32, (TW, TW), 0)
    c = lax.broadcasted_iota(jnp.int32, (TW, TW), 1)
    return jnp.where(r == c, 1.0, 0.0).astype(F32)


def eliminate(m_rows, v_rows, start, stop):
    groups = len(m_rows)
    full = (8, m_rows[0].shape[1])
    sub = lax.broadcasted_iota(jnp.int32, full, 0)

    def row(x, r):
        return jnp.broadcast_to(x[r : r + 1, :], full)

    for g in range(start, stop):
        lanes = [8 * g + k for k in range(8)]
        columns = [jnp.broadcast_to(m_rows[g][:, lane : lane + 1], full) for lane in lanes]
        a = {(r, k): row(columns[k], r) for k in range(8) for r in range(k, 8)}
        rm = [row(m_rows[g], r) for r in range(8)]
        rv = [row(v_rows[g], r) for r in range(8)]
        inverse = []
        for k in range(8):
            scale = lax.rsqrt(a[k, k])
            inverse.append(scale)
            for r in range(k + 1, 8):
                a[r, k] = a[r, k] * scale
            for c in range(k + 1, 8):
                for r in range(c, 8):
                    a[r, c] = a[r, c] - a[r, k] * a[c, k]
            rm[k] = rm[k] * scale
            rv[k] = rv[k] * scale
            for r in range(k + 1, 8):
                rm[r] = rm[r] - a[r, k] * rm[k]
                rv[r] = rv[r] - a[r, k] * rv[k]
        for i in range(g + 1, groups):
            factor = [jnp.broadcast_to(m_rows[i][:, lane : lane + 1], full) for lane in lanes]
            new_m, new_v = m_rows[i], v_rows[i]
            for k in range(8):
                factor[k] = factor[k] * inverse[k]
                for r in range(k + 1, 8):
                    factor[r] = factor[r] - factor[k] * a[r, k]
                new_m = new_m - factor[k] * rm[k]
                new_v = new_v - factor[k] * rv[k]
            m_rows[i], v_rows[i] = new_m, new_v
        top_m, top_v = rm[0], rv[0]
        for r in range(1, 8):
            top_m = jnp.where(sub == r, rm[r], top_m)
            top_v = jnp.where(sub == r, rv[r], top_v)
        m_rows[g], v_rows[g] = top_m, top_v
    return m_rows, v_rows


def eliminate_body(e_in, _, e_out):
    groups = range(TW // 8)
    m_rows = [e_in[8 * g : 8 * g + 8, :TW] for g in groups]
    v_rows = [e_in[8 * g : 8 * g + 8, TW:] for g in groups]
    m_rows, v_rows = eliminate(m_rows, v_rows, 0, TW // 8)
    r = lax.broadcasted_iota(jnp.int32, (8, TW), 0)
    c = lax.broadcasted_iota(jnp.int32, (8, TW), 1)
    for g in groups:
        e_out[8 * g : 8 * g + 8, :TW] = jnp.where(r + 8 * g <= c, m_rows[g], 0.0)
        e_out[8 * g : 8 * g + 8, TW:] = v_rows[g]


def eliminate_block(e, before):
    return call(eliminate_body, [VMEM, HBM], VMEM, sds((TW, 2 * TW), F32), "eliminate")(e, before)


def spread_body(b, e_in, s_in, v_in, s_ref, v_ref, e_out):
    lo, hi = b * TW, (b + 1) * TW
    s_ref[...] = s_in[...]
    if b == 0:
        v_ref[...] = jnp.zeros_like(v_ref)
    else:
        v_ref[...] = v_in[...]
    inv = e_in[:, TW:]
    s_ref[lo:hi, lo:hi] = e_in[:, :TW]
    v_ref[lo:hi, lo:hi] = inv
    if b > 0:
        v_ref[lo:hi, :lo] = hdot(inv, v_in[lo:hi, :lo], ((1,), (0,)))
    if hi < W:
        right = hdot(inv, s_in[lo:hi, hi:], ((1,), (0,)))
        s_ref[lo:hi, hi:] = right
        s_ref[hi:, hi:] -= hdot(right, right, ((0,), (0,)))
        s_ref[hi:, lo:hi] = jnp.zeros((W - hi, TW), F32)
        v_ref[hi:, :hi] -= hdot(right, v_ref[lo:hi, :hi], ((0,), (0,)))
        e_out[:, :TW] = s_ref[hi : hi + TW, hi : hi + TW]
        e_out[:, TW:] = unit()
    else:
        e_out[...] = e_in[...]


def spread(b, e, s, v):
    return call(
        functools.partial(spread_body, b),
        [VMEM] * 3,
        [VMEM] * 3,
        [sds((W, W), F32), sds((W, W), F32), sds((TW, 2 * TW), F32)],
        "spread",
    )(e, s, v)


def masked(ref, flags, i, upto=TJ):
    parts = []
    for j in range(upto):
        block = ref[:, j * TW : (j + 1) * TW]
        parts.append(jnp.where(flags[i, j] > 0, block, jnp.zeros_like(block)))
    return jnp.concatenate(parts, 1)


def project_body(me, occ, panel, x_ref, a_ref, c_ref):
    i = pl.program_id(0)

    @pl.when(i == 0)
    def _():
        c_ref[...] = jnp.zeros_like(c_ref)

    @pl.when(me[ROOT] == 0)
    def _():
        ah, al = split(masked(a_ref, panel, i))
        bh, bl = split(masked(x_ref, occ, i))
        ah_t, al_t = ah.T, al.T
        c_ref[...] += dot(ah_t, bh) + dot(al_t, bh) + dot(ah_t, bl)


def project(me, occ, panel, x, filed):
    block = pl.BlockSpec((TH, W), lambda i, *_: (i, 0))
    return pl.pallas_call(
        project_body,
        grid_spec=pltpu.PrefetchScalarGridSpec(
            num_scalar_prefetch=3,
            grid=(TI,),
            in_specs=[block, block],
            out_specs=pl.BlockSpec((W, W), lambda i, *_: (0, 0)),
        ),
        out_shape=sds((W, W), F32),
        compiler_params=params(),
        cost_estimate=CHEAP,
        name="project",
    )(me, occ, panel, x, filed)


def finish_body(me, occ, panel, x_ref, a_ref, xh, xl, out_ref):
    i = pl.program_id(0)
    keep = 1 - me[ROOT]
    ah, al = split(masked(a_ref, panel, i))
    taken = dot(ah, xh[...]) + dot(ah, xl[...]) + dot(al, xh[...])
    for j in range(TJ):
        at = slice(j * TW, (j + 1) * TW)
        out_ref[:, at] = x_ref[:, at] * (occ[i, j] * keep).astype(F32) - taken[:, at]


def finish(me, occ, panel, x, filed, xh, xl):
    rows = TI * TH
    block = pl.BlockSpec((TH, W), lambda i, *_: (i, 0))
    whole = pl.BlockSpec((W, W), lambda i, *_: (0, 0))
    return pl.pallas_call(
        finish_body,
        grid_spec=pltpu.PrefetchScalarGridSpec(
            num_scalar_prefetch=3,
            grid=(TI,),
            in_specs=[block, block, whole, whole],
            out_specs=block,
        ),
        out_shape=sds((rows, W), F32),
        compiler_params=params(),
        cost_estimate=CHEAP,
        name="finish",
    )(me, occ, panel, x, filed, xh, xl)


def shards(snapshots, tiles):
    col = lax.axis_index("col")
    z, _, core = site(lax.axis_index("row"))
    root = col == 0
    hop = jnp.where(core == 0, col, (4 - col) % 4)
    total_rows = snapshots.shape[0] * lax.axis_size("row")
    scale = jnp.float32(math.sqrt(total_rows))
    me = jnp.stack([root.astype(jnp.int32), hop, core, z, col]).astype(jnp.int32)

    panels, passed = [tiles], tiles
    for h in range(1, 4):
        passed = ring_step(passed)
        panels.append(jnp.where(hop == h, passed, panels[-1]))
    panel = panels[3]

    filed = None
    state = {}

    def ring(start, stop, filed, beside=None):
        got = [None] * LAG
        steps = stop - start + 3 * LAG
        for s in range(steps):
            last = s >= steps - LAG
            seen = panels[min(s // LAG, 3)] if start == 0 else panel
            filed, send = relay(s, start, stop, last, me, seen, snapshots, got[s % LAG], filed)
            if not last:
                got[s % LAG] = ring_step(send)
            if beside is not None:
                filed = beside(s, filed)
        return filed

    def gram_stage(name, filed):
        if name == "parts":
            keep, give, filed = gram_part(me, tiles, snapshots, filed)
            state["v"] = [keep, lax.ppermute(give, "row", SWAP)]
        elif name == "core":
            v, filed = add_parts(state["v"], filed)
            state["v"] = [v] + shifted(v, "y")
        elif name == "y":
            own, one, two, three, filed = add_cut(me, state["v"], filed)
            sent = [lax.ppermute(p, "row", SHIFT["z"][d]) for d, p in ((1, one), (2, two), (3, three))]
            state["v"] = [own] + sent
        elif name == "z":
            v, filed = add_parts(state["v"], filed)
            state["v"] = [v] + shifted(v, "col")
        elif name == "col":
            v, filed = choose(me, state["v"], filed)
            state["v"] = [v] + shifted(v, "z")
        elif name == "stack":
            v, filed = stack(me, state["v"], filed)
            state["v"] = [v, lax.ppermute(v, "row", SWAP)]
        elif name == "unpack":
            state["s"], state["e"], state["over"], filed = unpack(me, *state["v"], filed)
            state["inv"] = state["s"]
        elif name[0] == "e":
            state["e"] = eliminate_block(state["e"], filed)
        else:
            state["s"], state["inv"], state["e"] = spread(int(name[1]), state["e"], state["s"], state["inv"])
        return filed

    plan = {1: ["parts"], 2: ["core"], 4: ["y"], 6: ["z"], 7: ["col"], 9: ["stack"], 10: ["unpack"]}
    plan.update({11: ["e0", "s0"], 13: ["e1", "s1"], 15: ["e2", "s2"]})

    def beside(s, filed):
        for name in plan.get(s, []):
            filed = gram_stage(name, filed)
        return filed

    filed = ring(0, SHORT, None, beside)
    filed = lax.cond(state["over"][0, 0] > 0.5, lambda f: ring(SHORT, CHUNKS, f), lambda f: f, filed)
    prod = project(me, tiles, panel, snapshots, filed)
    gram_stage("e3", prod)
    gram_stage("s3", prod)
    proj = row_sum(prod)
    inv = state["inv"]
    mid = jnp.dot(inv, proj, precision=lax.Precision.HIGHEST)
    coef = jnp.dot(inv.T, mid, precision=lax.Precision.HIGHEST)
    coef = jnp.where(root, -scale * inv.T, coef)
    xh = lax.reduce_precision(coef, 8, 7)
    xl = (coef - xh).astype(BF16)
    out = finish(me, tiles, panel, snapshots, filed, xh.astype(BF16), xl)
    half = W // 2
    upper = state["s"]
    factors = jnp.stack([upper[:half, :half], upper[half:, half:]])
    return factors, out


def solution(mesh):
    placed = (P("row", "col"), P("row", "col"))
    return jax.shard_map(shards, mesh=mesh, in_specs=placed, out_specs=(P(), P("row", "col")), check_vma=False)
```

```python
import functools
import math

import jax
import jax.numpy as jnp
from jax import lax
from jax.experimental import pallas as pl
from jax.experimental.pallas import tpu as pltpu
from jax.sharding import PartitionSpec as P

TH = 512
TW = 128
TI = 8
TJ = 4
SLOTS = TI * TJ
PAIR = 2
LAG = 2
CHUNKS = SLOTS // PAIR
SHORT = 12
W = TJ * TW
F32 = jnp.float32
CHEAP = pl.CostEstimate(flops=1024, bytes_accessed=1024, transcendentals=0)
BF16 = jnp.bfloat16


def params(limit=16):
    return pltpu.CompilerParams(vmem_limit_bytes=limit * 1024 * 1024)


def sds(shape, dtype):
    return jax.ShapeDtypeStruct(shape, dtype)


def site(r):
    return r // 8, (r // 2) % 4, r % 2


def row_of(z, y, c):
    return (z % 4) * 8 + (y % 4) * 2 + c


def row_perm(f):
    return [(r, row_of(*f(*site(r)))) for r in range(32)]


SWAP = row_perm(lambda z, y, c: (z, y, 1 - c))
SHIFT = {
    "y": [row_perm(lambda z, y, c, d=d: (z, y + d, c)) for d in range(4)],
    "z": [row_perm(lambda z, y, c, d=d: (z + d, y, c)) for d in range(4)],
}
RING = [(r * 4 + x, r * 4 + (x + (1 if r % 2 == 0 else 3)) % 4) for r in range(32) for x in range(4)]


def ring_step(x):
    return lax.ppermute(x, ("row", "col"), RING)


def scatter4(x, axis, me):
    h = x.shape[0] // 4
    total = lax.dynamic_slice_in_dim(x, me * h, h, 0)
    for d in (1, 3, 2):
        part = lax.dynamic_slice_in_dim(x, lax.rem(me + d, 4) * h, h, 0)
        total = total + lax.ppermute(part, "row", SHIFT[axis][d])
    return total


def gather4(x, axis, me):
    h = x.shape[0]
    out = jnp.zeros((4 * h, x.shape[1]), x.dtype)
    for d in range(4):
        got = x if d == 0 else lax.ppermute(x, "row", SHIFT[axis][d])
        out = lax.dynamic_update_slice_in_dim(out, got, lax.rem(me + 4 - d, 4) * h, 0)
    return out


def core_scatter(x, c):
    h = x.shape[0] // 2
    mine = lax.dynamic_slice_in_dim(x, c * h, h, 0)
    other = lax.dynamic_slice_in_dim(x, (1 - c) * h, h, 0)
    return mine + lax.ppermute(other, "row", SWAP)


def core_gather(x, c):
    got = lax.ppermute(x, "row", SWAP)
    first = jnp.where(c == 0, x, got)
    second = jnp.where(c == 0, got, x)
    return jnp.concatenate([first, second], 0)


def row_sum(x):
    z, y, c = site(lax.axis_index("row"))
    v = core_scatter(x, c)
    v = scatter4(v, "y", y)
    v = scatter4(v, "z", z)
    v = gather4(v, "z", z)
    v = gather4(v, "y", y)
    return core_gather(v, c)


def shifted(x, axis):
    if axis == "col":
        return [lax.ppermute(x, "col", [(i, (i + d) % 4) for i in range(4)]) for d in (1, 2, 3)]
    return [lax.ppermute(x, "row", SHIFT[axis][d]) for d in (1, 2, 3)]


ANY = pl.BlockSpec(memory_space=pl.ANY)
VMEM = pl.BlockSpec(memory_space=pltpu.VMEM)
SMEM = pl.BlockSpec(memory_space=pltpu.SMEM)
ROOT, HOP, CORE, ZPOS, COL = range(5)
UPPER = [(i, j) for i in range(TJ) for j in range(i, TJ)]
BLOCKS = len(UPPER) // 2 * TW
HALF = BLOCKS + 32
QUARTER = HALF // 4


def kept(shape):
    return pltpu.VMEM(shape, F32)


FILED = kept((TI * TH, W))


def pin(x):
    return pltpu.with_memory_space_constraint(x, pltpu.VMEM)


def split(x):
    high = x.astype(BF16)
    return high, (x - high.astype(F32)).astype(BF16)


def dot(a, b):
    return jnp.dot(a, b, preferred_element_type=F32)


def hdot(a, b, dims):
    return lax.dot_general(a, b, (dims, ((), ())), precision=lax.Precision.HIGHEST, preferred_element_type=F32)


def call(body, ins, outs, shapes, name, scratch=(), aliases=None, limit=16):
    return pl.pallas_call(
        body,
        in_specs=ins,
        out_specs=outs,
        out_shape=shapes,
        scratch_shapes=list(scratch),
        input_output_aliases=aliases or {},
        compiler_params=params(limit),
        cost_estimate=CHEAP,
        name=name,
    )


def find(full, wanted):
    seen, place, found = jnp.int32(0), jnp.int32(0), jnp.int32(0)
    for t in range(SLOTS):
        hit = jnp.where((full[t] > 0) & (seen == wanted), 1, 0)
        place += hit * t
        found += hit
        seen += full[t]
    return place, found > 0


def relay_body(step, start, stop, fresh, passing, last, me, own, *refs):
    refs = list(refs)
    root = me[ROOT] > 0
    passed = refs.pop(0) if passing and step >= LAG else None
    x_ref = refs.pop(0)
    got = None if step < LAG else refs.pop(0)
    if not fresh:
        refs.pop(0)
    filed = refs.pop(0)
    send = None if last else refs.pop(0)
    seen = refs.pop(0) if passing else None
    (sem,) = refs
    full = []
    for t in range(SLOTS):
        flag = own[t % TI, t // TI]
        if passed is not None:
            flag = jnp.where(root, flag, passed[t % TI, t // TI])
        if seen is not None:
            seen[t % TI, t // TI] = flag
        full.append(flag)
    chunk = start + step - me[HOP] * LAG
    live = (chunk >= start) & (chunk < stop)

    def each(act):
        for e in range(PAIR):
            place, found = places[e]
            rows = pl.ds(pl.multiple_of((place % TI) * TH, TH), TH)
            cols = pl.ds(pl.multiple_of((place // TI) * TW, TW), TW)
            part = pl.ds(e * TH, TH)

            def move(src, e=e, rows=rows, cols=cols, part=part):
                act(pltpu.make_async_copy(src, filed.at[rows, cols], sem.at[2 * e]))
                if send is not None:
                    act(pltpu.make_async_copy(src, send.at[part, :], sem.at[2 * e + 1]))

            @pl.when(found & live & root)
            def _(move=move, rows=rows, cols=cols):
                move(x_ref.at[rows, cols])

            if got is not None:

                @pl.when(found & live & jnp.logical_not(root))
                def _(move=move, part=part):
                    move(got.at[part, :])

    places = [find(full, chunk * PAIR + e) for e in range(PAIR)]
    each(lambda c: c.start())
    each(lambda c: c.wait())


def relay(step, start, stop, last, me, own, passed, passing, x, got, filed):
    ins, args = [SMEM, SMEM], [me, own]
    if passing and step >= LAG:
        ins.append(SMEM)
        args.append(passed)
    ins.append(ANY)
    args.append(x)
    if step >= LAG:
        ins.append(ANY)
        args.append(got)
    aliases = {}
    if filed is not None:
        aliases = {len(args): 0}
        ins.append(ANY)
        args.append(pin(filed))
    shapes, outs = [FILED], [ANY]
    if not last:
        shapes.append(kept((PAIR * TH, TW)))
        outs.append(ANY)
    if passing:
        shapes.append(sds((TI, TJ), jnp.int32))
        outs.append(SMEM)
    out = list(
        call(
            functools.partial(relay_body, step, start, stop, filed is None, passing, last),
            ins,
            outs,
            shapes,
            "relay",
            [pltpu.SemaphoreType.DMA((2 * PAIR,))],
            aliases,
            4,
        )(*args)
    )
    filed = out.pop(0)
    send = None if last else out.pop(0)
    return filed, send, out.pop(0) if passing else None


def load_body(x_ref, out, sem):
    copies = [
        pltpu.make_async_copy(x_ref.at[pl.ds(i * TH, TH), :], out.at[pl.ds(i * TH, TH), :], sem.at[i]) for i in range(TI)
    ]
    for c in copies:
        c.start()
    for c in copies:
        c.wait()


def load(x):
    return call(load_body, [ANY], ANY, FILED, "load", [pltpu.SemaphoreType.DMA((TI,))])(x)


def gram_body(me, occ, x_ref, filed_in, keep, give, filed, gram_ref, cross_ref):
    i = pl.program_id(0)

    @pl.when(i == 0)
    def _():
        gram_ref[...] = jnp.zeros_like(gram_ref)
        cross_ref[...] = jnp.zeros_like(cross_ref)

    @pl.when(me[ROOT] > 0)
    def _():
        x = jnp.concatenate([x_ref[:, j * TW : (j + 1) * TW] * occ[i, j].astype(F32) for j in range(TJ)], 1)
        high, low = split(x)
        h = W // 2
        high_t, low_t = high.T, low.T
        gram_ref[:h, :] += dot(high_t[:h], high) + dot(low_t[:h], low)
        gram_ref[h:, h:] += dot(high_t[h:], high[:, h:]) + dot(low_t[h:], low[:, h:])
        cross_ref[...] += dot(high_t, low)

    @pl.when(i == TI - 1)
    def _():
        full = jnp.int32(0)
        for t in range(SLOTS):
            full += occ[t % TI, t // TI]
        over = jnp.where(full > SHORT * PAIR, 1.0, 0.0)
        keep[BLOCKS:, :] = jnp.full((HALF - BLOCKS, TW), over, F32)
        give[BLOCKS:, :] = jnp.full((HALF - BLOCKS, TW), over, F32)
        for b, (r, q) in enumerate(UPPER):
            rows, cols = slice(r * TW, (r + 1) * TW), slice(q * TW, (q + 1) * TW)
            block = gram_ref[rows, cols] + cross_ref[rows, cols] + cross_ref[cols, rows].T
            part, at = divmod(b * TW, BLOCKS)
            mine = me[CORE] == part

            @pl.when(mine)
            def _(block=block, at=at):
                keep[at : at + TW, :] = block

            @pl.when(jnp.logical_not(mine))
            def _(block=block, at=at):
                give[at : at + TW, :] = block


def gram_part(me, occ, x, filed):
    whole = pl.BlockSpec((HALF, TW), lambda i, *_: (0, 0))
    return pl.pallas_call(
        gram_body,
        grid_spec=pltpu.PrefetchScalarGridSpec(
            num_scalar_prefetch=2,
            grid=(TI,),
            in_specs=[pl.BlockSpec((TH, W), lambda i, me, occ: (i * me[ROOT], 0)), ANY],
            out_specs=[whole, whole, ANY],
            scratch_shapes=[pltpu.VMEM((W, W), F32), pltpu.VMEM((W, W), F32)],
        ),
        out_shape=[sds((HALF, TW), F32), sds((HALF, TW), F32), FILED],
        input_output_aliases={3: 2},
        compiler_params=params(24),
        cost_estimate=CHEAP,
        name="gram_part",
    )(me, occ, pin(x), pin(filed))


def add_body(*refs):
    ins, (_, out, _) = refs[:-3], refs[-3:]
    total = ins[0][...]
    for r in ins[1:]:
        total = total + r[...]
    out[...] = total


def add_parts(parts, filed):
    n = len(parts)
    return call(
        add_body,
        [VMEM] * n + [ANY],
        [VMEM, ANY],
        [sds(parts[0].shape, F32), FILED],
        "add_parts",
        aliases={n: 1},
    )(*parts, pin(filed))


def add_cut_body(me, a, b, c, d, _, own, one, two, three, __, total):
    total[...] = a[...] + b[...] + c[...] + d[...]
    for k, out in enumerate((own, one, two, three)):
        at = lax.rem(me[ZPOS] + k, 4) * QUARTER
        out[...] = total[pl.ds(pl.multiple_of(at, 8), QUARTER), :]


def add_cut(me, parts, filed):
    return call(
        add_cut_body,
        [SMEM] + [VMEM] * 4 + [ANY],
        [VMEM] * 4 + [ANY],
        [sds((QUARTER, TW), F32)] * 4 + [FILED],
        "add_cut",
        [pltpu.VMEM((HALF, TW), F32)],
        {5: 4},
    )(me, *parts, pin(filed))


def choose_body(me, a, b, c, d, _, out, __):
    for k, ref in enumerate((a, b, c, d)):

        @pl.when(me[COL] == k)
        def _(ref=ref):
            out[...] = ref[...]


def choose(me, parts, filed):
    return call(
        choose_body,
        [SMEM] + [VMEM] * 4 + [ANY],
        [VMEM, ANY],
        [sds((QUARTER, TW), F32), FILED],
        "choose",
        aliases={5: 1},
    )(me, *parts, pin(filed))


def stack_body(me, a, b, c, d, _, out, __):
    for k, ref in enumerate((a, b, c, d)):
        at = lax.rem(me[ZPOS] + 4 - k, 4) * QUARTER
        out[pl.ds(pl.multiple_of(at, 8), QUARTER), :] = ref[...]


def stack(me, parts, filed):
    return call(
        stack_body,
        [SMEM] + [VMEM] * 4 + [ANY],
        [VMEM, ANY],
        [sds((HALF, TW), F32), FILED],
        "stack",
        aliases={5: 1},
    )(me, *parts, pin(filed))


def unpack_body(me, mine, other, _, s_ref, e_ref, over_ref, __):
    over_ref[...] = mine[BLOCKS : BLOCKS + 8, :]
    s_ref[...] = jnp.zeros_like(s_ref)
    for b, (r, q) in enumerate(UPPER):
        part, at = divmod(b * TW, BLOCKS)
        block = jnp.where(me[CORE] == part, mine[at : at + TW, :], other[at : at + TW, :])
        s_ref[r * TW : (r + 1) * TW, q * TW : (q + 1) * TW] = block
        if b == 0:
            e_ref[:, :TW] = block
    e_ref[:, TW:] = unit()


def unpack(me, mine, other, filed):
    return call(
        unpack_body,
        [SMEM, VMEM, VMEM, ANY],
        [VMEM, VMEM, VMEM, ANY],
        [sds((W, W), F32), sds((TW, 2 * TW), F32), sds((8, TW), F32), FILED],
        "unpack",
        aliases={3: 3},
    )(me, mine, other, pin(filed))


def unit():
    r = lax.broadcasted_iota(jnp.int32, (TW, TW), 0)
    c = lax.broadcasted_iota(jnp.int32, (TW, TW), 1)
    return jnp.where(r == c, 1.0, 0.0).astype(F32)


def eliminate(m_rows, v_rows, start, stop):
    groups = len(m_rows)
    full = (8, m_rows[0].shape[1])
    sub = lax.broadcasted_iota(jnp.int32, full, 0)

    def row(x, r):
        return jnp.broadcast_to(x[r : r + 1, :], full)

    for g in range(start, stop):
        lanes = [8 * g + k for k in range(8)]
        columns = [jnp.broadcast_to(m_rows[g][:, lane : lane + 1], full) for lane in lanes]
        a = {(r, k): row(columns[k], r) for k in range(8) for r in range(k, 8)}
        rm = [row(m_rows[g], r) for r in range(8)]
        rv = [row(v_rows[g], r) for r in range(8)]
        inverse = []
        for k in range(8):
            scale = lax.rsqrt(a[k, k])
            inverse.append(scale)
            for r in range(k + 1, 8):
                a[r, k] = a[r, k] * scale
            for c in range(k + 1, 8):
                for r in range(c, 8):
                    a[r, c] = a[r, c] - a[r, k] * a[c, k]
            rm[k] = rm[k] * scale
            rv[k] = rv[k] * scale
            for r in range(k + 1, 8):
                rm[r] = rm[r] - a[r, k] * rm[k]
                rv[r] = rv[r] - a[r, k] * rv[k]
        for i in range(g + 1, groups):
            factor = [jnp.broadcast_to(m_rows[i][:, lane : lane + 1], full) for lane in lanes]
            new_m, new_v = m_rows[i], v_rows[i]
            for k in range(8):
                factor[k] = factor[k] * inverse[k]
                for r in range(k + 1, 8):
                    factor[r] = factor[r] - factor[k] * a[r, k]
                new_m = new_m - factor[k] * rm[k]
                new_v = new_v - factor[k] * rv[k]
            m_rows[i], v_rows[i] = new_m, new_v
        top_m, top_v = rm[0], rv[0]
        for r in range(1, 8):
            top_m = jnp.where(sub == r, rm[r], top_m)
            top_v = jnp.where(sub == r, rv[r], top_v)
        m_rows[g], v_rows[g] = top_m, top_v
    return m_rows, v_rows


def eliminate_body(e_in, _, e_out, __):
    groups = range(TW // 8)
    m_rows = [e_in[8 * g : 8 * g + 8, :TW] for g in groups]
    v_rows = [e_in[8 * g : 8 * g + 8, TW:] for g in groups]
    m_rows, v_rows = eliminate(m_rows, v_rows, 0, TW // 8)
    r = lax.broadcasted_iota(jnp.int32, (8, TW), 0)
    c = lax.broadcasted_iota(jnp.int32, (8, TW), 1)
    for g in groups:
        e_out[8 * g : 8 * g + 8, :TW] = jnp.where(r + 8 * g <= c, m_rows[g], 0.0)
        e_out[8 * g : 8 * g + 8, TW:] = v_rows[g]


def eliminate_block(e, filed):
    return call(
        eliminate_body, [VMEM, ANY], [VMEM, ANY], [sds((TW, 2 * TW), F32), FILED], "eliminate", aliases={1: 1}
    )(e, pin(filed))


def spread_body(b, e_in, s_in, v_in, s_ref, v_ref, e_out):
    lo, hi = b * TW, (b + 1) * TW
    s_ref[...] = s_in[...]
    if b == 0:
        v_ref[...] = jnp.zeros_like(v_ref)
    else:
        v_ref[...] = v_in[...]
    inv = e_in[:, TW:]
    s_ref[lo:hi, lo:hi] = e_in[:, :TW]
    v_ref[lo:hi, lo:hi] = inv
    if b > 0:
        v_ref[lo:hi, :lo] = hdot(inv, v_in[lo:hi, :lo], ((1,), (0,)))
    if hi < W:
        right = hdot(inv, s_in[lo:hi, hi:], ((1,), (0,)))
        s_ref[lo:hi, hi:] = right
        s_ref[hi:, hi:] -= hdot(right, right, ((0,), (0,)))
        s_ref[hi:, lo:hi] = jnp.zeros((W - hi, TW), F32)
        v_ref[hi:, :hi] -= hdot(right, v_ref[lo:hi, :hi], ((0,), (0,)))
        e_out[:, :TW] = s_ref[hi : hi + TW, hi : hi + TW]
        e_out[:, TW:] = unit()
    else:
        e_out[0] = s_ref[: W // 2, : W // 2]
        e_out[1] = s_ref[W // 2 :, W // 2 :]


def spread(b, e, s, v):
    return call(
        functools.partial(spread_body, b),
        [VMEM] * 3,
        [VMEM] * 3,
        [sds((W, W), F32), sds((W, W), F32), sds((TW, 2 * TW) if b < TJ - 1 else (2, W // 2, W // 2), F32)],
        "spread",
    )(e, s, v)


def masked(ref, flags, i, upto=TJ):
    parts = []
    for j in range(upto):
        block = ref[:, j * TW : (j + 1) * TW]
        parts.append(jnp.where(flags[i, j] > 0, block, jnp.zeros_like(block)))
    return jnp.concatenate(parts, 1)


def project_body(me, occ, panel, x_ref, a_ref, c_ref):
    i = pl.program_id(0)

    @pl.when(i == 0)
    def _():
        c_ref[...] = jnp.zeros_like(c_ref)

    @pl.when(me[ROOT] == 0)
    def _():
        ah, al = split(masked(a_ref, panel, i))
        bh, bl = split(masked(x_ref, occ, i))
        ah_t, al_t = ah.T, al.T
        c_ref[...] += dot(ah_t, bh) + dot(al_t, bh) + dot(ah_t, bl)


def project(me, occ, panel, x, filed):
    block = pl.BlockSpec((TH, W), lambda i, *_: (i, 0))
    return pl.pallas_call(
        project_body,
        grid_spec=pltpu.PrefetchScalarGridSpec(
            num_scalar_prefetch=3,
            grid=(TI,),
            in_specs=[block, block],
            out_specs=pl.BlockSpec((W, W), lambda i, *_: (0, 0)),
        ),
        out_shape=sds((W, W), F32),
        compiler_params=params(24),
        cost_estimate=CHEAP,
        name="project",
    )(me, occ, panel, pin(x), pin(filed))


def solve_body(scale, me, v_ref, c_ref, high_ref, low_ref):
    v = v_ref[...]
    coef = hdot(v, hdot(v, c_ref[...], ((1,), (0,))), ((0,), (0,)))
    coef = jnp.where(me[ROOT] > 0, -scale * v.T, coef)
    high_ref[...], low_ref[...] = split(coef)


def solve(scale, me, inv, proj):
    return call(
        functools.partial(solve_body, scale),
        [SMEM, VMEM, VMEM],
        [VMEM, VMEM],
        [sds((W, W), BF16)] * 2,
        "solve",
    )(me, inv, proj)


def finish_body(me, occ, panel, x_ref, a_ref, xh, xl, out_ref):
    i = pl.program_id(0)
    keep = 1 - me[ROOT]
    ah, al = split(masked(a_ref, panel, i))
    taken = dot(ah, xh[...]) + dot(ah, xl[...]) + dot(al, xh[...])
    for j in range(TJ):
        at = slice(j * TW, (j + 1) * TW)
        out_ref[:, at] = x_ref[:, at] * (occ[i, j] * keep).astype(F32) - taken[:, at]


def finish(me, occ, panel, x, filed, xh, xl):
    rows = TI * TH
    block = pl.BlockSpec((TH, W), lambda i, *_: (i, 0))
    whole = pl.BlockSpec((W, W), lambda i, *_: (0, 0))
    return pl.pallas_call(
        finish_body,
        grid_spec=pltpu.PrefetchScalarGridSpec(
            num_scalar_prefetch=3,
            grid=(TI,),
            in_specs=[block, block, whole, whole],
            out_specs=block,
        ),
        out_shape=sds((rows, W), F32),
        compiler_params=params(24),
        cost_estimate=CHEAP,
        name="finish",
    )(me, occ, panel, pin(x), pin(filed), xh, xl)


def shards(snapshots, tiles):
    col = lax.axis_index("col")
    z, _, core = site(lax.axis_index("row"))
    root = col == 0
    hop = jnp.where(core == 0, col, (4 - col) % 4)
    scale = math.sqrt(snapshots.shape[0] * lax.axis_size("row"))
    me = jnp.stack([root.astype(jnp.int32), hop, core, z, col]).astype(jnp.int32)
    state = {"x": snapshots, "panel": tiles}

    def ring(start, stop, filed, beside=None):
        got = [None] * LAG
        steps = stop - start + 3 * LAG
        for s in range(steps):
            last = s >= steps - LAG
            passing = start == 0 and s % LAG == 0 and s <= 3 * LAG
            own = tiles if passing else state["panel"]
            passed = ring_step(state["panel"]) if passing and s > 0 else None
            filed, send, seen = relay(s, start, stop, last, me, own, passed, passing, state["x"], got[s % LAG], filed)
            if passing:
                state["panel"] = seen
            if not last:
                got[s % LAG] = ring_step(send)
            if beside is not None:
                filed = beside(s, filed)
        return filed

    def gram_stage(name, filed):
        if name == "parts":
            state["x"] = load(snapshots)
            keep, give, filed = gram_part(me, tiles, state["x"], filed)
            state["v"] = [keep, lax.ppermute(give, "row", SWAP)]
        elif name == "core":
            v, filed = add_parts(state["v"], filed)
            state["v"] = [v] + shifted(v, "y")
        elif name == "y":
            own, one, two, three, filed = add_cut(me, state["v"], filed)
            sent = [lax.ppermute(p, "row", SHIFT["z"][d]) for d, p in ((1, one), (2, two), (3, three))]
            state["v"] = [own] + sent
        elif name == "z":
            v, filed = add_parts(state["v"], filed)
            state["v"] = [v] + shifted(v, "col")
        elif name == "col":
            v, filed = choose(me, state["v"], filed)
            state["v"] = [v] + shifted(v, "z")
        elif name == "stack":
            v, filed = stack(me, state["v"], filed)
            state["v"] = [v, lax.ppermute(v, "row", SWAP)]
        elif name == "unpack":
            state["s"], state["e"], state["over"], filed = unpack(me, *state["v"], filed)
            state["inv"] = state["s"]
        elif name[0] == "e":
            state["e"], filed = eliminate_block(state["e"], filed)
        else:
            state["s"], state["inv"], state["e"] = spread(int(name[1]), state["e"], state["s"], state["inv"])
        return filed

    plan = {1: ["parts"], 2: ["core"], 5: ["y"], 7: ["z"], 9: ["col"], 10: ["stack"], 11: ["unpack"]}
    plan.update({12: ["e0", "s0"], 13: ["e1", "s1"], 14: ["e2", "s2"], 15: ["e3", "s3"]})

    def beside(s, filed):
        for name in plan.get(s, []):
            filed = gram_stage(name, filed)
        return filed

    filed = ring(0, SHORT, None, beside)
    filed = lax.cond(state["over"][0, 0] > 0.5, lambda f: ring(SHORT, CHUNKS, f), lambda f: f, filed)
    x, panel = state["x"], state["panel"]
    proj = row_sum(project(me, tiles, panel, x, filed))
    xh, xl = solve(scale, me, state["inv"], proj)
    out = finish(me, tiles, panel, x, filed, xh, xl)
    return state["e"], out


def solution(mesh):
    placed = (P("row", "col"), P("row", "col"))
    return jax.shard_map(shards, mesh=mesh, in_specs=placed, out_specs=(P(), P("row", "col")), check_vma=False)
```

```python
import functools
import math

import jax
import jax.numpy as jnp
from jax import lax
from jax.experimental import pallas as pl
from jax.experimental.pallas import tpu as pltpu
from jax.sharding import PartitionSpec as P

TH = 512
TW = 128
TI = 8
TJ = 4
SLOTS = TI * TJ
PAIR = 2
LAG = 2
CHUNKS = SLOTS // PAIR
SHORT = 12
W = TJ * TW
F32 = jnp.float32
RELAY_COST = 5 * 10**9


def cost(flops):
    return pl.CostEstimate(flops=flops, bytes_accessed=0, transcendentals=0)

BF16 = jnp.bfloat16


def params(limit=16):
    return pltpu.CompilerParams(vmem_limit_bytes=limit * 1024 * 1024)


def sds(shape, dtype):
    return jax.ShapeDtypeStruct(shape, dtype)


def site(r):
    return r // 8, (r // 2) % 4, r % 2


def row_of(z, y, c):
    return (z % 4) * 8 + (y % 4) * 2 + c


def row_perm(f):
    return [(r, row_of(*f(*site(r)))) for r in range(32)]


SWAP = row_perm(lambda z, y, c: (z, y, 1 - c))
SHIFT = {
    "y": [row_perm(lambda z, y, c, d=d: (z, y + d, c)) for d in range(4)],
    "z": [row_perm(lambda z, y, c, d=d: (z + d, y, c)) for d in range(4)],
}
RING = [(r * 4 + x, r * 4 + (x + (1 if r % 2 == 0 else 3)) % 4) for r in range(32) for x in range(4)]


def ring_step(x):
    return lax.ppermute(x, ("row", "col"), RING)


def scatter4(x, axis, me):
    h = x.shape[0] // 4
    total = lax.dynamic_slice_in_dim(x, me * h, h, 0)
    for d in (1, 3, 2):
        part = lax.dynamic_slice_in_dim(x, lax.rem(me + d, 4) * h, h, 0)
        total = total + lax.ppermute(part, "row", SHIFT[axis][d])
    return total


def gather4(x, axis, me):
    h = x.shape[0]
    out = jnp.zeros((4 * h, x.shape[1]), x.dtype)
    for d in range(4):
        got = x if d == 0 else lax.ppermute(x, "row", SHIFT[axis][d])
        out = lax.dynamic_update_slice_in_dim(out, got, lax.rem(me + 4 - d, 4) * h, 0)
    return out


def core_scatter(x, c):
    h = x.shape[0] // 2
    mine = lax.dynamic_slice_in_dim(x, c * h, h, 0)
    other = lax.dynamic_slice_in_dim(x, (1 - c) * h, h, 0)
    return mine + lax.ppermute(other, "row", SWAP)


def core_gather(x, c):
    got = lax.ppermute(x, "row", SWAP)
    first = jnp.where(c == 0, x, got)
    second = jnp.where(c == 0, got, x)
    return jnp.concatenate([first, second], 0)


def row_sum(x):
    _, y, c = site(lax.axis_index("row"))
    v = core_scatter(x, c)
    v = scatter4(v, "y", y)
    one, two, three = shifted(v, "z")
    v = gather4(v + one + two + three, "y", y)
    return core_gather(v, c)


def shifted(x, axis):
    if axis == "col":
        return [lax.ppermute(x, "col", [(i, (i + d) % 4) for i in range(4)]) for d in (1, 2, 3)]
    return [lax.ppermute(x, "row", SHIFT[axis][d]) for d in (1, 2, 3)]


ANY = pl.BlockSpec(memory_space=pl.ANY)
VMEM = pl.BlockSpec(memory_space=pltpu.VMEM)
SMEM = pl.BlockSpec(memory_space=pltpu.SMEM)
ROOT, HOP, CORE, ZPOS, COL = range(5)
UPPER = [(i, j) for i in range(TJ) for j in range(i, TJ)]
BLOCKS = len(UPPER) // 2 * TW
HALF = BLOCKS + 32
QUARTER = HALF // 4


def kept(shape):
    return pltpu.VMEM(shape, F32)


FILED = kept((TI * TH, W))


def pin(x):
    return pltpu.with_memory_space_constraint(x, pltpu.VMEM)


def in_hbm(x):
    return pltpu.with_memory_space_constraint(x, pltpu.HBM)


def split(x):
    high = x.astype(BF16)
    return high, (x - high.astype(F32)).astype(BF16)


def dot(a, b):
    return jnp.dot(a, b, preferred_element_type=F32)


def hdot(a, b, dims):
    return lax.dot_general(a, b, (dims, ((), ())), precision=lax.Precision.HIGHEST, preferred_element_type=F32)


def call(body, ins, outs, shapes, name, scratch=(), aliases=None, limit=16, flops=0):
    return pl.pallas_call(
        body,
        in_specs=ins,
        out_specs=outs,
        out_shape=shapes,
        scratch_shapes=list(scratch),
        input_output_aliases=aliases or {},
        compiler_params=params(limit),
        cost_estimate=cost(flops),
        name=name,
    )


def find(full, wanted):
    seen, place, found = jnp.int32(0), jnp.int32(0), jnp.int32(0)
    for t in range(SLOTS):
        hit = jnp.where((full[t] > 0) & (seen == wanted), 1, 0)
        place += hit * t
        found += hit
        seen += full[t]
    return place, found > 0


def relay_body(step, start, stop, fresh, choosing, last, me, own, *refs):
    refs = list(refs)
    root = me[ROOT] > 0
    others = [refs.pop(0) for _ in range(3)] if choosing else []
    x_ref = refs.pop(0)
    got = None if step < LAG else refs.pop(0)
    if not fresh:
        refs.pop(0)
    filed = refs.pop(0)
    send = None if last else refs.pop(0)
    seen = refs.pop(0) if choosing else None
    (sem,) = refs
    full = []
    for t in range(SLOTS):
        at = t % TI, t // TI
        flag = own[at]
        for d, other in enumerate(others, 1):
            flag = jnp.where(me[COL] == d, other[at], flag)
        if seen is not None:
            seen[at] = flag
        full.append(flag)
    chunk = start + step - me[HOP] * LAG
    live = (chunk >= start) & (chunk < stop)

    def each(act):
        for e in range(PAIR):
            place, found = places[e]
            rows = pl.ds(pl.multiple_of((place % TI) * TH, TH), TH)
            cols = pl.ds(pl.multiple_of((place // TI) * TW, TW), TW)
            part = pl.ds(e * TH, TH)

            def move(src, e=e, rows=rows, cols=cols, part=part):
                act(pltpu.make_async_copy(src, filed.at[rows, cols], sem.at[2 * e]))
                if send is not None:
                    act(pltpu.make_async_copy(src, send.at[part, :], sem.at[2 * e + 1]))

            @pl.when(found & live & root)
            def _(move=move, rows=rows, cols=cols):
                move(x_ref.at[rows, cols])

            if got is not None:

                @pl.when(found & live & jnp.logical_not(root))
                def _(move=move, part=part):
                    move(got.at[part, :])

    places = [find(full, chunk * PAIR + e) for e in range(PAIR)]
    each(lambda c: c.start())
    each(lambda c: c.wait())


def relay(step, start, stop, last, me, own, others, x, got, filed):
    ins, args = [SMEM] * (2 + len(others)) + [ANY], [me, own, *others, x]
    if step >= LAG:
        ins.append(ANY)
        args.append(got)
    aliases = {}
    if filed is not None:
        aliases = {len(args): 0}
        ins.append(ANY)
        args.append(pin(filed))
    shapes, outs = [FILED], [ANY]
    if not last:
        shapes.append(kept((PAIR * TH, TW)))
        outs.append(ANY)
    if others:
        shapes.append(sds((TI, TJ), jnp.int32))
        outs.append(SMEM)
    out = list(
        call(
            functools.partial(relay_body, step, start, stop, filed is None, bool(others), last),
            ins,
            outs,
            shapes,
            "relay",
            [pltpu.SemaphoreType.DMA((2 * PAIR,))],
            aliases,
            4,
            RELAY_COST,
        )(*args)
    )
    filed = out.pop(0)
    send = None if last else out.pop(0)
    return filed, send, out.pop(0) if others else None


def load_body(x_ref, out, sem):
    copies = [
        pltpu.make_async_copy(x_ref.at[pl.ds(i * TH, TH), :], out.at[pl.ds(i * TH, TH), :], sem.at[i]) for i in range(TI)
    ]
    for c in copies:
        c.start()
    for c in copies:
        c.wait()


def load(x):
    return call(load_body, [ANY], ANY, FILED, "load", [pltpu.SemaphoreType.DMA((TI,))])(x)


def gram_body(me, occ, x_ref, filed_in, keep, give, filed, gram_ref, cross_ref):
    i = pl.program_id(0)

    @pl.when(i == 0)
    def _():
        gram_ref[...] = jnp.zeros_like(gram_ref)
        cross_ref[...] = jnp.zeros_like(cross_ref)

    @pl.when(me[ROOT] > 0)
    def _():
        x = jnp.concatenate([x_ref[:, j * TW : (j + 1) * TW] * occ[i, j].astype(F32) for j in range(TJ)], 1)
        high, low = split(x)
        h = W // 2
        high_t, low_t = high.T, low.T
        gram_ref[:h, :] += dot(high_t[:h], high) + dot(low_t[:h], low)
        gram_ref[h:, h:] += dot(high_t[h:], high[:, h:]) + dot(low_t[h:], low[:, h:])
        cross_ref[...] += dot(high_t, low)

    @pl.when(i == TI - 1)
    def _():
        full = jnp.int32(0)
        for t in range(SLOTS):
            full += occ[t % TI, t // TI]
        over = jnp.where(full > SHORT * PAIR, 1.0, 0.0)
        keep[BLOCKS:, :] = jnp.full((HALF - BLOCKS, TW), over, F32)
        give[BLOCKS:, :] = jnp.full((HALF - BLOCKS, TW), over, F32)
        for b, (r, q) in enumerate(UPPER):
            rows, cols = slice(r * TW, (r + 1) * TW), slice(q * TW, (q + 1) * TW)
            block = gram_ref[rows, cols] + cross_ref[rows, cols] + cross_ref[cols, rows].T
            part, at = divmod(b * TW, BLOCKS)
            mine = me[CORE] == part

            @pl.when(mine)
            def _(block=block, at=at):
                keep[at : at + TW, :] = block

            @pl.when(jnp.logical_not(mine))
            def _(block=block, at=at):
                give[at : at + TW, :] = block


def gram_part(me, occ, x, filed):
    whole = pl.BlockSpec((HALF, TW), lambda i, *_: (0, 0))
    return pl.pallas_call(
        gram_body,
        grid_spec=pltpu.PrefetchScalarGridSpec(
            num_scalar_prefetch=2,
            grid=(TI,),
            in_specs=[pl.BlockSpec((TH, W), lambda i, me, occ: (i * me[ROOT], 0)), ANY],
            out_specs=[whole, whole, ANY],
            scratch_shapes=[pltpu.VMEM((W, W), F32), pltpu.VMEM((W, W), F32)],
        ),
        out_shape=[sds((HALF, TW), F32), sds((HALF, TW), F32), FILED],
        input_output_aliases={3: 2},
        compiler_params=params(24),
        cost_estimate=cost(0),
        name="gram_part",
    )(me, occ, pin(x), pin(filed))


def add_body(*refs):
    ins, (_, out, _) = refs[:-3], refs[-3:]
    total = ins[0][...]
    for r in ins[1:]:
        total = total + r[...]
    out[...] = total


def add_parts(parts, filed):
    n = len(parts)
    return call(
        add_body,
        [VMEM] * n + [ANY],
        [VMEM, ANY],
        [sds(parts[0].shape, F32), FILED],
        "add_parts",
        aliases={n: 1},
    )(*parts, pin(filed))


def add_cut_body(me, a, b, c, d, _, own, one, two, three, __, total):
    total[...] = a[...] + b[...] + c[...] + d[...]
    for k, out in enumerate((own, one, two, three)):
        at = lax.rem(me[ZPOS] + k, 4) * QUARTER
        out[...] = total[pl.ds(pl.multiple_of(at, 8), QUARTER), :]


def add_cut(me, parts, filed):
    return call(
        add_cut_body,
        [SMEM] + [VMEM] * 4 + [ANY],
        [VMEM] * 4 + [ANY],
        [sds((QUARTER, TW), F32)] * 4 + [FILED],
        "add_cut",
        [pltpu.VMEM((HALF, TW), F32)],
        {5: 4},
    )(me, *parts, pin(filed))


def choose_body(me, a, b, c, d, _, out, __):
    for k, ref in enumerate((a, b, c, d)):

        @pl.when(me[COL] == k)
        def _(ref=ref):
            out[...] = ref[...]


def choose(me, parts, filed):
    return call(
        choose_body,
        [SMEM] + [VMEM] * 4 + [ANY],
        [VMEM, ANY],
        [sds((QUARTER, TW), F32), FILED],
        "choose",
        aliases={5: 1},
    )(me, *parts, pin(filed))


def stack_body(me, a, b, c, d, _, out, __):
    for k, ref in enumerate((a, b, c, d)):
        at = lax.rem(me[ZPOS] + 4 - k, 4) * QUARTER
        out[pl.ds(pl.multiple_of(at, 8), QUARTER), :] = ref[...]


def stack(me, parts, filed):
    return call(
        stack_body,
        [SMEM] + [VMEM] * 4 + [ANY],
        [VMEM, ANY],
        [sds((HALF, TW), F32), FILED],
        "stack",
        aliases={5: 1},
    )(me, *parts, pin(filed))


def unpack_body(me, mine, other, _, s_ref, e_ref, over_ref, __):
    over_ref[...] = mine[BLOCKS : BLOCKS + 8, :]
    s_ref[...] = jnp.zeros_like(s_ref)
    for b, (r, q) in enumerate(UPPER):
        part, at = divmod(b * TW, BLOCKS)
        block = jnp.where(me[CORE] == part, mine[at : at + TW, :], other[at : at + TW, :])
        s_ref[r * TW : (r + 1) * TW, q * TW : (q + 1) * TW] = block
        if b == 0:
            e_ref[:, :TW] = block
    e_ref[:, TW:] = unit()


def unpack(me, mine, other, filed):
    return call(
        unpack_body,
        [SMEM, VMEM, VMEM, ANY],
        [VMEM, VMEM, VMEM, ANY],
        [sds((W, W), F32), sds((TW, 2 * TW), F32), sds((8, TW), F32), FILED],
        "unpack",
        aliases={3: 3},
    )(me, mine, other, pin(filed))


def unit():
    r = lax.broadcasted_iota(jnp.int32, (TW, TW), 0)
    c = lax.broadcasted_iota(jnp.int32, (TW, TW), 1)
    return jnp.where(r == c, 1.0, 0.0).astype(F32)


def eliminate(m_rows, v_rows, start, stop):
    groups = len(m_rows)
    full = (8, m_rows[0].shape[1])
    sub = lax.broadcasted_iota(jnp.int32, full, 0)

    def row(x, r):
        return jnp.broadcast_to(x[r : r + 1, :], full)

    for g in range(start, stop):
        lanes = [8 * g + k for k in range(8)]
        columns = [jnp.broadcast_to(m_rows[g][:, lane : lane + 1], full) for lane in lanes]
        a = {(r, k): row(columns[k], r) for k in range(8) for r in range(k, 8)}
        rm = [row(m_rows[g], r) for r in range(8)]
        rv = [row(v_rows[g], r) for r in range(8)]
        inverse = []
        for k in range(8):
            scale = lax.rsqrt(a[k, k])
            inverse.append(scale)
            for r in range(k + 1, 8):
                a[r, k] = a[r, k] * scale
            for c in range(k + 1, 8):
                for r in range(c, 8):
                    a[r, c] = a[r, c] - a[r, k] * a[c, k]
            rm[k] = rm[k] * scale
            rv[k] = rv[k] * scale
            for r in range(k + 1, 8):
                rm[r] = rm[r] - a[r, k] * rm[k]
                rv[r] = rv[r] - a[r, k] * rv[k]
        for i in range(g + 1, groups):
            factor = [jnp.broadcast_to(m_rows[i][:, lane : lane + 1], full) for lane in lanes]
            new_m, new_v = m_rows[i], v_rows[i]
            for k in range(8):
                factor[k] = factor[k] * inverse[k]
                for r in range(k + 1, 8):
                    factor[r] = factor[r] - factor[k] * a[r, k]
                new_m = new_m - factor[k] * rm[k]
                new_v = new_v - factor[k] * rv[k]
            m_rows[i], v_rows[i] = new_m, new_v
        top_m, top_v = rm[0], rv[0]
        for r in range(1, 8):
            top_m = jnp.where(sub == r, rm[r], top_m)
            top_v = jnp.where(sub == r, rv[r], top_v)
        m_rows[g], v_rows[g] = top_m, top_v
    return m_rows, v_rows


def eliminate_body(e_in, _, e_out, __):
    groups = range(TW // 8)
    m_rows = [e_in[8 * g : 8 * g + 8, :TW] for g in groups]
    v_rows = [e_in[8 * g : 8 * g + 8, TW:] for g in groups]
    m_rows, v_rows = eliminate(m_rows, v_rows, 0, TW // 8)
    r = lax.broadcasted_iota(jnp.int32, (8, TW), 0)
    c = lax.broadcasted_iota(jnp.int32, (8, TW), 1)
    for g in groups:
        e_out[8 * g : 8 * g + 8, :TW] = jnp.where(r + 8 * g <= c, m_rows[g], 0.0)
        e_out[8 * g : 8 * g + 8, TW:] = v_rows[g]


def eliminate_block(e, filed):
    return call(
        eliminate_body, [VMEM, ANY], [VMEM, ANY], [sds((TW, 2 * TW), F32), FILED], "eliminate", aliases={1: 1}
    )(e, pin(filed))


def spread_body(b, e_in, s_in, v_in, s_ref, v_ref, e_out):
    lo, hi = b * TW, (b + 1) * TW
    s_ref[...] = s_in[...]
    if b == 0:
        v_ref[...] = jnp.zeros_like(v_ref)
    else:
        v_ref[...] = v_in[...]
    inv = e_in[:, TW:]
    s_ref[lo:hi, lo:hi] = e_in[:, :TW]
    v_ref[lo:hi, lo:hi] = inv
    if b > 0:
        v_ref[lo:hi, :lo] = hdot(inv, v_in[lo:hi, :lo], ((1,), (0,)))
    if hi < W:
        right = hdot(inv, s_in[lo:hi, hi:], ((1,), (0,)))
        s_ref[lo:hi, hi:] = right
        s_ref[hi:, hi:] -= hdot(right, right, ((0,), (0,)))
        s_ref[hi:, lo:hi] = jnp.zeros((W - hi, TW), F32)
        v_ref[hi:, :hi] -= hdot(right, v_ref[lo:hi, :hi], ((0,), (0,)))
        e_out[:, :TW] = s_ref[hi : hi + TW, hi : hi + TW]
        e_out[:, TW:] = unit()
    else:
        e_out[0] = s_ref[: W // 2, : W // 2]
        e_out[1] = s_ref[W // 2 :, W // 2 :]


def spread(b, e, s, v):
    return call(
        functools.partial(spread_body, b),
        [VMEM] * 3,
        [VMEM] * 3,
        [sds((W, W), F32), sds((W, W), F32), sds((TW, 2 * TW) if b < TJ - 1 else (2, W // 2, W // 2), F32)],
        "spread",
    )(e, s, v)


def masked(ref, flags, i, upto=TJ):
    parts = []
    for j in range(upto):
        block = ref[:, j * TW : (j + 1) * TW]
        parts.append(jnp.where(flags[i, j] > 0, block, jnp.zeros_like(block)))
    return jnp.concatenate(parts, 1)


def project_body(me, occ, panel, x_ref, a_ref, c_ref):
    i = pl.program_id(0)

    @pl.when(i == 0)
    def _():
        c_ref[...] = jnp.zeros_like(c_ref)

    @pl.when(me[ROOT] == 0)
    def _():
        ah, al = split(masked(a_ref, panel, i))
        bh, bl = split(masked(x_ref, occ, i))
        ah_t, al_t = ah.T, al.T
        c_ref[...] += dot(jnp.concatenate([ah_t, al_t, ah_t], 1), jnp.concatenate([bh, bh, bl], 0))


def project(me, occ, panel, x, filed):
    block = pl.BlockSpec((TH, W), lambda i, *_: (i, 0))
    return pl.pallas_call(
        project_body,
        grid_spec=pltpu.PrefetchScalarGridSpec(
            num_scalar_prefetch=3,
            grid=(TI,),
            in_specs=[block, block],
            out_specs=pl.BlockSpec((W, W), lambda i, *_: (0, 0)),
        ),
        out_shape=sds((W, W), F32),
        compiler_params=params(24),
        cost_estimate=cost(0),
        name="project",
    )(me, occ, panel, pin(x), in_hbm(filed))


def solve_body(scale, me, v_ref, c_ref, high_ref, low_ref):
    v = v_ref[...]
    coef = hdot(v, hdot(v, c_ref[...], ((1,), (0,))), ((0,), (0,)))
    coef = jnp.where(me[ROOT] > 0, -scale * v.T, coef)
    high_ref[...], low_ref[...] = split(coef)


def solve(scale, me, inv, proj):
    return call(
        functools.partial(solve_body, scale),
        [SMEM, VMEM, VMEM],
        [VMEM, VMEM],
        [sds((W, W), BF16)] * 2,
        "solve",
    )(me, inv, proj)


def finish_body(me, occ, panel, x_ref, a_ref, xh, xl, out_ref):
    i = pl.program_id(0)
    keep = 1 - me[ROOT]
    ah, al = split(masked(a_ref, panel, i))
    taken = dot(jnp.concatenate([ah, al, ah], 1), jnp.concatenate([xh[...], xh[...], xl[...]], 0))
    for j in range(TJ):
        at = slice(j * TW, (j + 1) * TW)
        out_ref[:, at] = x_ref[:, at] * (occ[i, j] * keep).astype(F32) - taken[:, at]


def finish(me, occ, panel, x, filed, xh, xl):
    rows = TI * TH
    block = pl.BlockSpec((TH, W), lambda i, *_: (i, 0))
    whole = pl.BlockSpec((W, W), lambda i, *_: (0, 0))
    return pl.pallas_call(
        finish_body,
        grid_spec=pltpu.PrefetchScalarGridSpec(
            num_scalar_prefetch=3,
            grid=(TI,),
            in_specs=[block, block, whole, whole],
            out_specs=block,
        ),
        out_shape=sds((rows, W), F32),
        compiler_params=params(24),
        cost_estimate=cost(0),
        name="finish",
    )(me, occ, panel, pin(x), in_hbm(filed), xh, xl)


def shards(snapshots, tiles):
    col = lax.axis_index("col")
    z, _, core = site(lax.axis_index("row"))
    root = col == 0
    hop = jnp.where(core == 0, col, (4 - col) % 4)
    scale = math.sqrt(snapshots.shape[0] * lax.axis_size("row"))
    me = jnp.stack([root.astype(jnp.int32), hop, core, z, col]).astype(jnp.int32)
    state = {"x": in_hbm(snapshots), "panel": tiles}
    flags = shifted(tiles, "col")

    def ring(start, stop, filed, beside=None):
        got = [None] * LAG
        steps = stop - start + 3 * LAG
        for s in range(steps):
            last = s >= steps - LAG
            others = flags if start == 0 and s == LAG else []
            filed, send, seen = relay(s, start, stop, last, me, state["panel"], others, state["x"], got[s % LAG], filed)
            if others:
                state["panel"] = seen
            if not last:
                got[s % LAG] = ring_step(send)
            if beside is not None:
                filed = beside(s, filed)
        return filed

    def gram_stage(name, filed):
        if name == "parts":
            state["x"] = load(snapshots)
            keep, give, filed = gram_part(me, tiles, state["x"], filed)
            state["v"] = [keep, lax.ppermute(give, "row", SWAP)]
        elif name == "core":
            v, filed = add_parts(state["v"], filed)
            state["v"] = [v] + shifted(v, "y")
        elif name == "y":
            own, one, two, three, filed = add_cut(me, state["v"], filed)
            sent = [lax.ppermute(p, "row", SHIFT["z"][d]) for d, p in ((1, one), (2, two), (3, three))]
            state["v"] = [own] + sent
        elif name == "z":
            v, filed = add_parts(state["v"], filed)
            state["v"] = [v] + shifted(v, "col")
        elif name == "col":
            v, filed = choose(me, state["v"], filed)
            state["v"] = [v] + shifted(v, "z")
        elif name == "stack":
            v, filed = stack(me, state["v"], filed)
            state["v"] = [v, lax.ppermute(v, "row", SWAP)]
        elif name == "unpack":
            state["s"], state["e"], state["over"], filed = unpack(me, *state["v"], filed)
            state["inv"] = state["s"]
        elif name[0] == "e":
            state["e"], filed = eliminate_block(state["e"], filed)
        else:
            state["s"], state["inv"], state["e"] = spread(int(name[1]), state["e"], state["s"], state["inv"])
        return filed

    plan = {1: ["parts"], 2: ["core"], 5: ["y"], 7: ["z"], 9: ["col"], 10: ["stack"], 11: ["unpack"]}
    plan.update({12: ["e0", "s0"], 13: ["e1", "s1"], 14: ["e2", "s2"], 15: ["e3", "s3"]})

    def beside(s, filed):
        for name in plan.get(s, []):
            filed = gram_stage(name, filed)
        return filed

    filed = ring(0, SHORT, None, beside)
    filed = lax.cond(state["over"][0, 0] > 0.5, lambda f: ring(SHORT, CHUNKS, f), lambda f: f, filed)
    x, panel = state["x"], state["panel"]
    proj = row_sum(project(me, tiles, panel, x, filed))
    xh, xl = solve(scale, me, state["inv"], proj)
    out = finish(me, tiles, panel, x, filed, xh, xl)
    return state["e"], out


def solution(mesh):
    placed = (P("row", "col"), P("row", "col"))
    return jax.shard_map(shards, mesh=mesh, in_specs=placed, out_specs=(P(), P("row", "col")), check_vma=False)
```

```python
import functools
import math

import jax
import jax.numpy as jnp
from jax import lax
from jax.experimental import pallas as pl
from jax.experimental.pallas import tpu as pltpu
from jax.sharding import PartitionSpec as P

TH = 512
TW = 128
TI = 8
TJ = 4
SLOTS = TI * TJ
PAIR = 2
LAG = 2
CHUNKS = SLOTS // PAIR
SHORT = 12
W = TJ * TW
F32 = jnp.float32
RELAY_COST = 5 * 10**9


def cost(flops):
    return pl.CostEstimate(flops=flops, bytes_accessed=0, transcendentals=0)

BF16 = jnp.bfloat16


def params(limit=16):
    return pltpu.CompilerParams(vmem_limit_bytes=limit * 1024 * 1024)


def sds(shape, dtype):
    return jax.ShapeDtypeStruct(shape, dtype)


def site(r):
    return r // 8, (r // 2) % 4, r % 2


def row_of(z, y, c):
    return (z % 4) * 8 + (y % 4) * 2 + c


def row_perm(f):
    return [(r, row_of(*f(*site(r)))) for r in range(32)]


SWAP = row_perm(lambda z, y, c: (z, y, 1 - c))
SHIFT = {
    "y": [row_perm(lambda z, y, c, d=d: (z, y + d, c)) for d in range(4)],
    "z": [row_perm(lambda z, y, c, d=d: (z + d, y, c)) for d in range(4)],
}
RING = [(r * 4 + x, r * 4 + (x + (1 if r % 2 == 0 else 3)) % 4) for r in range(32) for x in range(4)]


def ring_step(x):
    return lax.ppermute(x, ("row", "col"), RING)


def scatter4(x, axis, me):
    h = x.shape[0] // 4
    total = lax.dynamic_slice_in_dim(x, me * h, h, 0)
    for d in (1, 3, 2):
        part = lax.dynamic_slice_in_dim(x, lax.rem(me + d, 4) * h, h, 0)
        total = total + lax.ppermute(part, "row", SHIFT[axis][d])
    return total


def gather4(x, axis, me):
    h = x.shape[0]
    out = jnp.zeros((4 * h, x.shape[1]), x.dtype)
    for d in range(4):
        got = x if d == 0 else lax.ppermute(x, "row", SHIFT[axis][d])
        out = lax.dynamic_update_slice_in_dim(out, got, lax.rem(me + 4 - d, 4) * h, 0)
    return out


def core_scatter(x, c):
    h = x.shape[0] // 2
    mine = lax.dynamic_slice_in_dim(x, c * h, h, 0)
    other = lax.dynamic_slice_in_dim(x, (1 - c) * h, h, 0)
    return mine + lax.ppermute(other, "row", SWAP)


def core_gather(x, c):
    got = lax.ppermute(x, "row", SWAP)
    first = jnp.where(c == 0, x, got)
    second = jnp.where(c == 0, got, x)
    return jnp.concatenate([first, second], 0)


def row_sum(x):
    _, y, c = site(lax.axis_index("row"))
    v = core_scatter(x, c)
    v = scatter4(v, "y", y)
    one, two, three = shifted(v, "z")
    v = gather4(v + one + two + three, "y", y)
    return core_gather(v, c)


def shifted(x, axis):
    if axis == "col":
        return [lax.ppermute(x, "col", [(i, (i + d) % 4) for i in range(4)]) for d in (1, 2, 3)]
    return [lax.ppermute(x, "row", SHIFT[axis][d]) for d in (1, 2, 3)]


ANY = pl.BlockSpec(memory_space=pl.ANY)
VMEM = pl.BlockSpec(memory_space=pltpu.VMEM)
SMEM = pl.BlockSpec(memory_space=pltpu.SMEM)
ROOT, HOP, CORE, YPOS, COL = range(5)
UPPER = [(i, j) for i in range(TJ) for j in range(i, TJ)]
BLOCKS = len(UPPER) // 2 * TW
HALF = BLOCKS + 32
QUARTER = HALF // 4


def kept(shape):
    return pltpu.VMEM(shape, F32)


FILED = kept((TI * TH, W))


def pin(x):
    return pltpu.with_memory_space_constraint(x, pltpu.VMEM)


def in_hbm(x):
    return pltpu.with_memory_space_constraint(x, pltpu.HBM)


def split(x):
    high = x.astype(BF16)
    return high, (x - high.astype(F32)).astype(BF16)


def dot(a, b):
    return jnp.dot(a, b, preferred_element_type=F32)


def hdot(a, b, dims):
    return lax.dot_general(a, b, (dims, ((), ())), precision=lax.Precision.HIGHEST, preferred_element_type=F32)


def call(body, ins, outs, shapes, name, scratch=(), aliases=None, limit=16, flops=0):
    return pl.pallas_call(
        body,
        in_specs=ins,
        out_specs=outs,
        out_shape=shapes,
        scratch_shapes=list(scratch),
        input_output_aliases=aliases or {},
        compiler_params=params(limit),
        cost_estimate=cost(flops),
        name=name,
    )


def find(full, wanted):
    seen, place, found = jnp.int32(0), jnp.int32(0), jnp.int32(0)
    for t in range(SLOTS):
        hit = jnp.where((full[t] > 0) & (seen == wanted), 1, 0)
        place += hit * t
        found += hit
        seen += full[t]
    return place, found > 0


def relay_body(step, start, stop, fresh, choosing, last, me, own, *refs):
    refs = list(refs)
    root = me[ROOT] > 0
    others = [refs.pop(0) for _ in range(3)] if choosing else []
    x_ref = refs.pop(0)
    got = None if step < LAG else refs.pop(0)
    if not fresh:
        refs.pop(0)
    filed = refs.pop(0)
    send = None if last else refs.pop(0)
    seen = refs.pop(0) if choosing else None
    (sem,) = refs
    full = []
    for t in range(SLOTS):
        at = t % TI, t // TI
        flag = own[at]
        for d, other in enumerate(others, 1):
            flag = jnp.where(me[COL] == d, other[at], flag)
        if seen is not None:
            seen[at] = flag
        full.append(flag)
    chunk = start + step - me[HOP] * LAG
    live = (chunk >= start) & (chunk < stop)

    def each(act):
        for e in range(PAIR):
            place, found = places[e]
            rows = pl.ds(pl.multiple_of((place % TI) * TH, TH), TH)
            cols = pl.ds(pl.multiple_of((place // TI) * TW, TW), TW)
            part = pl.ds(e * TH, TH)

            def move(src, e=e, rows=rows, cols=cols, part=part):
                act(pltpu.make_async_copy(src, filed.at[rows, cols], sem.at[2 * e]))
                if send is not None:
                    act(pltpu.make_async_copy(src, send.at[part, :], sem.at[2 * e + 1]))

            @pl.when(found & live & root)
            def _(move=move, rows=rows, cols=cols):
                move(x_ref.at[rows, cols])

            if got is not None:

                @pl.when(found & live & jnp.logical_not(root))
                def _(move=move, part=part):
                    move(got.at[part, :])

    places = [find(full, chunk * PAIR + e) for e in range(PAIR)]
    each(lambda c: c.start())
    each(lambda c: c.wait())


def relay(step, start, stop, last, me, own, others, x, got, filed):
    ins, args = [SMEM] * (2 + len(others)) + [ANY], [me, own, *others, x]
    if step >= LAG:
        ins.append(ANY)
        args.append(got)
    aliases = {}
    if filed is not None:
        aliases = {len(args): 0}
        ins.append(ANY)
        args.append(pin(filed))
    shapes, outs = [FILED], [ANY]
    if not last:
        shapes.append(kept((PAIR * TH, TW)))
        outs.append(ANY)
    if others:
        shapes.append(sds((TI, TJ), jnp.int32))
        outs.append(SMEM)
    out = list(
        call(
            functools.partial(relay_body, step, start, stop, filed is None, bool(others), last),
            ins,
            outs,
            shapes,
            "relay",
            [pltpu.SemaphoreType.DMA((2 * PAIR,))],
            aliases,
            4,
            RELAY_COST,
        )(*args)
    )
    filed = out.pop(0)
    send = None if last else out.pop(0)
    return filed, send, out.pop(0) if others else None


def load_body(x_ref, out, sem):
    copies = [
        pltpu.make_async_copy(x_ref.at[pl.ds(i * TH, TH), :], out.at[pl.ds(i * TH, TH), :], sem.at[i]) for i in range(TI)
    ]
    for c in copies:
        c.start()
    for c in copies:
        c.wait()


def load(x):
    return call(load_body, [ANY], ANY, FILED, "load", [pltpu.SemaphoreType.DMA((TI,))])(x)


def gram_body(me, occ, x_ref, filed_in, keep, give, filed, gram_ref, cross_ref):
    i = pl.program_id(0)

    @pl.when(i == 0)
    def _():
        gram_ref[...] = jnp.zeros_like(gram_ref)
        cross_ref[...] = jnp.zeros_like(cross_ref)

    @pl.when(me[ROOT] > 0)
    def _():
        x = jnp.concatenate([x_ref[:, j * TW : (j + 1) * TW] * occ[i, j].astype(F32) for j in range(TJ)], 1)
        high, low = split(x)
        h = W // 2
        high_t, low_t = high.T, low.T
        gram_ref[:h, :] += dot(high_t[:h], high) + dot(low_t[:h], low)
        gram_ref[h:, h:] += dot(high_t[h:], high[:, h:]) + dot(low_t[h:], low[:, h:])
        cross_ref[...] += dot(high_t, low)

    @pl.when(i == TI - 1)
    def _():
        full = jnp.int32(0)
        for t in range(SLOTS):
            full += occ[t % TI, t // TI]
        over = jnp.where(full > SHORT * PAIR, 1.0, 0.0)
        keep[BLOCKS:, :] = jnp.full((HALF - BLOCKS, TW), over, F32)
        give[BLOCKS:, :] = jnp.full((HALF - BLOCKS, TW), over, F32)
        for b, (r, q) in enumerate(UPPER):
            rows, cols = slice(r * TW, (r + 1) * TW), slice(q * TW, (q + 1) * TW)
            block = gram_ref[rows, cols] + cross_ref[rows, cols] + cross_ref[cols, rows].T
            part, at = divmod(b * TW, BLOCKS)
            mine = me[CORE] == part

            @pl.when(mine)
            def _(block=block, at=at):
                keep[at : at + TW, :] = block

            @pl.when(jnp.logical_not(mine))
            def _(block=block, at=at):
                give[at : at + TW, :] = block


def gram_part(me, occ, x, filed):
    whole = pl.BlockSpec((HALF, TW), lambda i, *_: (0, 0))
    return pl.pallas_call(
        gram_body,
        grid_spec=pltpu.PrefetchScalarGridSpec(
            num_scalar_prefetch=2,
            grid=(TI,),
            in_specs=[pl.BlockSpec((TH, W), lambda i, me, occ: (i * me[ROOT], 0)), ANY],
            out_specs=[whole, whole, ANY],
            scratch_shapes=[pltpu.VMEM((W, W), F32), pltpu.VMEM((W, W), F32)],
        ),
        out_shape=[sds((HALF, TW), F32), sds((HALF, TW), F32), FILED],
        input_output_aliases={3: 2},
        compiler_params=params(24),
        cost_estimate=cost(0),
        name="gram_part",
    )(me, occ, pin(x), pin(filed))


def add_body(*refs):
    ins, (_, out, _) = refs[:-3], refs[-3:]
    total = ins[0][...]
    for r in ins[1:]:
        total = total + r[...]
    out[...] = total


def add_parts(parts, filed):
    n = len(parts)
    return call(
        add_body,
        [VMEM] * n + [ANY],
        [VMEM, ANY],
        [sds(parts[0].shape, F32), FILED],
        "add_parts",
        aliases={n: 1},
    )(*parts, pin(filed))


def add_cut_body(me, a, b, _, own, one, two, three, __, total):
    total[...] = a[...] + b[...]
    for k, out in enumerate((own, one, two, three)):
        at = lax.rem(me[YPOS] + k, 4) * QUARTER
        out[...] = total[pl.ds(pl.multiple_of(at, 8), QUARTER), :]


def add_cut(me, parts, filed):
    return call(
        add_cut_body,
        [SMEM] + [VMEM] * 2 + [ANY],
        [VMEM] * 4 + [ANY],
        [sds((QUARTER, TW), F32)] * 4 + [FILED],
        "add_cut",
        [pltpu.VMEM((HALF, TW), F32)],
        {3: 4},
    )(me, *parts, pin(filed))


def choose_body(me, a, b, c, d, _, out, __):
    for k, ref in enumerate((a, b, c, d)):

        @pl.when(me[COL] == k)
        def _(ref=ref):
            out[...] = ref[...]


def choose(me, parts, filed):
    return call(
        choose_body,
        [SMEM] + [VMEM] * 4 + [ANY],
        [VMEM, ANY],
        [sds((QUARTER, TW), F32), FILED],
        "choose",
        aliases={5: 1},
    )(me, *parts, pin(filed))


def stack_body(me, a, b, c, d, _, out, __):
    for k, ref in enumerate((a, b, c, d)):
        at = lax.rem(me[YPOS] + 4 - k, 4) * QUARTER
        out[pl.ds(pl.multiple_of(at, 8), QUARTER), :] = ref[...]


def stack(me, parts, filed):
    return call(
        stack_body,
        [SMEM] + [VMEM] * 4 + [ANY],
        [VMEM, ANY],
        [sds((HALF, TW), F32), FILED],
        "stack",
        aliases={5: 1},
    )(me, *parts, pin(filed))


def unpack_body(me, mine, other, _, s_ref, e_ref, over_ref, __):
    over_ref[...] = mine[BLOCKS : BLOCKS + 8, :]
    s_ref[...] = jnp.zeros_like(s_ref)
    for b, (r, q) in enumerate(UPPER):
        part, at = divmod(b * TW, BLOCKS)
        block = jnp.where(me[CORE] == part, mine[at : at + TW, :], other[at : at + TW, :])
        s_ref[r * TW : (r + 1) * TW, q * TW : (q + 1) * TW] = block
        if b == 0:
            e_ref[:, :TW] = block
    e_ref[:, TW:] = unit()


def unpack(me, mine, other, filed):
    return call(
        unpack_body,
        [SMEM, VMEM, VMEM, ANY],
        [VMEM, VMEM, VMEM, ANY],
        [sds((W, W), F32), sds((TW, 2 * TW), F32), sds((8, TW), F32), FILED],
        "unpack",
        aliases={3: 3},
    )(me, mine, other, pin(filed))


def unit():
    r = lax.broadcasted_iota(jnp.int32, (TW, TW), 0)
    c = lax.broadcasted_iota(jnp.int32, (TW, TW), 1)
    return jnp.where(r == c, 1.0, 0.0).astype(F32)


def eliminate(m_rows, v_rows, start, stop):
    groups = len(m_rows)
    full = (8, m_rows[0].shape[1])
    sub = lax.broadcasted_iota(jnp.int32, full, 0)

    def row(x, r):
        return jnp.broadcast_to(x[r : r + 1, :], full)

    for g in range(start, stop):
        lanes = [8 * g + k for k in range(8)]
        columns = [jnp.broadcast_to(m_rows[g][:, lane : lane + 1], full) for lane in lanes]
        a = {(r, k): row(columns[k], r) for k in range(8) for r in range(k, 8)}
        rm = [row(m_rows[g], r) for r in range(8)]
        rv = [row(v_rows[g], r) for r in range(8)]
        inverse = []
        for k in range(8):
            scale = lax.rsqrt(a[k, k])
            inverse.append(scale)
            for r in range(k + 1, 8):
                a[r, k] = a[r, k] * scale
            for c in range(k + 1, 8):
                for r in range(c, 8):
                    a[r, c] = a[r, c] - a[r, k] * a[c, k]
            rm[k] = rm[k] * scale
            rv[k] = rv[k] * scale
            for r in range(k + 1, 8):
                rm[r] = rm[r] - a[r, k] * rm[k]
                rv[r] = rv[r] - a[r, k] * rv[k]
        for i in range(g + 1, groups):
            factor = [jnp.broadcast_to(m_rows[i][:, lane : lane + 1], full) for lane in lanes]
            new_m, new_v = m_rows[i], v_rows[i]
            for k in range(8):
                factor[k] = factor[k] * inverse[k]
                for r in range(k + 1, 8):
                    factor[r] = factor[r] - factor[k] * a[r, k]
                new_m = new_m - factor[k] * rm[k]
                new_v = new_v - factor[k] * rv[k]
            m_rows[i], v_rows[i] = new_m, new_v
        top_m, top_v = rm[0], rv[0]
        for r in range(1, 8):
            top_m = jnp.where(sub == r, rm[r], top_m)
            top_v = jnp.where(sub == r, rv[r], top_v)
        m_rows[g], v_rows[g] = top_m, top_v
    return m_rows, v_rows


def eliminate_body(e_in, _, e_out, __):
    groups = range(TW // 8)
    m_rows = [e_in[8 * g : 8 * g + 8, :TW] for g in groups]
    v_rows = [e_in[8 * g : 8 * g + 8, TW:] for g in groups]
    m_rows, v_rows = eliminate(m_rows, v_rows, 0, TW // 8)
    r = lax.broadcasted_iota(jnp.int32, (8, TW), 0)
    c = lax.broadcasted_iota(jnp.int32, (8, TW), 1)
    for g in groups:
        e_out[8 * g : 8 * g + 8, :TW] = jnp.where(r + 8 * g <= c, m_rows[g], 0.0)
        e_out[8 * g : 8 * g + 8, TW:] = v_rows[g]


def eliminate_block(e, filed):
    return call(
        eliminate_body, [VMEM, ANY], [VMEM, ANY], [sds((TW, 2 * TW), F32), FILED], "eliminate", aliases={1: 1}
    )(e, pin(filed))


def spread_body(b, e_in, s_in, v_in, s_ref, v_ref, e_out):
    lo, hi = b * TW, (b + 1) * TW
    s_ref[...] = s_in[...]
    if b == 0:
        v_ref[...] = jnp.zeros_like(v_ref)
    else:
        v_ref[...] = v_in[...]
    inv = e_in[:, TW:]
    s_ref[lo:hi, lo:hi] = e_in[:, :TW]
    v_ref[lo:hi, lo:hi] = inv
    if b > 0:
        v_ref[lo:hi, :lo] = hdot(inv, v_in[lo:hi, :lo], ((1,), (0,)))
    if hi < W:
        right = hdot(inv, s_in[lo:hi, hi:], ((1,), (0,)))
        s_ref[lo:hi, hi:] = right
        s_ref[hi:, hi:] -= hdot(right, right, ((0,), (0,)))
        s_ref[hi:, lo:hi] = jnp.zeros((W - hi, TW), F32)
        v_ref[hi:, :hi] -= hdot(right, v_ref[lo:hi, :hi], ((0,), (0,)))
        e_out[:, :TW] = s_ref[hi : hi + TW, hi : hi + TW]
        e_out[:, TW:] = unit()
    else:
        e_out[0] = s_ref[: W // 2, : W // 2]
        e_out[1] = s_ref[W // 2 :, W // 2 :]


def spread(b, e, s, v):
    return call(
        functools.partial(spread_body, b),
        [VMEM] * 3,
        [VMEM] * 3,
        [sds((W, W), F32), sds((W, W), F32), sds((TW, 2 * TW) if b < TJ - 1 else (2, W // 2, W // 2), F32)],
        "spread",
    )(e, s, v)


def masked(ref, flags, i):
    rows = []
    for r in range(DEEP):
        parts = []
        for j in range(TJ):
            block = ref[r * TH : (r + 1) * TH, j * TW : (j + 1) * TW]
            parts.append(jnp.where(flags[i * DEEP + r, j] > 0, block, jnp.zeros_like(block)))
        rows.append(jnp.concatenate(parts, 1))
    return jnp.concatenate(rows, 0)


DEEP = 2


def project_body(me, occ, panel, x_ref, a_ref, c_ref):
    i = pl.program_id(0)

    @pl.when(i == 0)
    def _():
        c_ref[...] = jnp.zeros_like(c_ref)

    @pl.when(me[ROOT] == 0)
    def _():
        ah, al = split(masked(a_ref, panel, i))
        bh, bl = split(masked(x_ref, occ, i))
        ah_t, al_t = ah.T, al.T
        c_ref[...] += dot(jnp.concatenate([ah_t, al_t, ah_t], 1), jnp.concatenate([bh, bh, bl], 0))


def project(me, occ, panel, x, filed):
    block = pl.BlockSpec((DEEP * TH, W), lambda i, *_: (i, 0))
    return pl.pallas_call(
        project_body,
        grid_spec=pltpu.PrefetchScalarGridSpec(
            num_scalar_prefetch=3,
            grid=(TI // DEEP,),
            in_specs=[block, block],
            out_specs=pl.BlockSpec((W, W), lambda i, *_: (0, 0)),
        ),
        out_shape=sds((W, W), F32),
        compiler_params=params(40),
        cost_estimate=cost(0),
        name="project",
    )(me, occ, panel, in_hbm(x), in_hbm(filed))


def solve_body(scale, me, v_ref, c_ref, high_ref, low_ref):
    v = v_ref[...]
    coef = hdot(v, hdot(v, c_ref[...], ((1,), (0,))), ((0,), (0,)))
    coef = jnp.where(me[ROOT] > 0, -scale * v.T, coef)
    high_ref[...], low_ref[...] = split(coef)


def solve(scale, me, inv, proj):
    return call(
        functools.partial(solve_body, scale),
        [SMEM, VMEM, VMEM],
        [VMEM, VMEM],
        [sds((W, W), BF16)] * 2,
        "solve",
    )(me, inv, proj)


def finish_body(me, occ, panel, x_ref, a_ref, xh, xl, out_ref):
    i = pl.program_id(0)
    keep = 1 - me[ROOT]
    ah, al = split(masked(a_ref, panel, i))
    taken = dot(jnp.concatenate([ah, al, ah], 1), jnp.concatenate([xh[...], xh[...], xl[...]], 0))
    for r in range(DEEP):
        for j in range(TJ):
            at = slice(r * TH, (r + 1) * TH), slice(j * TW, (j + 1) * TW)
            out_ref[at] = x_ref[at] * (occ[i * DEEP + r, j] * keep).astype(F32) - taken[at]


def finish(me, occ, panel, x, filed, xh, xl):
    rows = TI * TH
    block = pl.BlockSpec((DEEP * TH, W), lambda i, *_: (i, 0))
    whole = pl.BlockSpec((W, W), lambda i, *_: (0, 0))
    return pl.pallas_call(
        finish_body,
        grid_spec=pltpu.PrefetchScalarGridSpec(
            num_scalar_prefetch=3,
            grid=(TI // DEEP,),
            in_specs=[block, block, whole, whole],
            out_specs=block,
        ),
        out_shape=sds((rows, W), F32),
        compiler_params=params(40),
        cost_estimate=cost(0),
        name="finish",
    )(me, occ, panel, in_hbm(x), in_hbm(filed), xh, xl)


def shards(snapshots, tiles):
    col = lax.axis_index("col")
    _, y, core = site(lax.axis_index("row"))
    root = col == 0
    hop = jnp.where(core == 0, col, (4 - col) % 4)
    scale = math.sqrt(snapshots.shape[0] * lax.axis_size("row"))
    me = jnp.stack([root.astype(jnp.int32), hop, core, y, col]).astype(jnp.int32)
    state = {"x": load(in_hbm(snapshots)), "panel": tiles}
    flags = shifted(tiles, "col")

    def ring(start, stop, filed, beside=None):
        got = [None] * LAG
        steps = stop - start + 3 * LAG
        for s in range(steps):
            last = s >= steps - LAG
            others = flags if start == 0 and s == LAG else []
            filed, send, seen = relay(s, start, stop, last, me, state["panel"], others, state["x"], got[s % LAG], filed)
            if others:
                state["panel"] = seen
            if not last:
                got[s % LAG] = ring_step(send)
            if beside is not None:
                filed = beside(s, filed)
        return filed

    def gram_stage(name, filed):
        if name == "parts":
            keep, give, filed = gram_part(me, tiles, state["x"], filed)
            state["v"] = [keep, lax.ppermute(give, "row", SWAP)]
        elif name == "core":
            own, one, two, three, filed = add_cut(me, state["v"], filed)
            sent = [lax.ppermute(p, "row", SHIFT["y"][d]) for d, p in ((1, one), (2, two), (3, three))]
            state["v"] = [own] + sent
        elif name == "y":
            v, filed = add_parts(state["v"], filed)
            state["v"] = [v] + shifted(v, "z")
        elif name == "z":
            v, filed = add_parts(state["v"], filed)
            state["v"] = [v] + shifted(v, "col")
        elif name == "col":
            v, filed = choose(me, state["v"], filed)
            state["v"] = [v] + shifted(v, "y")
        elif name == "stack":
            v, filed = stack(me, state["v"], filed)
            state["v"] = [v, lax.ppermute(v, "row", SWAP)]
        elif name == "unpack":
            state["s"], state["e"], state["over"], filed = unpack(me, *state["v"], filed)
            state["inv"] = state["s"]
        elif name[0] == "e":
            state["e"], filed = eliminate_block(state["e"], filed)
        else:
            state["s"], state["inv"], state["e"] = spread(int(name[1]), state["e"], state["s"], state["inv"])
        return filed

    plan = {1: ["parts"], 2: ["core"], 4: ["y"], 6: ["z"], 8: ["col"], 9: ["stack"], 10: ["unpack"]}
    plan.update({11: ["e0", "s0"], 12: ["e1"], 13: ["s1", "e2"], 14: ["s2"], 15: ["e3", "s3"]})

    def beside(s, filed):
        for name in plan.get(s, []):
            filed = gram_stage(name, filed)
        return filed

    filed = ring(0, SHORT, None, beside)
    filed = lax.cond(state["over"][0, 0] > 0.5, lambda f: ring(SHORT, CHUNKS, f), lambda f: f, filed)
    panel = state["panel"]
    proj = row_sum(project(me, tiles, panel, snapshots, filed))
    xh, xl = solve(scale, me, state["inv"], proj)
    out = finish(me, tiles, panel, snapshots, filed, xh, xl)
    return state["e"], out


def solution(mesh):
    placed = (P("row", "col"), P("row", "col"))
    return jax.shard_map(shards, mesh=mesh, in_specs=placed, out_specs=(P(), P("row", "col")), check_vma=False)
```

```python
import functools
import math

import jax
import jax.numpy as jnp
from jax import lax
from jax.experimental import pallas as pl
from jax.experimental.pallas import tpu as pltpu
from jax.sharding import PartitionSpec as P

TH = 512
TW = 128
TI = 8
TJ = 4
SLOTS = TI * TJ
PAIR = 2
LAG = 2
CHUNKS = SLOTS // PAIR
SHORT = 12
W = TJ * TW
F32 = jnp.float32
RELAY_COST = 5 * 10**9


def cost(flops):
    return pl.CostEstimate(flops=flops, bytes_accessed=0, transcendentals=0)

BF16 = jnp.bfloat16


def params(limit=16):
    return pltpu.CompilerParams(vmem_limit_bytes=limit * 1024 * 1024)


def sds(shape, dtype):
    return jax.ShapeDtypeStruct(shape, dtype)


def site(r):
    return r // 8, (r // 2) % 4, r % 2


def row_of(z, y, c):
    return (z % 4) * 8 + (y % 4) * 2 + c


def row_perm(f):
    return [(r, row_of(*f(*site(r)))) for r in range(32)]


SWAP = row_perm(lambda z, y, c: (z, y, 1 - c))
SHIFT = {
    "y": [row_perm(lambda z, y, c, d=d: (z, y + d, c)) for d in range(4)],
    "z": [row_perm(lambda z, y, c, d=d: (z + d, y, c)) for d in range(4)],
}
RING = [(r * 4 + x, r * 4 + (x + (1 if r % 2 == 0 else 3)) % 4) for r in range(32) for x in range(4)]


def ring_step(x):
    return lax.ppermute(x, ("row", "col"), RING)


def scatter4(x, axis, me):
    h = x.shape[0] // 4
    total = lax.dynamic_slice_in_dim(x, me * h, h, 0)
    for d in (1, 3, 2):
        part = lax.dynamic_slice_in_dim(x, lax.rem(me + d, 4) * h, h, 0)
        total = total + lax.ppermute(part, "row", SHIFT[axis][d])
    return total


def gather4(x, axis, me):
    h = x.shape[0]
    out = jnp.zeros((4 * h, x.shape[1]), x.dtype)
    for d in range(4):
        got = x if d == 0 else lax.ppermute(x, "row", SHIFT[axis][d])
        out = lax.dynamic_update_slice_in_dim(out, got, lax.rem(me + 4 - d, 4) * h, 0)
    return out


def core_scatter(x, c):
    h = x.shape[0] // 2
    mine = lax.dynamic_slice_in_dim(x, c * h, h, 0)
    other = lax.dynamic_slice_in_dim(x, (1 - c) * h, h, 0)
    return mine + lax.ppermute(other, "row", SWAP)


def core_gather(x, c):
    got = lax.ppermute(x, "row", SWAP)
    first = jnp.where(c == 0, x, got)
    second = jnp.where(c == 0, got, x)
    return jnp.concatenate([first, second], 0)


def row_sum(x):
    _, y, c = site(lax.axis_index("row"))
    v = core_scatter(x, c)
    v = scatter4(v, "y", y)
    one, two, three = shifted(v, "z")
    v = gather4(v + one + two + three, "y", y)
    return core_gather(v, c)


def shifted(x, axis):
    if axis == "col":
        return [lax.ppermute(x, "col", [(i, (i + d) % 4) for i in range(4)]) for d in (1, 2, 3)]
    return [lax.ppermute(x, "row", SHIFT[axis][d]) for d in (1, 2, 3)]


ANY = pl.BlockSpec(memory_space=pl.ANY)
VMEM = pl.BlockSpec(memory_space=pltpu.VMEM)
SMEM = pl.BlockSpec(memory_space=pltpu.SMEM)
ROOT, HOP, CORE, YPOS, COL = range(5)
UPPER = [(i, j) for i in range(TJ) for j in range(i, TJ)]
BLOCKS = len(UPPER) // 2 * TW
HALF = BLOCKS + 32
QUARTER = HALF // 4


def kept(shape):
    return pltpu.VMEM(shape, F32)


FILED = kept((TI * TH, W))


def pin(x):
    return pltpu.with_memory_space_constraint(x, pltpu.VMEM)


def in_hbm(x):
    return pltpu.with_memory_space_constraint(x, pltpu.HBM)


def split(x):
    high = x.astype(BF16)
    return high, (x - high.astype(F32)).astype(BF16)


def dot(a, b):
    return jnp.dot(a, b, preferred_element_type=F32)


def hdot(a, b, dims):
    return lax.dot_general(a, b, (dims, ((), ())), precision=lax.Precision.HIGHEST, preferred_element_type=F32)


def call(body, ins, outs, shapes, name, scratch=(), aliases=None, limit=16, flops=0):
    return pl.pallas_call(
        body,
        in_specs=ins,
        out_specs=outs,
        out_shape=shapes,
        scratch_shapes=list(scratch),
        input_output_aliases=aliases or {},
        compiler_params=params(limit),
        cost_estimate=cost(flops),
        name=name,
    )


def find(full, wanted):
    seen, place, found = jnp.int32(0), jnp.int32(0), jnp.int32(0)
    for t in range(SLOTS):
        hit = jnp.where((full[t] > 0) & (seen == wanted), 1, 0)
        place += hit * t
        found += hit
        seen += full[t]
    return place, found > 0


def relay_body(step, start, stop, fresh, choosing, last, staged, me, own, *refs):
    refs = list(refs)
    root = me[ROOT] > 0
    others = [refs.pop(0) for _ in range(3)] if choosing else []
    x_ref = refs.pop(0)
    got = None if step < LAG else refs.pop(0)
    if not fresh:
        refs.pop(0)
    filed = refs.pop(0)
    send = None if last else refs.pop(0)
    seen = refs.pop(0) if choosing else None
    (sem,) = refs
    full = []
    for t in range(SLOTS):
        at = t % TI, t // TI
        flag = own[at]
        for d, other in enumerate(others, 1):
            flag = jnp.where(me[COL] == d, other[at], flag)
        if seen is not None:
            seen[at] = flag
        full.append(flag)
    chunk = start + step - me[HOP] * LAG
    live = (chunk >= start) & (chunk < stop)

    def each(act, into_send, into_filed):
        for e in range(PAIR):
            place, found = places[e]
            rows = pl.ds(pl.multiple_of((place % TI) * TH, TH), TH)
            cols = pl.ds(pl.multiple_of((place // TI) * TW, TW), TW)
            part = pl.ds(e * TH, TH)

            def move(src, e=e, rows=rows, cols=cols, part=part):
                if into_filed:
                    act(pltpu.make_async_copy(src, filed.at[rows, cols], sem.at[2 * e]))
                if into_send:
                    act(pltpu.make_async_copy(src, send.at[part, :], sem.at[2 * e + 1]))

            @pl.when(found & live & root)
            def _(move=move, rows=rows, cols=cols, part=part):
                move(send.at[part, :] if staged and into_filed else x_ref.at[rows, cols])

            if got is not None:

                @pl.when(found & live & jnp.logical_not(root))
                def _(move=move, part=part):
                    move(got.at[part, :])

    places = [find(full, chunk * PAIR + e) for e in range(PAIR)]
    for into_send, into_filed in ((True, False), (False, True)) if staged else ((send is not None, True),):
        each(lambda c: c.start(), into_send, into_filed)
        each(lambda c: c.wait(), into_send, into_filed)


def relay(step, start, stop, last, me, own, others, x, got, filed):
    staged = start == 0 and step < LAG
    ins, args = [SMEM] * (2 + len(others)) + [ANY], [me, own, *others, in_hbm(x) if staged else pin(x)]
    if step >= LAG:
        ins.append(ANY)
        args.append(got)
    aliases = {}
    if filed is not None:
        aliases = {len(args): 0}
        ins.append(ANY)
        args.append(pin(filed))
    shapes, outs = [FILED], [ANY]
    if not last:
        shapes.append(kept((PAIR * TH, TW)))
        outs.append(ANY)
    if others:
        shapes.append(sds((TI, TJ), jnp.int32))
        outs.append(SMEM)
    out = list(
        call(
            functools.partial(relay_body, step, start, stop, filed is None, bool(others), last, staged),
            ins,
            outs,
            shapes,
            "relay",
            [pltpu.SemaphoreType.DMA((2 * PAIR,))],
            aliases,
            4,
            RELAY_COST,
        )(*args)
    )
    filed = out.pop(0)
    send = None if last else out.pop(0)
    return filed, send, out.pop(0) if others else None


def load_body(x_ref, _, out, sem):
    copies = [
        pltpu.make_async_copy(x_ref.at[pl.ds(i * TH, TH), :], out.at[pl.ds(i * TH, TH), :], sem.at[i]) for i in range(TI)
    ]
    for c in copies:
        c.start()
    for c in copies:
        c.wait()


def load(x, before):
    return call(load_body, [ANY, ANY], ANY, FILED, "load", [pltpu.SemaphoreType.DMA((TI,))])(in_hbm(x), before)


def gram_body(me, occ, x_ref, filed_in, keep, give, filed, gram_ref, cross_ref):
    i = pl.program_id(0)

    @pl.when(i == 0)
    def _():
        gram_ref[...] = jnp.zeros_like(gram_ref)
        cross_ref[...] = jnp.zeros_like(cross_ref)

    @pl.when(me[ROOT] > 0)
    def _():
        x = jnp.concatenate([x_ref[:, j * TW : (j + 1) * TW] * occ[i, j].astype(F32) for j in range(TJ)], 1)
        high, low = split(x)
        h = W // 2
        high_t, low_t = high.T, low.T
        gram_ref[:h, :] += dot(high_t[:h], high) + dot(low_t[:h], low)
        gram_ref[h:, h:] += dot(high_t[h:], high[:, h:]) + dot(low_t[h:], low[:, h:])
        cross_ref[...] += dot(high_t, low)

    @pl.when(i == TI - 1)
    def _():
        full = jnp.int32(0)
        for t in range(SLOTS):
            full += occ[t % TI, t // TI]
        over = jnp.where(full > SHORT * PAIR, 1.0, 0.0)
        keep[BLOCKS:, :] = jnp.full((HALF - BLOCKS, TW), over, F32)
        give[BLOCKS:, :] = jnp.full((HALF - BLOCKS, TW), over, F32)
        for b, (r, q) in enumerate(UPPER):
            rows, cols = slice(r * TW, (r + 1) * TW), slice(q * TW, (q + 1) * TW)
            block = gram_ref[rows, cols] + cross_ref[rows, cols] + cross_ref[cols, rows].T
            part, at = divmod(b * TW, BLOCKS)
            mine = me[CORE] == part

            @pl.when(mine)
            def _(block=block, at=at):
                keep[at : at + TW, :] = block

            @pl.when(jnp.logical_not(mine))
            def _(block=block, at=at):
                give[at : at + TW, :] = block


def gram_part(me, occ, x, filed):
    whole = pl.BlockSpec((HALF, TW), lambda i, *_: (0, 0))
    return pl.pallas_call(
        gram_body,
        grid_spec=pltpu.PrefetchScalarGridSpec(
            num_scalar_prefetch=2,
            grid=(TI,),
            in_specs=[pl.BlockSpec((TH, W), lambda i, me, occ: (i * me[ROOT], 0)), ANY],
            out_specs=[whole, whole, ANY],
            scratch_shapes=[pltpu.VMEM((W, W), F32), pltpu.VMEM((W, W), F32)],
        ),
        out_shape=[sds((HALF, TW), F32), sds((HALF, TW), F32), FILED],
        input_output_aliases={3: 2},
        compiler_params=params(24),
        cost_estimate=cost(0),
        name="gram_part",
    )(me, occ, pin(x), pin(filed))


def add_body(*refs):
    ins, (_, out, _) = refs[:-3], refs[-3:]
    total = ins[0][...]
    for r in ins[1:]:
        total = total + r[...]
    out[...] = total


def add_parts(parts, filed):
    n = len(parts)
    return call(
        add_body,
        [VMEM] * n + [ANY],
        [VMEM, ANY],
        [sds(parts[0].shape, F32), FILED],
        "add_parts",
        aliases={n: 1},
    )(*parts, pin(filed))


def add_cut_body(me, a, b, _, own, one, two, three, __, total):
    total[...] = a[...] + b[...]
    for k, out in enumerate((own, one, two, three)):
        at = lax.rem(me[YPOS] + k, 4) * QUARTER
        out[...] = total[pl.ds(pl.multiple_of(at, 8), QUARTER), :]


def add_cut(me, parts, filed):
    return call(
        add_cut_body,
        [SMEM] + [VMEM] * 2 + [ANY],
        [VMEM] * 4 + [ANY],
        [sds((QUARTER, TW), F32)] * 4 + [FILED],
        "add_cut",
        [pltpu.VMEM((HALF, TW), F32)],
        {3: 4},
    )(me, *parts, pin(filed))


def choose_body(me, a, b, c, d, _, out, __):
    for k, ref in enumerate((a, b, c, d)):

        @pl.when(me[COL] == k)
        def _(ref=ref):
            out[...] = ref[...]


def choose(me, parts, filed):
    return call(
        choose_body,
        [SMEM] + [VMEM] * 4 + [ANY],
        [VMEM, ANY],
        [sds((QUARTER, TW), F32), FILED],
        "choose",
        aliases={5: 1},
    )(me, *parts, pin(filed))


def stack_body(me, a, b, c, d, _, out, __):
    for k, ref in enumerate((a, b, c, d)):
        at = lax.rem(me[YPOS] + 4 - k, 4) * QUARTER
        out[pl.ds(pl.multiple_of(at, 8), QUARTER), :] = ref[...]


def stack(me, parts, filed):
    return call(
        stack_body,
        [SMEM] + [VMEM] * 4 + [ANY],
        [VMEM, ANY],
        [sds((HALF, TW), F32), FILED],
        "stack",
        aliases={5: 1},
    )(me, *parts, pin(filed))


def unpack_body(me, mine, other, _, s_ref, e_ref, over_ref, __):
    over_ref[...] = mine[BLOCKS : BLOCKS + 8, :]
    s_ref[...] = jnp.zeros_like(s_ref)
    for b, (r, q) in enumerate(UPPER):
        part, at = divmod(b * TW, BLOCKS)
        block = jnp.where(me[CORE] == part, mine[at : at + TW, :], other[at : at + TW, :])
        s_ref[r * TW : (r + 1) * TW, q * TW : (q + 1) * TW] = block
        if b == 0:
            e_ref[:, :TW] = block
    e_ref[:, TW:] = unit()


def unpack(me, mine, other, filed):
    return call(
        unpack_body,
        [SMEM, VMEM, VMEM, ANY],
        [VMEM, VMEM, VMEM, ANY],
        [sds((W, W), F32), sds((TW, 2 * TW), F32), sds((8, TW), F32), FILED],
        "unpack",
        aliases={3: 3},
    )(me, mine, other, pin(filed))


def unit():
    r = lax.broadcasted_iota(jnp.int32, (TW, TW), 0)
    c = lax.broadcasted_iota(jnp.int32, (TW, TW), 1)
    return jnp.where(r == c, 1.0, 0.0).astype(F32)


def eliminate(m_rows, v_rows, start, stop):
    groups = len(m_rows)
    full = (8, m_rows[0].shape[1])
    sub = lax.broadcasted_iota(jnp.int32, full, 0)

    def row(x, r):
        return jnp.broadcast_to(x[r : r + 1, :], full)

    for g in range(start, stop):
        lanes = [8 * g + k for k in range(8)]
        columns = [jnp.broadcast_to(m_rows[g][:, lane : lane + 1], full) for lane in lanes]
        a = {(r, k): row(columns[k], r) for k in range(8) for r in range(k, 8)}
        rm = [row(m_rows[g], r) for r in range(8)]
        rv = [row(v_rows[g], r) for r in range(8)]
        inverse = []
        for k in range(8):
            scale = lax.rsqrt(a[k, k])
            inverse.append(scale)
            for r in range(k + 1, 8):
                a[r, k] = a[r, k] * scale
            for c in range(k + 1, 8):
                for r in range(c, 8):
                    a[r, c] = a[r, c] - a[r, k] * a[c, k]
            rm[k] = rm[k] * scale
            rv[k] = rv[k] * scale
            for r in range(k + 1, 8):
                rm[r] = rm[r] - a[r, k] * rm[k]
                rv[r] = rv[r] - a[r, k] * rv[k]
        for i in range(g + 1, groups):
            factor = [jnp.broadcast_to(m_rows[i][:, lane : lane + 1], full) for lane in lanes]
            new_m, new_v = m_rows[i], v_rows[i]
            for k in range(8):
                factor[k] = factor[k] * inverse[k]
                for r in range(k + 1, 8):
                    factor[r] = factor[r] - factor[k] * a[r, k]
                new_m = new_m - factor[k] * rm[k]
                new_v = new_v - factor[k] * rv[k]
            m_rows[i], v_rows[i] = new_m, new_v
        top_m, top_v = rm[0], rv[0]
        for r in range(1, 8):
            top_m = jnp.where(sub == r, rm[r], top_m)
            top_v = jnp.where(sub == r, rv[r], top_v)
        m_rows[g], v_rows[g] = top_m, top_v
    return m_rows, v_rows


def eliminate_body(e_in, _, e_out, __):
    groups = range(TW // 8)
    m_rows = [e_in[8 * g : 8 * g + 8, :TW] for g in groups]
    v_rows = [e_in[8 * g : 8 * g + 8, TW:] for g in groups]
    m_rows, v_rows = eliminate(m_rows, v_rows, 0, TW // 8)
    r = lax.broadcasted_iota(jnp.int32, (8, TW), 0)
    c = lax.broadcasted_iota(jnp.int32, (8, TW), 1)
    for g in groups:
        e_out[8 * g : 8 * g + 8, :TW] = jnp.where(r + 8 * g <= c, m_rows[g], 0.0)
        e_out[8 * g : 8 * g + 8, TW:] = v_rows[g]


def eliminate_block(e, filed):
    return call(
        eliminate_body, [VMEM, ANY], [VMEM, ANY], [sds((TW, 2 * TW), F32), FILED], "eliminate", aliases={1: 1}
    )(e, pin(filed))


def spread_body(b, e_in, s_in, v_in, s_ref, v_ref, e_out):
    lo, hi = b * TW, (b + 1) * TW
    s_ref[...] = s_in[...]
    if b == 0:
        v_ref[...] = jnp.zeros_like(v_ref)
    else:
        v_ref[...] = v_in[...]
    inv = e_in[:, TW:]
    s_ref[lo:hi, lo:hi] = e_in[:, :TW]
    v_ref[lo:hi, lo:hi] = inv
    if b > 0:
        v_ref[lo:hi, :lo] = hdot(inv, v_in[lo:hi, :lo], ((1,), (0,)))
    if hi < W:
        right = hdot(inv, s_in[lo:hi, hi:], ((1,), (0,)))
        s_ref[lo:hi, hi:] = right
        s_ref[hi:, hi:] -= hdot(right, right, ((0,), (0,)))
        s_ref[hi:, lo:hi] = jnp.zeros((W - hi, TW), F32)
        v_ref[hi:, :hi] -= hdot(right, v_ref[lo:hi, :hi], ((0,), (0,)))
        e_out[:, :TW] = s_ref[hi : hi + TW, hi : hi + TW]
        e_out[:, TW:] = unit()
    else:
        e_out[0] = s_ref[: W // 2, : W // 2]
        e_out[1] = s_ref[W // 2 :, W // 2 :]


def spread(b, e, s, v):
    return call(
        functools.partial(spread_body, b),
        [VMEM] * 3,
        [VMEM] * 3,
        [sds((W, W), F32), sds((W, W), F32), sds((TW, 2 * TW) if b < TJ - 1 else (2, W // 2, W // 2), F32)],
        "spread",
    )(e, s, v)


def masked(ref, flags, i, r):
    parts = []
    for j in range(TJ):
        block = ref[r * TH : (r + 1) * TH, j * TW : (j + 1) * TW]
        parts.append(jnp.where(flags[i * DEEP + r, j] > 0, block, jnp.zeros_like(block)))
    return jnp.concatenate(parts, 1)


def occupied(flags, row):
    count, starts = jnp.int32(0), [jnp.int32(0)] * TJ
    for j in range(TJ):
        for q in range(j + 1):
            starts[q] += jnp.where((flags[row, j] > 0) & (count == q), j * TW, 0)
        count += jnp.where(flags[row, j] > 0, 1, 0)
    return count, [pl.ds(pl.multiple_of(v, TW), TW) for v in starts]


DEEP = 2


def project_body(me, occ, panel, x_ref, a_ref, c_ref):
    i = pl.program_id(0)

    @pl.when(i == 0)
    def _():
        c_ref[...] = jnp.zeros_like(c_ref)

    for r in range(DEEP):
        count, at = occupied(panel, i * DEEP + r)
        for k in range(1, TJ + 1):

            @pl.when((me[ROOT] == 0) & (count == k))
            def _(r=r, at=at[:k]):
                ah, al = split(jnp.concatenate([a_ref[r * TH : (r + 1) * TH, v] for v in at], 1))
                bh, bl = split(masked(x_ref, occ, i, r))
                ah_t, al_t = ah.T, al.T
                part = dot(jnp.concatenate([ah_t, al_t, ah_t], 1), jnp.concatenate([bh, bh, bl], 0))
                for q, v in enumerate(at):
                    c_ref[v, :] += part[q * TW : (q + 1) * TW]


def project(me, occ, panel, x, filed):
    block = pl.BlockSpec((DEEP * TH, W), lambda i, *_: (i, 0))
    return pl.pallas_call(
        project_body,
        grid_spec=pltpu.PrefetchScalarGridSpec(
            num_scalar_prefetch=3,
            grid=(TI // DEEP,),
            in_specs=[block, block],
            out_specs=pl.BlockSpec((W, W), lambda i, *_: (0, 0)),
        ),
        out_shape=sds((W, W), F32),
        compiler_params=params(40),
        cost_estimate=cost(0),
        name="project",
    )(me, occ, panel, in_hbm(x), in_hbm(filed))


def solve_body(scale, me, v_ref, c_ref, high_ref, low_ref):
    v = v_ref[...]
    coef = hdot(v, hdot(v, c_ref[...], ((1,), (0,))), ((0,), (0,)))
    coef = jnp.where(me[ROOT] > 0, -scale * v.T, coef)
    high_ref[...], low_ref[...] = split(coef)


def solve(scale, me, inv, proj):
    return call(
        functools.partial(solve_body, scale),
        [SMEM, VMEM, VMEM],
        [VMEM, VMEM],
        [sds((W, W), BF16)] * 2,
        "solve",
    )(me, inv, proj)


def finish_body(me, occ, panel, x_ref, a_ref, xh, xl, out_ref):
    i = pl.program_id(0)
    keep = 1 - me[ROOT]
    for r in range(DEEP):
        rows = slice(r * TH, (r + 1) * TH)
        count, at = occupied(panel, i * DEEP + r)
        for k in range(TJ + 1):

            @pl.when(count == k)
            def _(r=r, rows=rows, at=at[:k]):
                if at:
                    ah, al = split(jnp.concatenate([a_ref[rows, v] for v in at], 1))
                    high, low = [xh[v, :] for v in at], [xl[v, :] for v in at]
                    taken = dot(jnp.concatenate([ah, al, ah], 1), jnp.concatenate(high + high + low, 0))
                else:
                    taken = jnp.zeros((TH, W), F32)
                for j in range(TJ):
                    cols = slice(j * TW, (j + 1) * TW)
                    keep_tile = (occ[i * DEEP + r, j] * keep).astype(F32)
                    out_ref[rows, cols] = x_ref[rows, cols] * keep_tile - taken[:, cols]


def finish(me, occ, panel, x, filed, xh, xl):
    rows = TI * TH
    block = pl.BlockSpec((DEEP * TH, W), lambda i, *_: (i, 0))
    whole = pl.BlockSpec((W, W), lambda i, *_: (0, 0))
    return pl.pallas_call(
        finish_body,
        grid_spec=pltpu.PrefetchScalarGridSpec(
            num_scalar_prefetch=3,
            grid=(TI // DEEP,),
            in_specs=[block, block, whole, whole],
            out_specs=block,
        ),
        out_shape=sds((rows, W), F32),
        compiler_params=params(40),
        cost_estimate=cost(0),
        name="finish",
    )(me, occ, panel, in_hbm(x), in_hbm(filed), xh, xl)


def shards(snapshots, tiles):
    col = lax.axis_index("col")
    _, y, core = site(lax.axis_index("row"))
    root = col == 0
    hop = jnp.where(core == 0, col, (4 - col) % 4)
    scale = math.sqrt(snapshots.shape[0] * lax.axis_size("row"))
    me = jnp.stack([root.astype(jnp.int32), hop, core, y, col]).astype(jnp.int32)
    state = {"x": snapshots, "panel": tiles}
    flags = shifted(tiles, "col")

    def ring(start, stop, filed, beside=None):
        got = [None] * LAG
        steps = stop - start + 3 * LAG
        for s in range(steps):
            last = s >= steps - LAG
            others = flags if start == 0 and s == LAG else []
            filed, send, seen = relay(s, start, stop, last, me, state["panel"], others, state["x"], got[s % LAG], filed)
            if others:
                state["panel"] = seen
            if not last:
                got[s % LAG] = ring_step(send)
            if beside is not None:
                filed = beside(s, filed)
        return filed

    def gram_stage(name, filed):
        if name == "parts":
            state["x"] = load(snapshots, filed)
            keep, give, filed = gram_part(me, tiles, state["x"], filed)
            state["v"] = [keep, lax.ppermute(give, "row", SWAP)]
        elif name == "core":
            own, one, two, three, filed = add_cut(me, state["v"], filed)
            sent = [lax.ppermute(p, "row", SHIFT["y"][d]) for d, p in ((1, one), (2, two), (3, three))]
            state["v"] = [own] + sent
        elif name == "y":
            v, filed = add_parts(state["v"], filed)
            state["v"] = [v] + shifted(v, "z")
        elif name == "z":
            v, filed = add_parts(state["v"], filed)
            state["v"] = [v] + shifted(v, "col")
        elif name == "col":
            v, filed = choose(me, state["v"], filed)
            state["v"] = [v] + shifted(v, "y")
        elif name == "stack":
            v, filed = stack(me, state["v"], filed)
            state["v"] = [v, lax.ppermute(v, "row", SWAP)]
        elif name == "unpack":
            state["s"], state["e"], state["over"], filed = unpack(me, *state["v"], filed)
            state["inv"] = state["s"]
        elif name[0] == "e":
            state["e"], filed = eliminate_block(state["e"], filed)
        else:
            state["s"], state["inv"], state["e"] = spread(int(name[1]), state["e"], state["s"], state["inv"])
        return filed

    plan = {1: ["parts"], 2: ["core"], 4: ["y"], 6: ["z"], 8: ["col"], 9: ["stack"], 10: ["unpack"]}
    plan.update({11: ["e0", "s0"], 12: ["e1"], 13: ["s1", "e2"], 14: ["s2"], 15: ["e3", "s3"]})

    def beside(s, filed):
        for name in plan.get(s, []):
            filed = gram_stage(name, filed)
        return filed

    filed = ring(0, SHORT, None, beside)
    filed = lax.cond(state["over"][0, 0] > 0.5, lambda f: ring(SHORT, CHUNKS, f), lambda f: f, filed)
    panel = state["panel"]
    proj = row_sum(project(me, tiles, panel, snapshots, filed))
    xh, xl = solve(scale, me, state["inv"], proj)
    out = finish(me, tiles, panel, snapshots, filed, xh, xl)
    return state["e"], out


def solution(mesh):
    placed = (P("row", "col"), P("row", "col"))
    return jax.shard_map(shards, mesh=mesh, in_specs=placed, out_specs=(P(), P("row", "col")), check_vma=False)
```

```python
import functools
import math

import jax
import jax.numpy as jnp
from jax import lax
from jax.experimental import pallas as pl
from jax.experimental.pallas import tpu as pltpu
from jax.sharding import PartitionSpec as P

TH = 512
TW = 128
TI = 8
TJ = 4
SLOTS = TI * TJ
PAIR = 2
LAG = 2
CHUNKS = SLOTS // PAIR
SHORT = 12
W = TJ * TW
F32 = jnp.float32
RELAY_COST = 5 * 10**9


def cost(flops):
    return pl.CostEstimate(flops=flops, bytes_accessed=0, transcendentals=0)

BF16 = jnp.bfloat16


def params(limit=16):
    return pltpu.CompilerParams(vmem_limit_bytes=limit * 1024 * 1024)


def sds(shape, dtype):
    return jax.ShapeDtypeStruct(shape, dtype)


def site(r):
    return r // 8, (r // 2) % 4, r % 2


def row_of(z, y, c):
    return (z % 4) * 8 + (y % 4) * 2 + c


def row_perm(f):
    return [(r, row_of(*f(*site(r)))) for r in range(32)]


SWAP = row_perm(lambda z, y, c: (z, y, 1 - c))
SHIFT = {
    "y": [row_perm(lambda z, y, c, d=d: (z, y + d, c)) for d in range(4)],
    "z": [row_perm(lambda z, y, c, d=d: (z + d, y, c)) for d in range(4)],
}
RING = [(r * 4 + x, r * 4 + (x + (1 if r % 2 == 0 else 3)) % 4) for r in range(32) for x in range(4)]


def ring_step(x):
    return lax.ppermute(x, ("row", "col"), RING)


def scatter4(x, axis, me):
    h = x.shape[0] // 4
    total = lax.dynamic_slice_in_dim(x, me * h, h, 0)
    for d in (1, 3, 2):
        part = lax.dynamic_slice_in_dim(x, lax.rem(me + d, 4) * h, h, 0)
        total = total + lax.ppermute(part, "row", SHIFT[axis][d])
    return total


def gather4(x, axis, me):
    h = x.shape[0]
    out = jnp.zeros((4 * h, x.shape[1]), x.dtype)
    for d in range(4):
        got = x if d == 0 else lax.ppermute(x, "row", SHIFT[axis][d])
        out = lax.dynamic_update_slice_in_dim(out, got, lax.rem(me + 4 - d, 4) * h, 0)
    return out


def core_scatter(x, c):
    h = x.shape[0] // 2
    mine = lax.dynamic_slice_in_dim(x, c * h, h, 0)
    other = lax.dynamic_slice_in_dim(x, (1 - c) * h, h, 0)
    return mine + lax.ppermute(other, "row", SWAP)


def core_gather(x, c):
    got = lax.ppermute(x, "row", SWAP)
    first = jnp.where(c == 0, x, got)
    second = jnp.where(c == 0, got, x)
    return jnp.concatenate([first, second], 0)


def row_sum(x, beside):
    _, y, c = site(lax.axis_index("row"))
    v = core_scatter(x, c)
    v = scatter4(v, "y", y)
    v = add_beside([v] + shifted(v, "z"), beside)
    return core_gather(gather4(v, "y", y), c)


def shifted(x, axis):
    if axis == "col":
        return [lax.ppermute(x, "col", [(i, (i + d) % 4) for i in range(4)]) for d in (1, 2, 3)]
    return [lax.ppermute(x, "row", SHIFT[axis][d]) for d in (1, 2, 3)]


ANY = pl.BlockSpec(memory_space=pl.ANY)
VMEM = pl.BlockSpec(memory_space=pltpu.VMEM)
SMEM = pl.BlockSpec(memory_space=pltpu.SMEM)
ROOT, HOP, CORE, YPOS, COL = range(5)
UPPER = [(i, j) for i in range(TJ) for j in range(i, TJ)]
BLOCKS = len(UPPER) // 2 * TW
HALF = BLOCKS + 32
QUARTER = HALF // 4


def kept(shape):
    return pltpu.VMEM(shape, F32)


FILED = kept((TI * TH, W))


def pin(x):
    return pltpu.with_memory_space_constraint(x, pltpu.VMEM)


def in_hbm(x):
    return pltpu.with_memory_space_constraint(x, pltpu.HBM)


def split(x):
    high = x.astype(BF16)
    return high, (x - high.astype(F32)).astype(BF16)


def dot(a, b):
    return jnp.dot(a, b, preferred_element_type=F32)


def hdot(a, b, dims):
    return lax.dot_general(a, b, (dims, ((), ())), precision=lax.Precision.HIGHEST, preferred_element_type=F32)


def call(body, ins, outs, shapes, name, scratch=(), aliases=None, limit=16, flops=0):
    return pl.pallas_call(
        body,
        in_specs=ins,
        out_specs=outs,
        out_shape=shapes,
        scratch_shapes=list(scratch),
        input_output_aliases=aliases or {},
        compiler_params=params(limit),
        cost_estimate=cost(flops),
        name=name,
    )


def find(full, wanted):
    seen, place, found = jnp.int32(0), jnp.int32(0), jnp.int32(0)
    for t in range(SLOTS):
        hit = jnp.where((full[t] > 0) & (seen == wanted), 1, 0)
        place += hit * t
        found += hit
        seen += full[t]
    return place, found > 0


def relay_body(step, start, stop, fresh, choosing, last, staged, me, own, *refs):
    refs = list(refs)
    root = me[ROOT] > 0
    others = [refs.pop(0) for _ in range(3)] if choosing else []
    x_ref = refs.pop(0)
    got = None if step < LAG else refs.pop(0)
    if not fresh:
        refs.pop(0)
    filed = refs.pop(0)
    send = None if last else refs.pop(0)
    seen = refs.pop(0) if choosing else None
    (sem,) = refs
    full = []
    for t in range(SLOTS):
        at = t % TI, t // TI
        flag = own[at]
        for d, other in enumerate(others, 1):
            flag = jnp.where(me[COL] == d, other[at], flag)
        if seen is not None:
            seen[at] = flag
        full.append(flag)
    chunk = start + step - me[HOP] * LAG
    live = (chunk >= start) & (chunk < stop)

    def each(act, into_send, into_filed):
        for e in range(PAIR):
            place, found = places[e]
            rows = pl.ds(pl.multiple_of((place % TI) * TH, TH), TH)
            cols = pl.ds(pl.multiple_of((place // TI) * TW, TW), TW)
            part = pl.ds(e * TH, TH)

            def move(src, e=e, rows=rows, cols=cols, part=part):
                if into_filed:
                    act(pltpu.make_async_copy(src, filed.at[rows, cols], sem.at[2 * e]))
                if into_send:
                    act(pltpu.make_async_copy(src, send.at[part, :], sem.at[2 * e + 1]))

            @pl.when(found & live & root)
            def _(move=move, rows=rows, cols=cols, part=part):
                move(send.at[part, :] if staged and into_filed else x_ref.at[rows, cols])

            if got is not None:

                @pl.when(found & live & jnp.logical_not(root))
                def _(move=move, part=part):
                    move(got.at[part, :])

    places = [find(full, chunk * PAIR + e) for e in range(PAIR)]
    for into_send, into_filed in ((True, False), (False, True)) if staged else ((send is not None, True),):
        each(lambda c: c.start(), into_send, into_filed)
        each(lambda c: c.wait(), into_send, into_filed)


def relay(step, start, stop, last, me, own, others, x, got, filed):
    staged = start == 0 and step < LAG
    ins, args = [SMEM] * (2 + len(others)) + [ANY], [me, own, *others, in_hbm(x) if staged else pin(x)]
    if step >= LAG:
        ins.append(ANY)
        args.append(got)
    aliases = {}
    if filed is not None:
        aliases = {len(args): 0}
        ins.append(ANY)
        args.append(pin(filed))
    shapes, outs = [FILED], [ANY]
    if not last:
        shapes.append(kept((PAIR * TH, TW)))
        outs.append(ANY)
    if others:
        shapes.append(sds((TI, TJ), jnp.int32))
        outs.append(SMEM)
    out = list(
        call(
            functools.partial(relay_body, step, start, stop, filed is None, bool(others), last, staged),
            ins,
            outs,
            shapes,
            "relay",
            [pltpu.SemaphoreType.DMA((2 * PAIR,))],
            aliases,
            4,
            RELAY_COST,
        )(*args)
    )
    filed = out.pop(0)
    send = None if last else out.pop(0)
    return filed, send, out.pop(0) if others else None


def load_body(x_ref, _, out, sem):
    copies = [
        pltpu.make_async_copy(x_ref.at[pl.ds(i * TH, TH), :], out.at[pl.ds(i * TH, TH), :], sem.at[i]) for i in range(TI)
    ]
    for c in copies:
        c.start()
    for c in copies:
        c.wait()


def load(x, before):
    return call(load_body, [ANY, ANY], ANY, FILED, "load", [pltpu.SemaphoreType.DMA((TI,))])(in_hbm(x), before)


def gram_body(me, occ, x_ref, filed_in, keep, give, filed, gram_ref, cross_ref):
    i = pl.program_id(0)

    @pl.when(i == 0)
    def _():
        gram_ref[...] = jnp.zeros_like(gram_ref)
        cross_ref[...] = jnp.zeros_like(cross_ref)

    @pl.when(me[ROOT] > 0)
    def _():
        x = jnp.concatenate([x_ref[:, j * TW : (j + 1) * TW] * occ[i, j].astype(F32) for j in range(TJ)], 1)
        high, low = split(x)
        h = W // 2
        high_t, low_t = high.T, low.T
        gram_ref[:h, :] += dot(high_t[:h], high) + dot(low_t[:h], low)
        gram_ref[h:, h:] += dot(high_t[h:], high[:, h:]) + dot(low_t[h:], low[:, h:])
        cross_ref[...] += dot(high_t, low)

    @pl.when(i == TI - 1)
    def _():
        full = jnp.int32(0)
        for t in range(SLOTS):
            full += occ[t % TI, t // TI]
        over = jnp.where(full > SHORT * PAIR, 1.0, 0.0)
        keep[BLOCKS:, :] = jnp.full((HALF - BLOCKS, TW), over, F32)
        give[BLOCKS:, :] = jnp.full((HALF - BLOCKS, TW), over, F32)
        for b, (r, q) in enumerate(UPPER):
            rows, cols = slice(r * TW, (r + 1) * TW), slice(q * TW, (q + 1) * TW)
            block = gram_ref[rows, cols] + cross_ref[rows, cols] + cross_ref[cols, rows].T
            part, at = divmod(b * TW, BLOCKS)
            mine = me[CORE] == part

            @pl.when(mine)
            def _(block=block, at=at):
                keep[at : at + TW, :] = block

            @pl.when(jnp.logical_not(mine))
            def _(block=block, at=at):
                give[at : at + TW, :] = block


def gram_part(me, occ, x, filed):
    whole = pl.BlockSpec((HALF, TW), lambda i, *_: (0, 0))
    return pl.pallas_call(
        gram_body,
        grid_spec=pltpu.PrefetchScalarGridSpec(
            num_scalar_prefetch=2,
            grid=(TI,),
            in_specs=[pl.BlockSpec((TH, W), lambda i, me, occ: (i * me[ROOT], 0)), ANY],
            out_specs=[whole, whole, ANY],
            scratch_shapes=[pltpu.VMEM((W, W), F32), pltpu.VMEM((W, W), F32)],
        ),
        out_shape=[sds((HALF, TW), F32), sds((HALF, TW), F32), FILED],
        input_output_aliases={3: 2},
        compiler_params=params(24),
        cost_estimate=cost(0),
        name="gram_part",
    )(me, occ, pin(x), pin(filed))


def add_body(*refs):
    ins, (_, out, _) = refs[:-3], refs[-3:]
    total = ins[0][...]
    for r in ins[1:]:
        total = total + r[...]
    out[...] = total


def add_parts(parts, filed):
    n = len(parts)
    return call(
        add_body,
        [VMEM] * n + [ANY],
        [VMEM, ANY],
        [sds(parts[0].shape, F32), FILED],
        "add_parts",
        aliases={n: 1},
    )(*parts, pin(filed))


def add_beside_body(*refs):
    add_body(*refs[:-2], None, refs[-1], None)


def add_beside(parts, beside):
    return call(add_beside_body, [VMEM] * len(parts) + [ANY], VMEM, sds(parts[0].shape, F32), "add_beside")(*parts, beside)


def add_cut_body(me, a, b, _, own, one, two, three, __, total):
    total[...] = a[...] + b[...]
    for k, out in enumerate((own, one, two, three)):
        at = lax.rem(me[YPOS] + k, 4) * QUARTER
        out[...] = total[pl.ds(pl.multiple_of(at, 8), QUARTER), :]


def add_cut(me, parts, filed):
    return call(
        add_cut_body,
        [SMEM] + [VMEM] * 2 + [ANY],
        [VMEM] * 4 + [ANY],
        [sds((QUARTER, TW), F32)] * 4 + [FILED],
        "add_cut",
        [pltpu.VMEM((HALF, TW), F32)],
        {3: 4},
    )(me, *parts, pin(filed))


def choose_body(me, a, b, c, d, _, out, __):
    for k, ref in enumerate((a, b, c, d)):

        @pl.when(me[COL] == k)
        def _(ref=ref):
            out[...] = ref[...]


def choose(me, parts, filed):
    return call(
        choose_body,
        [SMEM] + [VMEM] * 4 + [ANY],
        [VMEM, ANY],
        [sds((QUARTER, TW), F32), FILED],
        "choose",
        aliases={5: 1},
    )(me, *parts, pin(filed))


def stack_body(me, a, b, c, d, _, out, __):
    for k, ref in enumerate((a, b, c, d)):
        at = lax.rem(me[YPOS] + 4 - k, 4) * QUARTER
        out[pl.ds(pl.multiple_of(at, 8), QUARTER), :] = ref[...]


def stack(me, parts, filed):
    return call(
        stack_body,
        [SMEM] + [VMEM] * 4 + [ANY],
        [VMEM, ANY],
        [sds((HALF, TW), F32), FILED],
        "stack",
        aliases={5: 1},
    )(me, *parts, pin(filed))


def unpack_body(me, mine, other, _, s_ref, e_ref, over_ref, __):
    over_ref[...] = mine[BLOCKS : BLOCKS + 8, :]
    s_ref[...] = jnp.zeros_like(s_ref)
    for b, (r, q) in enumerate(UPPER):
        part, at = divmod(b * TW, BLOCKS)
        block = jnp.where(me[CORE] == part, mine[at : at + TW, :], other[at : at + TW, :])
        s_ref[r * TW : (r + 1) * TW, q * TW : (q + 1) * TW] = block
        if b == 0:
            e_ref[:, :TW] = block
    e_ref[:, TW:] = unit()


def unpack(me, mine, other, filed):
    return call(
        unpack_body,
        [SMEM, VMEM, VMEM, ANY],
        [VMEM, VMEM, VMEM, ANY],
        [sds((W, W), F32), sds((TW, 2 * TW), F32), sds((8, TW), F32), FILED],
        "unpack",
        aliases={3: 3},
    )(me, mine, other, pin(filed))


def unit():
    r = lax.broadcasted_iota(jnp.int32, (TW, TW), 0)
    c = lax.broadcasted_iota(jnp.int32, (TW, TW), 1)
    return jnp.where(r == c, 1.0, 0.0).astype(F32)


def eliminate(m_rows, v_rows, start, stop):
    groups = len(m_rows)
    full = (8, m_rows[0].shape[1])
    sub = lax.broadcasted_iota(jnp.int32, full, 0)

    def row(x, r):
        return jnp.broadcast_to(x[r : r + 1, :], full)

    for g in range(start, stop):
        lanes = [8 * g + k for k in range(8)]
        columns = [jnp.broadcast_to(m_rows[g][:, lane : lane + 1], full) for lane in lanes]
        a = {(r, k): row(columns[k], r) for k in range(8) for r in range(k, 8)}
        rm = [row(m_rows[g], r) for r in range(8)]
        rv = [row(v_rows[g], r) for r in range(8)]
        inverse = []
        for k in range(8):
            scale = lax.rsqrt(a[k, k])
            inverse.append(scale)
            for r in range(k + 1, 8):
                a[r, k] = a[r, k] * scale
            for c in range(k + 1, 8):
                for r in range(c, 8):
                    a[r, c] = a[r, c] - a[r, k] * a[c, k]
            rm[k] = rm[k] * scale
            rv[k] = rv[k] * scale
            for r in range(k + 1, 8):
                rm[r] = rm[r] - a[r, k] * rm[k]
                rv[r] = rv[r] - a[r, k] * rv[k]
        for i in range(g + 1, groups):
            factor = [jnp.broadcast_to(m_rows[i][:, lane : lane + 1], full) for lane in lanes]
            new_m, new_v = m_rows[i], v_rows[i]
            for k in range(8):
                factor[k] = factor[k] * inverse[k]
                for r in range(k + 1, 8):
                    factor[r] = factor[r] - factor[k] * a[r, k]
                new_m = new_m - factor[k] * rm[k]
                new_v = new_v - factor[k] * rv[k]
            m_rows[i], v_rows[i] = new_m, new_v
        top_m, top_v = rm[0], rv[0]
        for r in range(1, 8):
            top_m = jnp.where(sub == r, rm[r], top_m)
            top_v = jnp.where(sub == r, rv[r], top_v)
        m_rows[g], v_rows[g] = top_m, top_v
    return m_rows, v_rows


def eliminate_body(e_in, _, e_out, __):
    groups = range(TW // 8)
    m_rows = [e_in[8 * g : 8 * g + 8, :TW] for g in groups]
    v_rows = [e_in[8 * g : 8 * g + 8, TW:] for g in groups]
    m_rows, v_rows = eliminate(m_rows, v_rows, 0, TW // 8)
    r = lax.broadcasted_iota(jnp.int32, (8, TW), 0)
    c = lax.broadcasted_iota(jnp.int32, (8, TW), 1)
    for g in groups:
        e_out[8 * g : 8 * g + 8, :TW] = jnp.where(r + 8 * g <= c, m_rows[g], 0.0)
        e_out[8 * g : 8 * g + 8, TW:] = v_rows[g]


def eliminate_block(e, filed):
    return call(
        eliminate_body, [VMEM, ANY], [VMEM, ANY], [sds((TW, 2 * TW), F32), FILED], "eliminate", aliases={1: 1}
    )(e, pin(filed))


def eliminate_last(e, before):
    body = lambda e_in, _, e_out: eliminate_body(e_in, None, e_out, None)
    return call(body, [VMEM, ANY], VMEM, sds((TW, 2 * TW), F32), "eliminate", flops=RELAY_COST)(e, before)


def spread_body(b, e_in, s_in, v_in, s_ref, v_ref, e_out):
    lo, hi = b * TW, (b + 1) * TW
    s_ref[...] = s_in[...]
    if b == 0:
        v_ref[...] = jnp.zeros_like(v_ref)
    else:
        v_ref[...] = v_in[...]
    inv = e_in[:, TW:]
    s_ref[lo:hi, lo:hi] = e_in[:, :TW]
    v_ref[lo:hi, lo:hi] = inv
    if b > 0:
        v_ref[lo:hi, :lo] = hdot(inv, v_in[lo:hi, :lo], ((1,), (0,)))
    if hi < W:
        right = hdot(inv, s_in[lo:hi, hi:], ((1,), (0,)))
        s_ref[lo:hi, hi:] = right
        s_ref[hi:, hi:] -= hdot(right, right, ((0,), (0,)))
        s_ref[hi:, lo:hi] = jnp.zeros((W - hi, TW), F32)
        v_ref[hi:, :hi] -= hdot(right, v_ref[lo:hi, :hi], ((0,), (0,)))
        e_out[:, :TW] = s_ref[hi : hi + TW, hi : hi + TW]
        e_out[:, TW:] = unit()
    else:
        e_out[0] = s_ref[: W // 2, : W // 2]
        e_out[1] = s_ref[W // 2 :, W // 2 :]


def spread(b, e, s, v):
    return call(
        functools.partial(spread_body, b),
        [VMEM] * 3,
        [VMEM] * 3,
        [sds((W, W), F32), sds((W, W), F32), sds((TW, 2 * TW) if b < TJ - 1 else (2, W // 2, W // 2), F32)],
        "spread",
    )(e, s, v)


def masked(ref, flags, i, r):
    parts = []
    for j in range(TJ):
        block = ref[r * TH : (r + 1) * TH, j * TW : (j + 1) * TW]
        parts.append(jnp.where(flags[i * DEEP + r, j] > 0, block, jnp.zeros_like(block)))
    return jnp.concatenate(parts, 1)


def occupied(flags, row):
    count, starts = jnp.int32(0), [jnp.int32(0)] * TJ
    for j in range(TJ):
        for q in range(j + 1):
            starts[q] += jnp.where((flags[row, j] > 0) & (count == q), j * TW, 0)
        count += jnp.where(flags[row, j] > 0, 1, 0)
    return count, [pl.ds(pl.multiple_of(v, TW), TW) for v in starts]


DEEP = 2


def project_body(me, occ, panel, x_ref, a_ref, c_ref):
    i = pl.program_id(0)

    @pl.when(i == 0)
    def _():
        c_ref[...] = jnp.zeros_like(c_ref)

    for r in range(DEEP):
        count, at = occupied(panel, i * DEEP + r)
        for k in range(1, TJ + 1):

            @pl.when((me[ROOT] == 0) & (count == k))
            def _(r=r, at=at[:k]):
                ah, al = split(jnp.concatenate([a_ref[r * TH : (r + 1) * TH, v] for v in at], 1))
                bh, bl = split(masked(x_ref, occ, i, r))
                ah_t, al_t = ah.T, al.T
                part = dot(jnp.concatenate([ah_t, al_t, ah_t], 1), jnp.concatenate([bh, bh, bl], 0))
                for q, v in enumerate(at):
                    c_ref[v, :] += part[q * TW : (q + 1) * TW]


def project(me, occ, panel, x, filed):
    block = pl.BlockSpec((DEEP * TH, W), lambda i, *_: (i, 0))
    return pl.pallas_call(
        project_body,
        grid_spec=pltpu.PrefetchScalarGridSpec(
            num_scalar_prefetch=3,
            grid=(TI // DEEP,),
            in_specs=[block, block],
            out_specs=pl.BlockSpec((W, W), lambda i, *_: (0, 0)),
        ),
        out_shape=sds((W, W), F32),
        compiler_params=params(40),
        cost_estimate=cost(0),
        name="project",
    )(me, occ, panel, in_hbm(x), in_hbm(filed))


def solve_body(scale, me, v_ref, c_ref, high_ref, low_ref):
    v = v_ref[...]
    coef = hdot(v, hdot(v, c_ref[...], ((1,), (0,))), ((0,), (0,)))
    coef = jnp.where(me[ROOT] > 0, -scale * v.T, coef)
    high_ref[...], low_ref[...] = split(coef)


def solve(scale, me, inv, proj):
    return call(
        functools.partial(solve_body, scale),
        [SMEM, VMEM, VMEM],
        [VMEM, VMEM],
        [sds((W, W), BF16)] * 2,
        "solve",
    )(me, inv, proj)


def finish_body(me, occ, panel, x_ref, a_ref, xh, xl, out_ref):
    i = pl.program_id(0)
    keep = 1 - me[ROOT]
    for r in range(DEEP):
        rows = slice(r * TH, (r + 1) * TH)
        count, at = occupied(panel, i * DEEP + r)
        for k in range(TJ + 1):

            @pl.when(count == k)
            def _(r=r, rows=rows, at=at[:k]):
                if at:
                    ah, al = split(jnp.concatenate([a_ref[rows, v] for v in at], 1))
                    high, low = [xh[v, :] for v in at], [xl[v, :] for v in at]
                    taken = dot(jnp.concatenate([ah, al, ah], 1), jnp.concatenate(high + high + low, 0))
                else:
                    taken = jnp.zeros((TH, W), F32)
                for j in range(TJ):
                    cols = slice(j * TW, (j + 1) * TW)
                    keep_tile = (occ[i * DEEP + r, j] * keep).astype(F32)
                    out_ref[rows, cols] = x_ref[rows, cols] * keep_tile - taken[:, cols]


def finish(me, occ, panel, x, filed, xh, xl):
    rows = TI * TH
    block = pl.BlockSpec((DEEP * TH, W), lambda i, *_: (i, 0))
    whole = pl.BlockSpec((W, W), lambda i, *_: (0, 0))
    return pl.pallas_call(
        finish_body,
        grid_spec=pltpu.PrefetchScalarGridSpec(
            num_scalar_prefetch=3,
            grid=(TI // DEEP,),
            in_specs=[block, block, whole, whole],
            out_specs=block,
        ),
        out_shape=sds((rows, W), F32),
        compiler_params=params(40),
        cost_estimate=cost(0),
        name="finish",
    )(me, occ, panel, in_hbm(x), in_hbm(filed), xh, xl)


def shards(snapshots, tiles):
    col = lax.axis_index("col")
    _, y, core = site(lax.axis_index("row"))
    root = col == 0
    hop = jnp.where(core == 0, col, (4 - col) % 4)
    scale = math.sqrt(snapshots.shape[0] * lax.axis_size("row"))
    me = jnp.stack([root.astype(jnp.int32), hop, core, y, col]).astype(jnp.int32)
    state = {"x": snapshots, "panel": tiles}
    flags = shifted(tiles, "col")

    def ring(start, stop, filed, beside=None):
        got = [None] * LAG
        steps = stop - start + 3 * LAG
        for s in range(steps):
            last = s >= steps - LAG
            others = flags if start == 0 and s == LAG else []
            filed, send, seen = relay(s, start, stop, last, me, state["panel"], others, state["x"], got[s % LAG], filed)
            if others:
                state["panel"] = seen
            if not last:
                got[s % LAG] = ring_step(send)
            if beside is not None:
                filed = beside(s, filed)
        return filed

    def gram_stage(name, filed):
        if name == "load":
            state["x"] = load(snapshots, filed)
        elif name == "parts":
            keep, give, filed = gram_part(me, tiles, state["x"], filed)
            state["v"] = [keep, lax.ppermute(give, "row", SWAP)]
        elif name == "core":
            own, one, two, three, filed = add_cut(me, state["v"], filed)
            sent = [lax.ppermute(p, "row", SHIFT["y"][d]) for d, p in ((1, one), (2, two), (3, three))]
            state["v"] = [own] + sent
        elif name == "y":
            v, filed = add_parts(state["v"], filed)
            state["v"] = [v] + shifted(v, "z")
        elif name == "z":
            v, filed = add_parts(state["v"], filed)
            state["v"] = [v] + shifted(v, "col")
        elif name == "col":
            v, filed = choose(me, state["v"], filed)
            state["v"] = [v] + shifted(v, "y")
        elif name == "stack":
            v, filed = stack(me, state["v"], filed)
            state["v"] = [v, lax.ppermute(v, "row", SWAP)]
        elif name == "unpack":
            state["s"], state["e"], state["over"], filed = unpack(me, *state["v"], filed)
            state["inv"] = state["s"]
        elif name[0] == "e":
            state["e"], filed = eliminate_block(state["e"], filed)
        else:
            state["s"], state["inv"], state["e"] = spread(int(name[1]), state["e"], state["s"], state["inv"])
        return filed

    plan = {1: ["load"], 3: ["parts"], 4: ["core"], 6: ["y"], 7: ["z"], 9: ["col"], 10: ["stack"], 11: ["unpack"]}
    plan.update({12: ["e0", "s0"], 13: ["e1"], 14: ["s1", "e2"], 15: ["s2"]})

    def beside(s, filed):
        for name in plan.get(s, []):
            filed = gram_stage(name, filed)
        return filed

    filed = ring(0, SHORT, None, beside)
    filed = lax.cond(state["over"][0, 0] > 0.5, lambda f: ring(SHORT, CHUNKS, f), lambda f: f, filed)
    panel = state["panel"]
    prod = project(me, tiles, panel, snapshots, filed)
    state["e"] = eliminate_last(state["e"], prod)
    proj = row_sum(prod, state["e"])
    gram_stage("s3", filed)
    xh, xl = solve(scale, me, state["inv"], proj)
    out = finish(me, tiles, panel, snapshots, filed, xh, xl)
    return state["e"], out


def solution(mesh):
    placed = (P("row", "col"), P("row", "col"))
    return jax.shard_map(shards, mesh=mesh, in_specs=placed, out_specs=(P(), P("row", "col")), check_vma=False)
```

```python
import functools
import math

import jax
import jax.numpy as jnp
from jax import lax
from jax.experimental import pallas as pl
from jax.experimental.pallas import tpu as pltpu
from jax.sharding import PartitionSpec as P

TH = 512
TW = 128
TI = 8
TJ = 4
SLOTS = TI * TJ
PAIR = 2
LAG = 2
CHUNKS = SLOTS // PAIR
SHORT = 12
W = TJ * TW
F32 = jnp.float32
RELAY_COST = 5 * 10**9


def cost(flops):
    return pl.CostEstimate(flops=flops, bytes_accessed=0, transcendentals=0)

BF16 = jnp.bfloat16


def params(limit=16):
    return pltpu.CompilerParams(vmem_limit_bytes=limit * 1024 * 1024)


def sds(shape, dtype):
    return jax.ShapeDtypeStruct(shape, dtype)


def site(r):
    return r // 8, (r // 2) % 4, r % 2


def row_of(z, y, c):
    return (z % 4) * 8 + (y % 4) * 2 + c


def row_perm(f):
    return [(r, row_of(*f(*site(r)))) for r in range(32)]


SWAP = row_perm(lambda z, y, c: (z, y, 1 - c))
SHIFT = {
    "y": [row_perm(lambda z, y, c, d=d: (z, y + d, c)) for d in range(4)],
    "z": [row_perm(lambda z, y, c, d=d: (z + d, y, c)) for d in range(4)],
}
RING = [(r * 4 + x, r * 4 + (x + (1 if r % 2 == 0 else 3)) % 4) for r in range(32) for x in range(4)]


def ring_step(x):
    return lax.ppermute(x, ("row", "col"), RING)


def gather4(x, axis, me):
    h = x.shape[0]
    out = jnp.zeros((4 * h, x.shape[1]), x.dtype)
    for d in range(4):
        got = x if d == 0 else lax.ppermute(x, "row", SHIFT[axis][d])
        out = lax.dynamic_update_slice_in_dim(out, got, lax.rem(me + 4 - d, 4) * h, 0)
    return out


def core_gather(x, c):
    got = lax.ppermute(x, "row", SWAP)
    first = jnp.where(c == 0, x, got)
    second = jnp.where(c == 0, got, x)
    return jnp.concatenate([first, second], 0)


def row_sum(me, keep, give, beside):
    _, y, c = site(lax.axis_index("row"))
    own, one, two, three = add_and_cut(me, keep, lax.ppermute(give, "row", SWAP))
    sent = [lax.ppermute(p, "row", SHIFT["y"][d]) for d, p in ((1, one), (2, two), (3, three))]
    v = add_beside([own] + sent, own)
    v = add_beside([v] + shifted(v, "z"), beside)
    return core_gather(gather4(v, "y", y), c)


def shifted(x, axis):
    if axis == "col":
        return [lax.ppermute(x, "col", [(i, (i + d) % 4) for i in range(4)]) for d in (1, 2, 3)]
    return [lax.ppermute(x, "row", SHIFT[axis][d]) for d in (1, 2, 3)]


ANY = pl.BlockSpec(memory_space=pl.ANY)
VMEM = pl.BlockSpec(memory_space=pltpu.VMEM)
SMEM = pl.BlockSpec(memory_space=pltpu.SMEM)
ROOT, HOP, CORE, YPOS, COL = range(5)
UPPER = [(i, j) for i in range(TJ) for j in range(i, TJ)]
BLOCKS = len(UPPER) // 2 * TW
HALF = BLOCKS + 32
QUARTER = HALF // 4


def kept(shape):
    return pltpu.VMEM(shape, F32)


FILED = kept((TI * TH, W))


def pin(x):
    return pltpu.with_memory_space_constraint(x, pltpu.VMEM)


def in_hbm(x):
    return pltpu.with_memory_space_constraint(x, pltpu.HBM)


def split(x):
    high = x.astype(BF16)
    return high, (x - high.astype(F32)).astype(BF16)


def dot(a, b):
    return jnp.dot(a, b, preferred_element_type=F32)


def hdot(a, b, dims):
    return lax.dot_general(a, b, (dims, ((), ())), precision=lax.Precision.HIGHEST, preferred_element_type=F32)


def call(body, ins, outs, shapes, name, scratch=(), aliases=None, limit=16, flops=0):
    return pl.pallas_call(
        body,
        in_specs=ins,
        out_specs=outs,
        out_shape=shapes,
        scratch_shapes=list(scratch),
        input_output_aliases=aliases or {},
        compiler_params=params(limit),
        cost_estimate=cost(flops),
        name=name,
    )


def find(full, wanted):
    seen, place, found = jnp.int32(0), jnp.int32(0), jnp.int32(0)
    for t in range(SLOTS):
        hit = jnp.where((full[t] > 0) & (seen == wanted), 1, 0)
        place += hit * t
        found += hit
        seen += full[t]
    return place, found > 0


def relay_body(step, start, stop, fresh, choosing, last, staged, me, own, *refs):
    refs = list(refs)
    root = me[ROOT] > 0
    others = [refs.pop(0) for _ in range(3)] if choosing else []
    x_ref = refs.pop(0)
    got = None if step < LAG else refs.pop(0)
    if not fresh:
        refs.pop(0)
    filed = refs.pop(0)
    send = None if last else refs.pop(0)
    seen = refs.pop(0) if choosing else None
    (sem,) = refs
    full = []
    for t in range(SLOTS):
        at = t % TI, t // TI
        flag = own[at]
        for d, other in enumerate(others, 1):
            flag = jnp.where(me[COL] == d, other[at], flag)
        if seen is not None:
            seen[at] = flag
        full.append(flag)
    chunk = start + step - me[HOP] * LAG
    live = (chunk >= start) & (chunk < stop)

    def each(act, into_send, into_filed):
        for e in range(PAIR):
            place, found = places[e]
            rows = pl.ds(pl.multiple_of((place % TI) * TH, TH), TH)
            cols = pl.ds(pl.multiple_of((place // TI) * TW, TW), TW)
            part = pl.ds(e * TH, TH)

            def move(src, e=e, rows=rows, cols=cols, part=part):
                if into_filed:
                    act(pltpu.make_async_copy(src, filed.at[rows, cols], sem.at[2 * e]))
                if into_send:
                    act(pltpu.make_async_copy(src, send.at[part, :], sem.at[2 * e + 1]))

            @pl.when(found & live & root)
            def _(move=move, rows=rows, cols=cols, part=part):
                move(send.at[part, :] if staged and into_filed else x_ref.at[rows, cols])

            if got is not None:

                @pl.when(found & live & jnp.logical_not(root))
                def _(move=move, part=part):
                    move(got.at[part, :])

    places = [find(full, chunk * PAIR + e) for e in range(PAIR)]
    for into_send, into_filed in ((True, False), (False, True)) if staged else ((send is not None, True),):
        each(lambda c: c.start(), into_send, into_filed)
        each(lambda c: c.wait(), into_send, into_filed)


def relay(step, start, stop, last, me, own, others, x, got, filed):
    staged = start == 0 and step < LAG
    ins, args = [SMEM] * (2 + len(others)) + [ANY], [me, own, *others, in_hbm(x) if staged else pin(x)]
    if step >= LAG:
        ins.append(ANY)
        args.append(got)
    aliases = {}
    if filed is not None:
        aliases = {len(args): 0}
        ins.append(ANY)
        args.append(pin(filed))
    shapes, outs = [FILED], [ANY]
    if not last:
        shapes.append(kept((PAIR * TH, TW)))
        outs.append(ANY)
    if others:
        shapes.append(sds((TI, TJ), jnp.int32))
        outs.append(SMEM)
    out = list(
        call(
            functools.partial(relay_body, step, start, stop, filed is None, bool(others), last, staged),
            ins,
            outs,
            shapes,
            "relay",
            [pltpu.SemaphoreType.DMA((2 * PAIR,))],
            aliases,
            4,
            RELAY_COST,
        )(*args)
    )
    filed = out.pop(0)
    send = None if last else out.pop(0)
    return filed, send, out.pop(0) if others else None


def load_body(x_ref, _, out, sem):
    copies = [
        pltpu.make_async_copy(x_ref.at[pl.ds(i * TH, TH), :], out.at[pl.ds(i * TH, TH), :], sem.at[i]) for i in range(TI)
    ]
    for c in copies:
        c.start()
    for c in copies:
        c.wait()


def load(x, before):
    return call(load_body, [ANY, ANY], ANY, FILED, "load", [pltpu.SemaphoreType.DMA((TI,))])(in_hbm(x), before)


def gram_body(me, occ, x_ref, filed_in, keep, give, filed, gram_ref, cross_ref):
    i = pl.program_id(0)

    @pl.when(i == 0)
    def _():
        gram_ref[...] = jnp.zeros_like(gram_ref)
        cross_ref[...] = jnp.zeros_like(cross_ref)

    @pl.when(me[ROOT] > 0)
    def _():
        x = jnp.concatenate([x_ref[:, j * TW : (j + 1) * TW] * occ[i, j].astype(F32) for j in range(TJ)], 1)
        high, low = split(x)
        h = W // 2
        high_t, low_t = high.T, low.T
        gram_ref[:h, :] += dot(high_t[:h], high) + dot(low_t[:h], low)
        gram_ref[h:, h:] += dot(high_t[h:], high[:, h:]) + dot(low_t[h:], low[:, h:])
        cross_ref[...] += dot(high_t, low)

    @pl.when(i == TI - 1)
    def _():
        full = jnp.int32(0)
        for t in range(SLOTS):
            full += occ[t % TI, t // TI]
        over = jnp.where(full > SHORT * PAIR, 1.0, 0.0)
        keep[BLOCKS:, :] = jnp.full((HALF - BLOCKS, TW), over, F32)
        give[BLOCKS:, :] = jnp.full((HALF - BLOCKS, TW), over, F32)
        for b, (r, q) in enumerate(UPPER):
            rows, cols = slice(r * TW, (r + 1) * TW), slice(q * TW, (q + 1) * TW)
            block = gram_ref[rows, cols] + cross_ref[rows, cols] + cross_ref[cols, rows].T
            part, at = divmod(b * TW, BLOCKS)
            mine = me[CORE] == part

            @pl.when(mine)
            def _(block=block, at=at):
                keep[at : at + TW, :] = block

            @pl.when(jnp.logical_not(mine))
            def _(block=block, at=at):
                give[at : at + TW, :] = block


def gram_part(me, occ, x, filed):
    whole = pl.BlockSpec((HALF, TW), lambda i, *_: (0, 0))
    return pl.pallas_call(
        gram_body,
        grid_spec=pltpu.PrefetchScalarGridSpec(
            num_scalar_prefetch=2,
            grid=(TI,),
            in_specs=[pl.BlockSpec((TH, W), lambda i, me, occ: (i * me[ROOT], 0)), ANY],
            out_specs=[whole, whole, ANY],
            scratch_shapes=[pltpu.VMEM((W, W), F32), pltpu.VMEM((W, W), F32)],
        ),
        out_shape=[sds((HALF, TW), F32), sds((HALF, TW), F32), FILED],
        input_output_aliases={3: 2},
        compiler_params=params(24),
        cost_estimate=cost(0),
        name="gram_part",
    )(me, occ, pin(x), pin(filed))


def add_body(*refs):
    ins, (_, out, _) = refs[:-3], refs[-3:]
    total = ins[0][...]
    for r in ins[1:]:
        total = total + r[...]
    out[...] = total


def add_parts(parts, filed):
    n = len(parts)
    return call(
        add_body,
        [VMEM] * n + [ANY],
        [VMEM, ANY],
        [sds(parts[0].shape, F32), FILED],
        "add_parts",
        aliases={n: 1},
    )(*parts, pin(filed))


def add_beside_body(*refs):
    add_body(*refs[:-2], None, refs[-1], None)


def add_beside(parts, beside):
    return call(add_beside_body, [VMEM] * len(parts) + [ANY], VMEM, sds(parts[0].shape, F32), "add_beside")(*parts, beside)


def add_cut_body(me, a, b, _, own, one, two, three, __, total):
    total[...] = a[...] + b[...]
    for k, out in enumerate((own, one, two, three)):
        at = lax.rem(me[YPOS] + k, 4) * QUARTER
        out[...] = total[pl.ds(pl.multiple_of(at, 8), QUARTER), :]


def add_cut(me, parts, filed):
    return call(
        add_cut_body,
        [SMEM] + [VMEM] * 2 + [ANY],
        [VMEM] * 4 + [ANY],
        [sds((QUARTER, TW), F32)] * 4 + [FILED],
        "add_cut",
        [pltpu.VMEM((HALF, TW), F32)],
        {3: 4},
    )(me, *parts, pin(filed))


def choose_body(me, a, b, c, d, _, out, __):
    for k, ref in enumerate((a, b, c, d)):

        @pl.when(me[COL] == k)
        def _(ref=ref):
            out[...] = ref[...]


def choose(me, parts, filed):
    return call(
        choose_body,
        [SMEM] + [VMEM] * 4 + [ANY],
        [VMEM, ANY],
        [sds((QUARTER, TW), F32), FILED],
        "choose",
        aliases={5: 1},
    )(me, *parts, pin(filed))


def stack_body(me, a, b, c, d, _, out, __):
    for k, ref in enumerate((a, b, c, d)):
        at = lax.rem(me[YPOS] + 4 - k, 4) * QUARTER
        out[pl.ds(pl.multiple_of(at, 8), QUARTER), :] = ref[...]


def stack(me, parts, filed):
    return call(
        stack_body,
        [SMEM] + [VMEM] * 4 + [ANY],
        [VMEM, ANY],
        [sds((HALF, TW), F32), FILED],
        "stack",
        aliases={5: 1},
    )(me, *parts, pin(filed))


def unpack_body(me, mine, other, _, s_ref, e_ref, over_ref, __):
    over_ref[...] = mine[BLOCKS : BLOCKS + 8, :]
    s_ref[...] = jnp.zeros_like(s_ref)
    for b, (r, q) in enumerate(UPPER):
        part, at = divmod(b * TW, BLOCKS)
        block = jnp.where(me[CORE] == part, mine[at : at + TW, :], other[at : at + TW, :])
        s_ref[r * TW : (r + 1) * TW, q * TW : (q + 1) * TW] = block
        if b == 0:
            e_ref[:, :TW] = block
    e_ref[:, TW:] = unit()


def unpack(me, mine, other, filed):
    return call(
        unpack_body,
        [SMEM, VMEM, VMEM, ANY],
        [VMEM, VMEM, VMEM, ANY],
        [sds((W, W), F32), sds((TW, 2 * TW), F32), sds((8, TW), F32), FILED],
        "unpack",
        aliases={3: 3},
    )(me, mine, other, pin(filed))


def unit():
    r = lax.broadcasted_iota(jnp.int32, (TW, TW), 0)
    c = lax.broadcasted_iota(jnp.int32, (TW, TW), 1)
    return jnp.where(r == c, 1.0, 0.0).astype(F32)


def eliminate(m_rows, v_rows, start, stop):
    groups = len(m_rows)
    full = (8, m_rows[0].shape[1])
    sub = lax.broadcasted_iota(jnp.int32, full, 0)

    def row(x, r):
        return jnp.broadcast_to(x[r : r + 1, :], full)

    for g in range(start, stop):
        lanes = [8 * g + k for k in range(8)]
        columns = [jnp.broadcast_to(m_rows[g][:, lane : lane + 1], full) for lane in lanes]
        a = {(r, k): row(columns[k], r) for k in range(8) for r in range(k, 8)}
        rm = [row(m_rows[g], r) for r in range(8)]
        rv = [row(v_rows[g], r) for r in range(8)]
        inverse = []
        for k in range(8):
            scale = lax.rsqrt(a[k, k])
            inverse.append(scale)
            for r in range(k + 1, 8):
                a[r, k] = a[r, k] * scale
            for c in range(k + 1, 8):
                for r in range(c, 8):
                    a[r, c] = a[r, c] - a[r, k] * a[c, k]
            rm[k] = rm[k] * scale
            rv[k] = rv[k] * scale
            for r in range(k + 1, 8):
                rm[r] = rm[r] - a[r, k] * rm[k]
                rv[r] = rv[r] - a[r, k] * rv[k]
        for i in range(g + 1, groups):
            factor = [jnp.broadcast_to(m_rows[i][:, lane : lane + 1], full) for lane in lanes]
            new_m, new_v = m_rows[i], v_rows[i]
            for k in range(8):
                factor[k] = factor[k] * inverse[k]
                for r in range(k + 1, 8):
                    factor[r] = factor[r] - factor[k] * a[r, k]
                new_m = new_m - factor[k] * rm[k]
                new_v = new_v - factor[k] * rv[k]
            m_rows[i], v_rows[i] = new_m, new_v
        top_m, top_v = rm[0], rv[0]
        for r in range(1, 8):
            top_m = jnp.where(sub == r, rm[r], top_m)
            top_v = jnp.where(sub == r, rv[r], top_v)
        m_rows[g], v_rows[g] = top_m, top_v
    return m_rows, v_rows


def eliminate_body(e_in, _, e_out, __):
    groups = range(TW // 8)
    m_rows = [e_in[8 * g : 8 * g + 8, :TW] for g in groups]
    v_rows = [e_in[8 * g : 8 * g + 8, TW:] for g in groups]
    m_rows, v_rows = eliminate(m_rows, v_rows, 0, TW // 8)
    r = lax.broadcasted_iota(jnp.int32, (8, TW), 0)
    c = lax.broadcasted_iota(jnp.int32, (8, TW), 1)
    for g in groups:
        e_out[8 * g : 8 * g + 8, :TW] = jnp.where(r + 8 * g <= c, m_rows[g], 0.0)
        e_out[8 * g : 8 * g + 8, TW:] = v_rows[g]


def eliminate_block(e, filed):
    return call(
        eliminate_body, [VMEM, ANY], [VMEM, ANY], [sds((TW, 2 * TW), F32), FILED], "eliminate", aliases={1: 1}
    )(e, pin(filed))


def eliminate_last(e, before):
    body = lambda e_in, _, e_out: eliminate_body(e_in, None, e_out, None)
    return call(body, [VMEM, ANY], VMEM, sds((TW, 2 * TW), F32), "eliminate", flops=RELAY_COST)(e, before)


def spread_body(b, e_in, s_in, v_in, s_ref, v_ref, e_out):
    lo, hi = b * TW, (b + 1) * TW
    s_ref[...] = s_in[...]
    if b == 0:
        v_ref[...] = jnp.zeros_like(v_ref)
    else:
        v_ref[...] = v_in[...]
    inv = e_in[:, TW:]
    s_ref[lo:hi, lo:hi] = e_in[:, :TW]
    v_ref[lo:hi, lo:hi] = inv
    if b > 0:
        v_ref[lo:hi, :lo] = hdot(inv, v_in[lo:hi, :lo], ((1,), (0,)))
    if hi < W:
        right = hdot(inv, s_in[lo:hi, hi:], ((1,), (0,)))
        s_ref[lo:hi, hi:] = right
        s_ref[hi:, hi:] -= hdot(right, right, ((0,), (0,)))
        s_ref[hi:, lo:hi] = jnp.zeros((W - hi, TW), F32)
        v_ref[hi:, :hi] -= hdot(right, v_ref[lo:hi, :hi], ((0,), (0,)))
        e_out[:, :TW] = s_ref[hi : hi + TW, hi : hi + TW]
        e_out[:, TW:] = unit()
    else:
        e_out[0] = s_ref[: W // 2, : W // 2]
        e_out[1] = s_ref[W // 2 :, W // 2 :]


def spread(b, e, s, v):
    return call(
        functools.partial(spread_body, b),
        [VMEM] * 3,
        [VMEM] * 3,
        [sds((W, W), F32), sds((W, W), F32), sds((TW, 2 * TW) if b < TJ - 1 else (2, W // 2, W // 2), F32)],
        "spread",
    )(e, s, v)


def masked(ref, flags, i, r):
    parts = []
    for j in range(TJ):
        block = ref[r * TH : (r + 1) * TH, j * TW : (j + 1) * TW]
        parts.append(jnp.where(flags[i * DEEP + r, j] > 0, block, jnp.zeros_like(block)))
    return jnp.concatenate(parts, 1)


def occupied(flags, row):
    count, starts = jnp.int32(0), [jnp.int32(0)] * TJ
    for j in range(TJ):
        for q in range(j + 1):
            starts[q] += jnp.where((flags[row, j] > 0) & (count == q), j * TW, 0)
        count += jnp.where(flags[row, j] > 0, 1, 0)
    return count, [pl.ds(pl.multiple_of(v, TW), TW) for v in starts]


DEEP = 2


def project_body(me, occ, panel, x_ref, a_ref, keep, give, c_ref):
    i = pl.program_id(0)

    @pl.when(i == 0)
    def _():
        c_ref[...] = jnp.zeros_like(c_ref)

    for r in range(DEEP):
        count, at = occupied(panel, i * DEEP + r)
        for k in range(1, TJ + 1):

            @pl.when((me[ROOT] == 0) & (count == k))
            def _(r=r, at=at[:k]):
                ah, al = split(jnp.concatenate([a_ref[r * TH : (r + 1) * TH, v] for v in at], 1))
                bh, bl = split(masked(x_ref, occ, i, r))
                ah_t, al_t = ah.T, al.T
                part = dot(jnp.concatenate([ah_t, al_t, ah_t], 1), jnp.concatenate([bh, bh, bl], 0))
                for q, v in enumerate(at):
                    c_ref[v, :] += part[q * TW : (q + 1) * TW]

    @pl.when(i == TI // DEEP - 1)
    def _():
        half = W // 2
        mine = pl.multiple_of(me[CORE] * half, half)
        keep[...] = c_ref[pl.ds(mine, half), :]
        give[...] = c_ref[pl.ds(half - mine, half), :]


def project(me, occ, panel, x, filed):
    block = pl.BlockSpec((DEEP * TH, W), lambda i, *_: (i, 0))
    whole = pl.BlockSpec((W // 2, W), lambda i, *_: (0, 0))
    return pl.pallas_call(
        project_body,
        grid_spec=pltpu.PrefetchScalarGridSpec(
            num_scalar_prefetch=3,
            grid=(TI // DEEP,),
            in_specs=[block, block],
            out_specs=[whole, whole],
            scratch_shapes=[pltpu.VMEM((W, W), F32)],
        ),
        out_shape=[sds((W // 2, W), F32)] * 2,
        compiler_params=params(40),
        cost_estimate=cost(0),
        name="project",
    )(me, occ, panel, in_hbm(x), in_hbm(filed))


def halve_body(me, a, b, own, one, two, three, total):
    total[...] = a[...] + b[...]
    h = W // 8
    for k, out in enumerate((own, one, two, three)):
        at = lax.rem(me[YPOS] + k, 4) * h
        out[...] = total[pl.ds(pl.multiple_of(at, h), h), :]


def add_and_cut(me, a, b):
    return call(
        halve_body,
        [SMEM, VMEM, VMEM],
        [VMEM] * 4,
        [sds((W // 8, W), F32)] * 4,
        "add_and_cut",
        [pltpu.VMEM((W // 2, W), F32)],
    )(me, a, b)


def solve_body(scale, me, v_ref, c_ref, high_ref, low_ref):
    v, h = v_ref[...], W // 2
    rows, cols = ((1,), (0,)), ((0,), (0,))
    top = hdot(v[:h, :h], c_ref[:h, :], rows)
    low = hdot(v[h:, :], c_ref[...], rows)
    coef = jnp.concatenate([hdot(v[:h, :h], top, cols) + hdot(v[h:, :h], low, cols), hdot(v[h:, h:], low, cols)], 0)
    coef = jnp.where(me[ROOT] > 0, -scale * v.T, coef)
    high_ref[...], low_ref[...] = split(coef)


def solve(scale, me, inv, proj):
    return call(
        functools.partial(solve_body, scale),
        [SMEM, VMEM, VMEM],
        [VMEM, VMEM],
        [sds((W, W), BF16)] * 2,
        "solve",
    )(me, inv, proj)


def finish_body(me, occ, panel, x_ref, a_ref, xh, xl, out_ref):
    i = pl.program_id(0)
    keep = 1 - me[ROOT]
    for r in range(DEEP):
        rows = slice(r * TH, (r + 1) * TH)
        count, at = occupied(panel, i * DEEP + r)
        for k in range(TJ + 1):

            @pl.when(count == k)
            def _(r=r, rows=rows, at=at[:k]):
                if at:
                    ah, al = split(jnp.concatenate([a_ref[rows, v] for v in at], 1))
                    high, low = [xh[v, :] for v in at], [xl[v, :] for v in at]
                    taken = dot(jnp.concatenate([ah, al, ah], 1), jnp.concatenate(high + high + low, 0))
                else:
                    taken = jnp.zeros((TH, W), F32)
                for j in range(TJ):
                    cols = slice(j * TW, (j + 1) * TW)
                    keep_tile = (occ[i * DEEP + r, j] * keep).astype(F32)
                    out_ref[rows, cols] = x_ref[rows, cols] * keep_tile - taken[:, cols]


def finish(me, occ, panel, x, filed, xh, xl):
    rows = TI * TH
    block = pl.BlockSpec((DEEP * TH, W), lambda i, *_: (i, 0))
    whole = pl.BlockSpec((W, W), lambda i, *_: (0, 0))
    return pl.pallas_call(
        finish_body,
        grid_spec=pltpu.PrefetchScalarGridSpec(
            num_scalar_prefetch=3,
            grid=(TI // DEEP,),
            in_specs=[block, block, whole, whole],
            out_specs=block,
        ),
        out_shape=sds((rows, W), F32),
        compiler_params=params(40),
        cost_estimate=cost(0),
        name="finish",
    )(me, occ, panel, in_hbm(x), in_hbm(filed), xh, xl)


def shards(snapshots, tiles):
    col = lax.axis_index("col")
    _, y, core = site(lax.axis_index("row"))
    root = col == 0
    hop = jnp.where(core == 0, col, (4 - col) % 4)
    scale = math.sqrt(snapshots.shape[0] * lax.axis_size("row"))
    me = jnp.stack([root.astype(jnp.int32), hop, core, y, col]).astype(jnp.int32)
    state = {"x": snapshots, "panel": tiles}
    flags = shifted(tiles, "col")

    def ring(start, stop, filed, beside=None):
        got = [None] * LAG
        steps = stop - start + 3 * LAG
        for s in range(steps):
            last = s >= steps - LAG
            others = flags if start == 0 and s == LAG else []
            filed, send, seen = relay(s, start, stop, last, me, state["panel"], others, state["x"], got[s % LAG], filed)
            if others:
                state["panel"] = seen
            if not last:
                got[s % LAG] = ring_step(send)
            if beside is not None:
                filed = beside(s, filed)
        return filed

    def gram_stage(name, filed):
        if name == "load":
            state["x"] = load(snapshots, filed)
        elif name == "parts":
            keep, give, filed = gram_part(me, tiles, state["x"], filed)
            state["v"] = [keep, lax.ppermute(give, "row", SWAP)]
        elif name == "core":
            own, one, two, three, filed = add_cut(me, state["v"], filed)
            sent = [lax.ppermute(p, "row", SHIFT["y"][d]) for d, p in ((1, one), (2, two), (3, three))]
            state["v"] = [own] + sent
        elif name == "y":
            v, filed = add_parts(state["v"], filed)
            state["v"] = [v] + shifted(v, "z")
        elif name == "z":
            v, filed = add_parts(state["v"], filed)
            state["v"] = [v] + shifted(v, "col")
        elif name == "col":
            v, filed = choose(me, state["v"], filed)
            state["v"] = [v] + shifted(v, "y")
        elif name == "stack":
            v, filed = stack(me, state["v"], filed)
            state["v"] = [v, lax.ppermute(v, "row", SWAP)]
        elif name == "unpack":
            state["s"], state["e"], state["over"], filed = unpack(me, *state["v"], filed)
            state["inv"] = state["s"]
        elif name[0] == "e":
            state["e"], filed = eliminate_block(state["e"], filed)
        else:
            state["s"], state["inv"], state["e"] = spread(int(name[1]), state["e"], state["s"], state["inv"])
        return filed

    plan = {1: ["load"], 3: ["parts"], 4: ["core"], 6: ["y"], 7: ["z"], 9: ["col"], 10: ["stack"], 11: ["unpack"]}
    plan.update({12: ["e0", "s0"], 13: ["e1"], 14: ["s1", "e2"], 15: ["s2"]})

    def beside(s, filed):
        for name in plan.get(s, []):
            filed = gram_stage(name, filed)
        return filed

    filed = ring(0, SHORT, None, beside)
    filed = lax.cond(state["over"][0, 0] > 0.5, lambda f: ring(SHORT, CHUNKS, f), lambda f: f, filed)
    panel = state["panel"]
    keep, give = project(me, tiles, panel, snapshots, filed)
    state["e"] = eliminate_last(state["e"], keep)
    proj = row_sum(me, keep, give, state["e"])
    gram_stage("s3", filed)
    xh, xl = solve(scale, me, state["inv"], proj)
    out = finish(me, tiles, panel, snapshots, filed, xh, xl)
    return state["e"], out


def solution(mesh):
    placed = (P("row", "col"), P("row", "col"))
    return jax.shard_map(shards, mesh=mesh, in_specs=placed, out_specs=(P(), P("row", "col")), check_vma=False)
```

```python
import functools
import math

import jax
import jax.numpy as jnp
from jax import lax
from jax.experimental import pallas as pl
from jax.experimental.pallas import tpu as pltpu
from jax.sharding import PartitionSpec as P

TH = 512
TW = 128
TI = 8
TJ = 4
SLOTS = TI * TJ
PAIR = 2
LAG = 2
CHUNKS = SLOTS // PAIR
SHORT = 12
W = TJ * TW
F32 = jnp.float32
RELAY_COST = 5 * 10**9


def cost(flops):
    return pl.CostEstimate(flops=flops, bytes_accessed=0, transcendentals=0)

BF16 = jnp.bfloat16


def params(limit=16):
    return pltpu.CompilerParams(vmem_limit_bytes=limit * 1024 * 1024)


def sds(shape, dtype):
    return jax.ShapeDtypeStruct(shape, dtype)


def site(r):
    return r // 8, (r // 2) % 4, r % 2


def row_of(z, y, c):
    return (z % 4) * 8 + (y % 4) * 2 + c


def row_perm(f):
    return [(r, row_of(*f(*site(r)))) for r in range(32)]


SWAP = row_perm(lambda z, y, c: (z, y, 1 - c))
SHIFT = {
    "y": [row_perm(lambda z, y, c, d=d: (z, y + d, c)) for d in range(4)],
    "z": [row_perm(lambda z, y, c, d=d: (z + d, y, c)) for d in range(4)],
}
RING = [(r * 4 + x, r * 4 + (x + (1 if r % 2 == 0 else 3)) % 4) for r in range(32) for x in range(4)]


def ring_step(x):
    return lax.ppermute(x, ("row", "col"), RING)


def gather4(x, axis, me):
    h = x.shape[0]
    out = jnp.zeros((4 * h, x.shape[1]), x.dtype)
    for d in range(4):
        got = x if d == 0 else lax.ppermute(x, "row", SHIFT[axis][d])
        out = lax.dynamic_update_slice_in_dim(out, got, lax.rem(me + 4 - d, 4) * h, 0)
    return out


def core_gather(x, c):
    got = lax.ppermute(x, "row", SWAP)
    first = jnp.where(c == 0, x, got)
    second = jnp.where(c == 0, got, x)
    return jnp.concatenate([first, second], 0)


def row_sum(me, keep, give, beside):
    _, y, c = site(lax.axis_index("row"))
    own, one, two, three = add_and_cut(me, keep, lax.ppermute(give, "row", SWAP))
    sent = [lax.ppermute(p, "row", SHIFT["y"][d]) for d, p in ((1, one), (2, two), (3, three))]
    v = add_beside([own] + sent, own)
    v = add_beside([v] + shifted(v, "z"), beside)
    return core_gather(gather4(v, "y", y), c)


def shifted(x, axis):
    if axis == "col":
        return [lax.ppermute(x, "col", [(i, (i + d) % 4) for i in range(4)]) for d in (1, 2, 3)]
    return [lax.ppermute(x, "row", SHIFT[axis][d]) for d in (1, 2, 3)]


ANY = pl.BlockSpec(memory_space=pl.ANY)
VMEM = pl.BlockSpec(memory_space=pltpu.VMEM)
SMEM = pl.BlockSpec(memory_space=pltpu.SMEM)
ROOT, HOP, CORE, YPOS, COL = range(5)
UPPER = [(i, j) for i in range(TJ) for j in range(i, TJ)]
BLOCKS = len(UPPER) // 2 * TW
HALF = BLOCKS + 32
QUARTER = HALF // 4


def kept(shape):
    return pltpu.VMEM(shape, F32)


FILED = kept((TI * TH, W))


def pin(x):
    return pltpu.with_memory_space_constraint(x, pltpu.VMEM)


def in_hbm(x):
    return pltpu.with_memory_space_constraint(x, pltpu.HBM)


def split(x):
    high = x.astype(BF16)
    return high, (x - high.astype(F32)).astype(BF16)


def dot(a, b):
    return jnp.dot(a, b, preferred_element_type=F32)


def hdot(a, b, dims):
    return lax.dot_general(a, b, (dims, ((), ())), precision=lax.Precision.HIGHEST, preferred_element_type=F32)


def call(body, ins, outs, shapes, name, scratch=(), aliases=None, limit=16, flops=0):
    return pl.pallas_call(
        body,
        in_specs=ins,
        out_specs=outs,
        out_shape=shapes,
        scratch_shapes=list(scratch),
        input_output_aliases=aliases or {},
        compiler_params=params(limit),
        cost_estimate=cost(flops),
        name=name,
    )


def find(full, wanted):
    seen, place, found = jnp.int32(0), jnp.int32(0), jnp.int32(0)
    for t in range(SLOTS):
        hit = jnp.where((full[t] > 0) & (seen == wanted), 1, 0)
        place += hit * t
        found += hit
        seen += full[t]
    return place, found > 0


def relay_body(step, start, stop, fresh, choosing, last, staged, me, own, *refs):
    refs = list(refs)
    root = me[ROOT] > 0
    others = [refs.pop(0) for _ in range(3)] if choosing else []
    x_ref = refs.pop(0)
    got = None if step < LAG else refs.pop(0)
    if not fresh:
        refs.pop(0)
    filed = refs.pop(0)
    send = None if last else refs.pop(0)
    seen = refs.pop(0) if choosing else None
    (sem,) = refs
    full = []
    for t in range(SLOTS):
        at = t % TI, t // TI
        flag = own[at]
        for d, other in enumerate(others, 1):
            flag = jnp.where(me[COL] == d, other[at], flag)
        if seen is not None:
            seen[at] = flag
        full.append(flag)
    chunk = start + step - me[HOP] * LAG
    live = (chunk >= start) & (chunk < stop)

    def each(act, into_send, into_filed):
        for e in range(PAIR):
            place, found = places[e]
            rows = pl.ds(pl.multiple_of((place % TI) * TH, TH), TH)
            cols = pl.ds(pl.multiple_of((place // TI) * TW, TW), TW)
            part = pl.ds(e * TH, TH)

            def move(src, e=e, rows=rows, cols=cols, part=part):
                if into_filed:
                    act(pltpu.make_async_copy(src, filed.at[rows, cols], sem.at[2 * e]))
                if into_send:
                    act(pltpu.make_async_copy(src, send.at[part, :], sem.at[2 * e + 1]))

            @pl.when(found & live & root)
            def _(move=move, rows=rows, cols=cols, part=part):
                move(send.at[part, :] if staged and into_filed else x_ref.at[rows, cols])

            if got is not None:

                @pl.when(found & live & jnp.logical_not(root))
                def _(move=move, part=part):
                    move(got.at[part, :])

    places = [find(full, chunk * PAIR + e) for e in range(PAIR)]
    for into_send, into_filed in ((True, False), (False, True)) if staged else ((send is not None, True),):
        each(lambda c: c.start(), into_send, into_filed)
        each(lambda c: c.wait(), into_send, into_filed)


def relay(step, start, stop, last, me, own, others, x, got, filed):
    staged = start == 0 and step < LAG
    ins, args = [SMEM] * (2 + len(others)) + [ANY], [me, own, *others, in_hbm(x) if staged else pin(x)]
    if step >= LAG:
        ins.append(ANY)
        args.append(got)
    aliases = {}
    if filed is not None:
        aliases = {len(args): 0}
        ins.append(ANY)
        args.append(pin(filed))
    shapes, outs = [FILED], [ANY]
    if not last:
        shapes.append(kept((PAIR * TH, TW)))
        outs.append(ANY)
    if others:
        shapes.append(sds((TI, TJ), jnp.int32))
        outs.append(SMEM)
    out = list(
        call(
            functools.partial(relay_body, step, start, stop, filed is None, bool(others), last, staged),
            ins,
            outs,
            shapes,
            "relay",
            [pltpu.SemaphoreType.DMA((2 * PAIR,))],
            aliases,
            4,
            RELAY_COST,
        )(*args)
    )
    filed = out.pop(0)
    send = None if last else out.pop(0)
    return filed, send, out.pop(0) if others else None


def load_body(x_ref, _, out, sem):
    copies = [
        pltpu.make_async_copy(x_ref.at[pl.ds(i * TH, TH), :], out.at[pl.ds(i * TH, TH), :], sem.at[i]) for i in range(TI)
    ]
    for c in copies:
        c.start()
    for c in copies:
        c.wait()


def load(x, before):
    return call(load_body, [ANY, ANY], ANY, FILED, "load", [pltpu.SemaphoreType.DMA((TI,))])(in_hbm(x), before)


def gram_body(me, occ, x_ref, filed_in, keep, give, filed, gram_ref, cross_ref):
    i = pl.program_id(0)

    @pl.when(i == 0)
    def _():
        gram_ref[...] = jnp.zeros_like(gram_ref)
        cross_ref[...] = jnp.zeros_like(cross_ref)

    @pl.when(me[ROOT] > 0)
    def _():
        x = jnp.concatenate([x_ref[:, j * TW : (j + 1) * TW] * occ[i, j].astype(F32) for j in range(TJ)], 1)
        high, low = split(x)
        h = W // 2
        high_t, low_t = high.T, low.T
        gram_ref[:h, :] += dot(high_t[:h], high) + dot(low_t[:h], low)
        gram_ref[h:, h:] += dot(high_t[h:], high[:, h:]) + dot(low_t[h:], low[:, h:])
        cross_ref[...] += dot(high_t, low)

    @pl.when(i == TI - 1)
    def _():
        full = jnp.int32(0)
        for t in range(SLOTS):
            full += occ[t % TI, t // TI]
        over = jnp.where(full > SHORT * PAIR, 1.0, 0.0)
        keep[BLOCKS:, :] = jnp.full((HALF - BLOCKS, TW), over, F32)
        give[BLOCKS:, :] = jnp.full((HALF - BLOCKS, TW), over, F32)
        for b, (r, q) in enumerate(UPPER):
            rows, cols = slice(r * TW, (r + 1) * TW), slice(q * TW, (q + 1) * TW)
            block = gram_ref[rows, cols] + cross_ref[rows, cols] + cross_ref[cols, rows].T
            part, at = divmod(b * TW, BLOCKS)
            mine = me[CORE] == part

            @pl.when(mine)
            def _(block=block, at=at):
                keep[at : at + TW, :] = block

            @pl.when(jnp.logical_not(mine))
            def _(block=block, at=at):
                give[at : at + TW, :] = block


def gram_part(me, occ, x, filed):
    whole = pl.BlockSpec((HALF, TW), lambda i, *_: (0, 0))
    return pl.pallas_call(
        gram_body,
        grid_spec=pltpu.PrefetchScalarGridSpec(
            num_scalar_prefetch=2,
            grid=(TI,),
            in_specs=[pl.BlockSpec((TH, W), lambda i, me, occ: (i * me[ROOT], 0)), ANY],
            out_specs=[whole, whole, ANY],
            scratch_shapes=[pltpu.VMEM((W, W), F32), pltpu.VMEM((W, W), F32)],
        ),
        out_shape=[sds((HALF, TW), F32), sds((HALF, TW), F32), FILED],
        input_output_aliases={3: 2},
        compiler_params=params(24),
        cost_estimate=cost(0),
        name="gram_part",
    )(me, occ, pin(x), pin(filed))


def add_body(*refs):
    ins, (_, out, _) = refs[:-3], refs[-3:]
    total = ins[0][...]
    for r in ins[1:]:
        total = total + r[...]
    out[...] = total


def add_parts(parts, filed):
    n = len(parts)
    return call(
        add_body,
        [VMEM] * n + [ANY],
        [VMEM, ANY],
        [sds(parts[0].shape, F32), FILED],
        "add_parts",
        aliases={n: 1},
    )(*parts, pin(filed))


def add_beside_body(*refs):
    add_body(*refs[:-2], None, refs[-1], None)


def add_beside(parts, beside):
    return call(add_beside_body, [VMEM] * len(parts) + [ANY], VMEM, sds(parts[0].shape, F32), "add_beside")(*parts, beside)


def add_cut_body(me, a, b, _, own, one, two, three, __, total):
    total[...] = a[...] + b[...]
    for k, out in enumerate((own, one, two, three)):
        at = lax.rem(me[YPOS] + k, 4) * QUARTER
        out[...] = total[pl.ds(pl.multiple_of(at, 8), QUARTER), :]


def add_cut(me, parts, filed):
    return call(
        add_cut_body,
        [SMEM] + [VMEM] * 2 + [ANY],
        [VMEM] * 4 + [ANY],
        [sds((QUARTER, TW), F32)] * 4 + [FILED],
        "add_cut",
        [pltpu.VMEM((HALF, TW), F32)],
        {3: 4},
    )(me, *parts, pin(filed))


def choose_body(me, a, b, c, d, _, out, __):
    for k, ref in enumerate((a, b, c, d)):

        @pl.when(me[COL] == k)
        def _(ref=ref):
            out[...] = ref[...]


def choose(me, parts, filed):
    return call(
        choose_body,
        [SMEM] + [VMEM] * 4 + [ANY],
        [VMEM, ANY],
        [sds((QUARTER, TW), F32), FILED],
        "choose",
        aliases={5: 1},
    )(me, *parts, pin(filed))


def stack_body(me, a, b, c, d, _, out, __):
    for k, ref in enumerate((a, b, c, d)):
        at = lax.rem(me[YPOS] + 4 - k, 4) * QUARTER
        out[pl.ds(pl.multiple_of(at, 8), QUARTER), :] = ref[...]


def stack(me, parts, filed):
    return call(
        stack_body,
        [SMEM] + [VMEM] * 4 + [ANY],
        [VMEM, ANY],
        [sds((HALF, TW), F32), FILED],
        "stack",
        aliases={5: 1},
    )(me, *parts, pin(filed))


def unpack_body(me, mine, other, _, s_ref, e_ref, over_ref, __):
    over_ref[...] = mine[BLOCKS : BLOCKS + 8, :]
    s_ref[...] = jnp.zeros_like(s_ref)
    for b, (r, q) in enumerate(UPPER):
        part, at = divmod(b * TW, BLOCKS)
        block = jnp.where(me[CORE] == part, mine[at : at + TW, :], other[at : at + TW, :])
        s_ref[r * TW : (r + 1) * TW, q * TW : (q + 1) * TW] = block
        if b == 0:
            e_ref[:, :TW] = block
    e_ref[:, TW:] = unit()


def unpack(me, mine, other, filed):
    return call(
        unpack_body,
        [SMEM, VMEM, VMEM, ANY],
        [VMEM, VMEM, VMEM, ANY],
        [sds((W, W), F32), sds((TW, 2 * TW), F32), sds((8, TW), F32), FILED],
        "unpack",
        aliases={3: 3},
    )(me, mine, other, pin(filed))


def unit():
    r = lax.broadcasted_iota(jnp.int32, (TW, TW), 0)
    c = lax.broadcasted_iota(jnp.int32, (TW, TW), 1)
    return jnp.where(r == c, 1.0, 0.0).astype(F32)


def eliminate(m_rows, v_rows, start, stop):
    groups = len(m_rows)
    full = (8, m_rows[0].shape[1])
    sub = lax.broadcasted_iota(jnp.int32, full, 0)

    def row(x, r):
        return jnp.broadcast_to(x[r : r + 1, :], full)

    for g in range(start, stop):
        lanes = [8 * g + k for k in range(8)]
        columns = [jnp.broadcast_to(m_rows[g][:, lane : lane + 1], full) for lane in lanes]
        a = {(r, k): row(columns[k], r) for k in range(8) for r in range(k, 8)}
        rm = [row(m_rows[g], r) for r in range(8)]
        rv = [row(v_rows[g], r) for r in range(8)]
        inverse = []
        for k in range(8):
            scale = lax.rsqrt(a[k, k])
            inverse.append(scale)
            for r in range(k + 1, 8):
                a[r, k] = a[r, k] * scale
            for c in range(k + 1, 8):
                for r in range(c, 8):
                    a[r, c] = a[r, c] - a[r, k] * a[c, k]
            rm[k] = rm[k] * scale
            rv[k] = rv[k] * scale
            for r in range(k + 1, 8):
                rm[r] = rm[r] - a[r, k] * rm[k]
                rv[r] = rv[r] - a[r, k] * rv[k]
        for i in range(g + 1, groups):
            factor = [jnp.broadcast_to(m_rows[i][:, lane : lane + 1], full) for lane in lanes]
            new_m, new_v = m_rows[i], v_rows[i]
            for k in range(8):
                factor[k] = factor[k] * inverse[k]
                for r in range(k + 1, 8):
                    factor[r] = factor[r] - factor[k] * a[r, k]
                new_m = new_m - factor[k] * rm[k]
                new_v = new_v - factor[k] * rv[k]
            m_rows[i], v_rows[i] = new_m, new_v
        top_m, top_v = rm[0], rv[0]
        for r in range(1, 8):
            top_m = jnp.where(sub == r, rm[r], top_m)
            top_v = jnp.where(sub == r, rv[r], top_v)
        m_rows[g], v_rows[g] = top_m, top_v
    return m_rows, v_rows


def eliminate_body(e_in, _, e_out, __):
    groups = range(TW // 8)
    m_rows = [e_in[8 * g : 8 * g + 8, :TW] for g in groups]
    v_rows = [e_in[8 * g : 8 * g + 8, TW:] for g in groups]
    m_rows, v_rows = eliminate(m_rows, v_rows, 0, TW // 8)
    r = lax.broadcasted_iota(jnp.int32, (8, TW), 0)
    c = lax.broadcasted_iota(jnp.int32, (8, TW), 1)
    for g in groups:
        e_out[8 * g : 8 * g + 8, :TW] = jnp.where(r + 8 * g <= c, m_rows[g], 0.0)
        e_out[8 * g : 8 * g + 8, TW:] = v_rows[g]


def eliminate_block(e, filed):
    return call(
        eliminate_body, [VMEM, ANY], [VMEM, ANY], [sds((TW, 2 * TW), F32), FILED], "eliminate", aliases={1: 1}
    )(e, pin(filed))


def eliminate_last(e, before):
    body = lambda e_in, _, e_out: eliminate_body(e_in, None, e_out, None)
    return call(body, [VMEM, ANY], VMEM, sds((TW, 2 * TW), F32), "eliminate", flops=RELAY_COST)(e, before)


def spread_body(b, e_in, s_in, v_in, s_ref, v_ref, e_out):
    lo, hi = b * TW, (b + 1) * TW
    s_ref[...] = s_in[...]
    if b == 0:
        v_ref[...] = jnp.zeros_like(v_ref)
    else:
        v_ref[...] = v_in[...]
    inv = e_in[:, TW:]
    s_ref[lo:hi, lo:hi] = e_in[:, :TW]
    v_ref[lo:hi, lo:hi] = inv
    if b > 0:
        v_ref[lo:hi, :lo] = hdot(inv, v_in[lo:hi, :lo], ((1,), (0,)))
    if hi < W:
        right = hdot(inv, s_in[lo:hi, hi:], ((1,), (0,)))
        s_ref[lo:hi, hi:] = right
        s_ref[hi:, hi:] -= hdot(right, right, ((0,), (0,)))
        s_ref[hi:, lo:hi] = jnp.zeros((W - hi, TW), F32)
        v_ref[hi:, :hi] -= hdot(right, v_ref[lo:hi, :hi], ((0,), (0,)))
        e_out[:, :TW] = s_ref[hi : hi + TW, hi : hi + TW]
        e_out[:, TW:] = unit()
    else:
        e_out[0] = s_ref[: W // 2, : W // 2]
        e_out[1] = s_ref[W // 2 :, W // 2 :]


def spread(b, e, s, v):
    return call(
        functools.partial(spread_body, b),
        [VMEM] * 3,
        [VMEM] * 3,
        [sds((W, W), F32), sds((W, W), F32), sds((TW, 2 * TW) if b < TJ - 1 else (2, W // 2, W // 2), F32)],
        "spread",
    )(e, s, v)


def masked(ref, flags, i, r):
    parts = []
    for j in range(TJ):
        block = ref[r * TH : (r + 1) * TH, j * TW : (j + 1) * TW]
        parts.append(jnp.where(flags[i * DEEP + r, j] > 0, block, jnp.zeros_like(block)))
    return jnp.concatenate(parts, 1)


def occupied(flags, row):
    count, starts = jnp.int32(0), [jnp.int32(0)] * TJ
    for j in range(TJ):
        for q in range(j + 1):
            starts[q] += jnp.where((flags[row, j] > 0) & (count == q), j * TW, 0)
        count += jnp.where(flags[row, j] > 0, 1, 0)
    return count, [pl.ds(pl.multiple_of(v, TW), TW) for v in starts]


DEEP = 2


def project_body(me, occ, panel, x_ref, a_ref, keep, give, c_ref):
    i = pl.program_id(0)

    @pl.when(i == 0)
    def _():
        c_ref[...] = jnp.zeros_like(c_ref)

    for r in range(DEEP):
        count, at = occupied(panel, i * DEEP + r)
        for k in range(1, TJ + 1):

            @pl.when((me[ROOT] == 0) & (count == k))
            def _(r=r, at=at[:k]):
                ah, al = split(jnp.concatenate([a_ref[r * TH : (r + 1) * TH, v] for v in at], 1))
                bh, bl = split(masked(x_ref, occ, i, r))
                ah_t, al_t = ah.T, al.T
                part = dot(jnp.concatenate([ah_t, al_t, ah_t], 1), jnp.concatenate([bh, bh, bl], 0))
                for q, v in enumerate(at):
                    c_ref[v, :] += part[q * TW : (q + 1) * TW]

    @pl.when(i == TI // DEEP - 1)
    def _():
        half = W // 2
        mine = pl.multiple_of(me[CORE] * half, half)
        keep[...] = c_ref[pl.ds(mine, half), :]
        give[...] = c_ref[pl.ds(half - mine, half), :]


def project(me, occ, panel, x, filed):
    block = pl.BlockSpec((DEEP * TH, W), lambda i, *_: (i, 0))
    whole = pl.BlockSpec((W // 2, W), lambda i, *_: (0, 0))
    return pl.pallas_call(
        project_body,
        grid_spec=pltpu.PrefetchScalarGridSpec(
            num_scalar_prefetch=3,
            grid=(TI // DEEP,),
            in_specs=[block, block],
            out_specs=[whole, whole],
            scratch_shapes=[pltpu.VMEM((W, W), F32)],
        ),
        out_shape=[sds((W // 2, W), F32)] * 2,
        compiler_params=params(40),
        cost_estimate=cost(0),
        name="project",
    )(me, occ, panel, in_hbm(x), in_hbm(filed))


def halve_body(me, a, b, own, one, two, three, total):
    total[...] = a[...] + b[...]
    h = W // 8
    for k, out in enumerate((own, one, two, three)):
        at = lax.rem(me[YPOS] + k, 4) * h
        out[...] = total[pl.ds(pl.multiple_of(at, h), h), :]


def add_and_cut(me, a, b):
    return call(
        halve_body,
        [SMEM, VMEM, VMEM],
        [VMEM] * 4,
        [sds((W // 8, W), F32)] * 4,
        "add_and_cut",
        [pltpu.VMEM((W // 2, W), F32)],
    )(me, a, b)


def solve_body(scale, me, v_ref, c_ref, high_ref, low_ref):
    v, h = v_ref[...], W // 2
    rows, cols = ((1,), (0,)), ((0,), (0,))
    top = hdot(v[:h, :h], c_ref[:h, :], rows)
    low = hdot(v[h:, :], c_ref[...], rows)
    coef = jnp.concatenate([hdot(v[:h, :h], top, cols) + hdot(v[h:, :h], low, cols), hdot(v[h:, h:], low, cols)], 0)
    coef = jnp.where(me[ROOT] > 0, -scale * v.T, coef)
    high_ref[...], low_ref[...] = split(coef)


def solve(scale, me, inv, proj):
    return call(
        functools.partial(solve_body, scale),
        [SMEM, VMEM, VMEM],
        [VMEM, VMEM],
        [sds((W, W), BF16)] * 2,
        "solve",
    )(me, inv, proj)


def finish_body(me, occ, panel, x_ref, a_ref, xh, xl, out_ref):
    i = pl.program_id(0)
    keep = 1 - me[ROOT]
    for r in range(DEEP):
        rows = slice(r * TH, (r + 1) * TH)
        count, at = occupied(panel, i * DEEP + r)
        for k in range(TJ + 1):

            @pl.when(count == k)
            def _(r=r, rows=rows, at=at[:k]):
                if at:
                    ah, al = split(jnp.concatenate([a_ref[rows, v] for v in at], 1))
                    high, low = [xh[v, :] for v in at], [xl[v, :] for v in at]
                    taken = dot(jnp.concatenate([ah, al, ah], 1), jnp.concatenate(high + high + low, 0))
                else:
                    taken = jnp.zeros((TH, W), F32)
                for j in range(TJ):
                    cols = slice(j * TW, (j + 1) * TW)
                    keep_tile = (occ[i * DEEP + r, j] * keep).astype(F32)
                    out_ref[rows, cols] = x_ref[rows, cols] * keep_tile - taken[:, cols]


def finish(me, occ, panel, x, filed, xh, xl):
    rows = TI * TH
    block = pl.BlockSpec((DEEP * TH, W), lambda i, *_: (i, 0))
    whole = pl.BlockSpec((W, W), lambda i, *_: (0, 0))
    return pl.pallas_call(
        finish_body,
        grid_spec=pltpu.PrefetchScalarGridSpec(
            num_scalar_prefetch=3,
            grid=(TI // DEEP,),
            in_specs=[block, block, whole, whole],
            out_specs=block,
        ),
        out_shape=sds((rows, W), F32),
        compiler_params=params(40),
        cost_estimate=cost(0),
        name="finish",
    )(me, occ, panel, in_hbm(x), in_hbm(filed), xh, xl)


def shards(snapshots, tiles):
    col = lax.axis_index("col")
    _, y, core = site(lax.axis_index("row"))
    root = col == 0
    hop = jnp.where(core == 0, col, (4 - col) % 4)
    scale = math.sqrt(snapshots.shape[0] * lax.axis_size("row"))
    me = jnp.stack([root.astype(jnp.int32), hop, core, y, col]).astype(jnp.int32)
    state = {"x": snapshots, "panel": tiles}
    flags = shifted(tiles, "col")

    def ring(start, stop, filed, beside=None):
        got = [None] * LAG
        steps = stop - start + 3 * LAG
        for s in range(steps):
            last = s >= steps - LAG
            others = flags if start == 0 and s == LAG else []
            filed, send, seen = relay(s, start, stop, last, me, state["panel"], others, state["x"], got[s % LAG], filed)
            if others:
                state["panel"] = seen
            if not last:
                got[s % LAG] = ring_step(send)
            if beside is not None:
                filed = beside(s, filed)
        return filed

    def gram_stage(name, filed):
        if name == "load":
            state["x"] = load(snapshots, filed)
        elif name == "parts":
            keep, give, filed = gram_part(me, tiles, state["x"], filed)
            state["v"] = [keep, lax.ppermute(give, "row", SWAP)]
        elif name == "core":
            own, one, two, three, filed = add_cut(me, state["v"], filed)
            sent = [lax.ppermute(p, "row", SHIFT["y"][d]) for d, p in ((1, one), (2, two), (3, three))]
            state["v"] = [own] + sent
        elif name == "y":
            v, filed = add_parts(state["v"], filed)
            state["v"] = [v] + shifted(v, "z")
        elif name == "z":
            v, filed = add_parts(state["v"], filed)
            state["v"] = [v] + shifted(v, "col")
        elif name == "col":
            v, filed = choose(me, state["v"], filed)
            state["v"] = [v] + shifted(v, "y")
        elif name == "stack":
            v, filed = stack(me, state["v"], filed)
            state["v"] = [v, lax.ppermute(v, "row", SWAP)]
        elif name == "unpack":
            state["s"], state["e"], state["over"], filed = unpack(me, *state["v"], filed)
            state["inv"] = state["s"]
        elif name[0] == "e":
            state["e"], filed = eliminate_block(state["e"], filed)
        else:
            state["s"], state["inv"], state["e"] = spread(int(name[1]), state["e"], state["s"], state["inv"])
        return filed

    plan = {1: ["load"], 3: ["parts"], 4: ["core"], 6: ["y"], 7: ["z"], 9: ["col"], 10: ["stack"], 11: ["unpack", "e0", "s0"]}
    plan.update({12: ["e1", "s1"], 13: ["e2", "s2"]})

    def beside(s, filed):
        for name in plan.get(s, []):
            filed = gram_stage(name, filed)
        return filed

    filed = ring(0, SHORT, None, beside)
    filed = lax.cond(state["over"][0, 0] > 0.5, lambda f: ring(SHORT, CHUNKS, f), lambda f: f, filed)
    panel = state["panel"]
    keep, give = project(me, tiles, panel, snapshots, filed)
    state["e"] = eliminate_last(state["e"], keep)
    proj = row_sum(me, keep, give, state["e"])
    gram_stage("s3", filed)
    xh, xl = solve(scale, me, state["inv"], proj)
    out = finish(me, tiles, panel, snapshots, filed, xh, xl)
    return state["e"], out


def solution(mesh):
    placed = (P("row", "col"), P("row", "col"))
    return jax.shard_map(shards, mesh=mesh, in_specs=placed, out_specs=(P(), P("row", "col")), check_vma=False)
```

```python
import functools
import math

import jax
import jax.numpy as jnp
from jax import lax
from jax.experimental import pallas as pl
from jax.experimental.pallas import tpu as pltpu
from jax.sharding import PartitionSpec as P

TH = 512
TW = 128
TI = 8
TJ = 4
SLOTS = TI * TJ
PAIR = 2
LAG = 2
CHUNKS = SLOTS // PAIR
SHORT = 12
W = TJ * TW
F32 = jnp.float32
RELAY_COST = 5 * 10**9


def cost(flops):
    return pl.CostEstimate(flops=flops, bytes_accessed=0, transcendentals=0)

BF16 = jnp.bfloat16


def params(limit=16):
    return pltpu.CompilerParams(vmem_limit_bytes=limit * 1024 * 1024)


def sds(shape, dtype):
    return jax.ShapeDtypeStruct(shape, dtype)


def site(r):
    return r // 8, (r // 2) % 4, r % 2


def row_of(z, y, c):
    return (z % 4) * 8 + (y % 4) * 2 + c


def row_perm(f):
    return [(r, row_of(*f(*site(r)))) for r in range(32)]


SWAP = row_perm(lambda z, y, c: (z, y, 1 - c))
SHIFT = {
    "y": [row_perm(lambda z, y, c, d=d: (z, y + d, c)) for d in range(4)],
    "z": [row_perm(lambda z, y, c, d=d: (z + d, y, c)) for d in range(4)],
}
RING = [(r * 4 + x, r * 4 + (x + (1 if r % 2 == 0 else 3)) % 4) for r in range(32) for x in range(4)]


def ring_step(x):
    return lax.ppermute(x, ("row", "col"), RING)


def gather4(x, axis, me):
    h = x.shape[0]
    out = jnp.zeros((4 * h, x.shape[1]), x.dtype)
    for d in range(4):
        got = x if d == 0 else lax.ppermute(x, "row", SHIFT[axis][d])
        out = lax.dynamic_update_slice_in_dim(out, got, lax.rem(me + 4 - d, 4) * h, 0)
    return out


def core_gather(x, c):
    got = lax.ppermute(x, "row", SWAP)
    first = jnp.where(c == 0, x, got)
    second = jnp.where(c == 0, got, x)
    return jnp.concatenate([first, second], 0)


def row_sum(me, keep, give, beside):
    _, y, c = site(lax.axis_index("row"))
    own, one, two, three = add_and_cut(me, keep, lax.ppermute(give, "row", SWAP))
    sent = [lax.ppermute(p, "row", SHIFT["y"][d]) for d, p in ((1, one), (2, two), (3, three))]
    v = add_beside([own] + sent, own)
    v = add_beside([v] + shifted(v, "z"), beside)
    return core_gather(gather4(v, "y", y), c)


def shifted(x, axis):
    if axis == "col":
        return [lax.ppermute(x, "col", [(i, (i + d) % 4) for i in range(4)]) for d in (1, 2, 3)]
    return [lax.ppermute(x, "row", SHIFT[axis][d]) for d in (1, 2, 3)]


ANY = pl.BlockSpec(memory_space=pl.ANY)
VMEM = pl.BlockSpec(memory_space=pltpu.VMEM)
SMEM = pl.BlockSpec(memory_space=pltpu.SMEM)
ROOT, HOP, CORE, YPOS, COL = range(5)
UPPER = [(i, j) for i in range(TJ) for j in range(i, TJ)]
BLOCKS = len(UPPER) // 2 * TW
HALF = BLOCKS + 32
QUARTER = HALF // 4


def kept(shape):
    return pltpu.VMEM(shape, F32)


FILED = kept((TI * TH, W))


def pin(x):
    return pltpu.with_memory_space_constraint(x, pltpu.VMEM)


def in_hbm(x):
    return pltpu.with_memory_space_constraint(x, pltpu.HBM)


def split(x):
    high = x.astype(BF16)
    return high, (x - high.astype(F32)).astype(BF16)


def dot(a, b):
    return jnp.dot(a, b, preferred_element_type=F32)


def hdot(a, b, dims):
    return lax.dot_general(a, b, (dims, ((), ())), precision=lax.Precision.HIGHEST, preferred_element_type=F32)


def call(body, ins, outs, shapes, name, scratch=(), aliases=None, limit=16, flops=0):
    return pl.pallas_call(
        body,
        in_specs=ins,
        out_specs=outs,
        out_shape=shapes,
        scratch_shapes=list(scratch),
        input_output_aliases=aliases or {},
        compiler_params=params(limit),
        cost_estimate=cost(flops),
        name=name,
    )


def find(full, wanted):
    seen, place, found = jnp.int32(0), jnp.int32(0), jnp.int32(0)
    for t in range(SLOTS):
        hit = jnp.where((full[t] > 0) & (seen == wanted), 1, 0)
        place += hit * t
        found += hit
        seen += full[t]
    return place, found > 0


def relay_body(step, start, stop, fresh, choosing, last, staged, me, own, *refs):
    refs = list(refs)
    root = me[ROOT] > 0
    others = [refs.pop(0) for _ in range(3)] if choosing else []
    x_ref = refs.pop(0)
    got = None if step < LAG else refs.pop(0)
    if not fresh:
        refs.pop(0)
    filed = refs.pop(0)
    send = None if last else refs.pop(0)
    seen = refs.pop(0) if choosing else None
    (sem,) = refs
    full = []
    for t in range(SLOTS):
        at = t % TI, t // TI
        flag = own[at]
        for d, other in enumerate(others, 1):
            flag = jnp.where(me[COL] == d, other[at], flag)
        if seen is not None:
            seen[at] = flag
        full.append(flag)
    chunk = start + step - me[HOP] * LAG
    live = (chunk >= start) & (chunk < stop)

    def each(act, into_send, into_filed):
        for e in range(PAIR):
            place, found = places[e]
            rows = pl.ds(pl.multiple_of((place % TI) * TH, TH), TH)
            cols = pl.ds(pl.multiple_of((place // TI) * TW, TW), TW)
            part = pl.ds(e * TH, TH)

            def move(src, e=e, rows=rows, cols=cols, part=part):
                if into_filed:
                    act(pltpu.make_async_copy(src, filed.at[rows, cols], sem.at[2 * e]))
                if into_send:
                    act(pltpu.make_async_copy(src, send.at[part, :], sem.at[2 * e + 1]))

            @pl.when(found & live & root)
            def _(move=move, rows=rows, cols=cols, part=part):
                move(send.at[part, :] if staged and into_filed else x_ref.at[rows, cols])

            if got is not None:

                @pl.when(found & live & jnp.logical_not(root))
                def _(move=move, part=part):
                    move(got.at[part, :])

    places = [find(full, chunk * PAIR + e) for e in range(PAIR)]
    for into_send, into_filed in ((True, False), (False, True)) if staged else ((send is not None, True),):
        each(lambda c: c.start(), into_send, into_filed)
        each(lambda c: c.wait(), into_send, into_filed)


def relay(step, start, stop, last, me, own, others, x, got, filed):
    staged = start == 0 and step < LAG
    ins, args = [SMEM] * (2 + len(others)) + [ANY], [me, own, *others, in_hbm(x) if staged else pin(x)]
    if step >= LAG:
        ins.append(ANY)
        args.append(got)
    aliases = {}
    if filed is not None:
        aliases = {len(args): 0}
        ins.append(ANY)
        args.append(pin(filed))
    shapes, outs = [FILED], [ANY]
    if not last:
        shapes.append(kept((PAIR * TH, TW)))
        outs.append(ANY)
    if others:
        shapes.append(sds((TI, TJ), jnp.int32))
        outs.append(SMEM)
    out = list(
        call(
            functools.partial(relay_body, step, start, stop, filed is None, bool(others), last, staged),
            ins,
            outs,
            shapes,
            "relay",
            [pltpu.SemaphoreType.DMA((2 * PAIR,))],
            aliases,
            4,
            RELAY_COST,
        )(*args)
    )
    filed = out.pop(0)
    send = None if last else out.pop(0)
    return filed, send, out.pop(0) if others else None


def load_body(x_ref, _, out, sem):
    copies = [
        pltpu.make_async_copy(x_ref.at[pl.ds(i * TH, TH), :], out.at[pl.ds(i * TH, TH), :], sem.at[i]) for i in range(TI)
    ]
    for c in copies:
        c.start()
    for c in copies:
        c.wait()


def load(x, before):
    return call(load_body, [ANY, ANY], ANY, FILED, "load", [pltpu.SemaphoreType.DMA((TI,))])(in_hbm(x), before)


def gram_body(me, occ, x_ref, filed_in, keep, give, filed, gram_ref, cross_ref):
    i = pl.program_id(0)

    @pl.when(i == 0)
    def _():
        gram_ref[...] = jnp.zeros_like(gram_ref)
        cross_ref[...] = jnp.zeros_like(cross_ref)

    @pl.when(me[ROOT] > 0)
    def _():
        x = jnp.concatenate([x_ref[:, j * TW : (j + 1) * TW] * occ[i, j].astype(F32) for j in range(TJ)], 1)
        high, low = split(x)
        h = W // 2
        high_t, low_t = high.T, low.T
        gram_ref[:h, :] += dot(high_t[:h], high) + dot(low_t[:h], low)
        gram_ref[h:, h:] += dot(high_t[h:], high[:, h:]) + dot(low_t[h:], low[:, h:])
        cross_ref[...] += dot(high_t, low)

    @pl.when(i == TI - 1)
    def _():
        full = jnp.int32(0)
        for t in range(SLOTS):
            full += occ[t % TI, t // TI]
        over = jnp.where(full > SHORT * PAIR, 1.0, 0.0)
        keep[BLOCKS:, :] = jnp.full((HALF - BLOCKS, TW), over, F32)
        give[BLOCKS:, :] = jnp.full((HALF - BLOCKS, TW), over, F32)
        for b, (r, q) in enumerate(UPPER):
            rows, cols = slice(r * TW, (r + 1) * TW), slice(q * TW, (q + 1) * TW)
            block = gram_ref[rows, cols] + cross_ref[rows, cols] + cross_ref[cols, rows].T
            part, at = divmod(b * TW, BLOCKS)
            mine = me[CORE] == part

            @pl.when(mine)
            def _(block=block, at=at):
                keep[at : at + TW, :] = block

            @pl.when(jnp.logical_not(mine))
            def _(block=block, at=at):
                give[at : at + TW, :] = block


def gram_part(me, occ, x, filed):
    whole = pl.BlockSpec((HALF, TW), lambda i, *_: (0, 0))
    return pl.pallas_call(
        gram_body,
        grid_spec=pltpu.PrefetchScalarGridSpec(
            num_scalar_prefetch=2,
            grid=(TI,),
            in_specs=[pl.BlockSpec((TH, W), lambda i, me, occ: (i * me[ROOT], 0)), ANY],
            out_specs=[whole, whole, ANY],
            scratch_shapes=[pltpu.VMEM((W, W), F32), pltpu.VMEM((W, W), F32)],
        ),
        out_shape=[sds((HALF, TW), F32), sds((HALF, TW), F32), FILED],
        input_output_aliases={3: 2},
        compiler_params=params(24),
        cost_estimate=cost(0),
        name="gram_part",
    )(me, occ, pin(x), pin(filed))


def add_body(*refs):
    ins, (_, out, _) = refs[:-3], refs[-3:]
    total = ins[0][...]
    for r in ins[1:]:
        total = total + r[...]
    out[...] = total


def add_parts(parts, filed):
    n = len(parts)
    return call(
        add_body,
        [VMEM] * n + [ANY],
        [VMEM, ANY],
        [sds(parts[0].shape, F32), FILED],
        "add_parts",
        aliases={n: 1},
    )(*parts, pin(filed))


def add_beside_body(*refs):
    add_body(*refs[:-2], None, refs[-1], None)


def add_beside(parts, beside):
    return call(add_beside_body, [VMEM] * len(parts) + [ANY], VMEM, sds(parts[0].shape, F32), "add_beside")(*parts, beside)


def add_cut_body(me, a, b, _, own, one, two, three, __, total):
    total[...] = a[...] + b[...]
    for k, out in enumerate((own, one, two, three)):
        at = lax.rem(me[YPOS] + k, 4) * QUARTER
        out[...] = total[pl.ds(pl.multiple_of(at, 8), QUARTER), :]


def add_cut(me, parts, filed):
    return call(
        add_cut_body,
        [SMEM] + [VMEM] * 2 + [ANY],
        [VMEM] * 4 + [ANY],
        [sds((QUARTER, TW), F32)] * 4 + [FILED],
        "add_cut",
        [pltpu.VMEM((HALF, TW), F32)],
        {3: 4},
    )(me, *parts, pin(filed))


def choose_body(me, a, b, c, d, _, out, __):
    for k, ref in enumerate((a, b, c, d)):

        @pl.when(me[COL] == k)
        def _(ref=ref):
            out[...] = ref[...]


def choose(me, parts, filed):
    return call(
        choose_body,
        [SMEM] + [VMEM] * 4 + [ANY],
        [VMEM, ANY],
        [sds((QUARTER, TW), F32), FILED],
        "choose",
        aliases={5: 1},
    )(me, *parts, pin(filed))


def stack_body(me, a, b, c, d, _, out, __):
    for k, ref in enumerate((a, b, c, d)):
        at = lax.rem(me[YPOS] + 4 - k, 4) * QUARTER
        out[pl.ds(pl.multiple_of(at, 8), QUARTER), :] = ref[...]


def stack(me, parts, filed):
    return call(
        stack_body,
        [SMEM] + [VMEM] * 4 + [ANY],
        [VMEM, ANY],
        [sds((HALF, TW), F32), FILED],
        "stack",
        aliases={5: 1},
    )(me, *parts, pin(filed))


def unpack_body(me, mine, other, _, s_ref, e_ref, over_ref, __):
    over_ref[...] = mine[BLOCKS : BLOCKS + 8, :]
    s_ref[...] = jnp.zeros_like(s_ref)
    for b, (r, q) in enumerate(UPPER):
        part, at = divmod(b * TW, BLOCKS)
        block = jnp.where(me[CORE] == part, mine[at : at + TW, :], other[at : at + TW, :])
        s_ref[r * TW : (r + 1) * TW, q * TW : (q + 1) * TW] = block
        if b == 0:
            e_ref[:, :TW] = block
    e_ref[:, TW:] = unit()


def unpack(me, mine, other, filed):
    return call(
        unpack_body,
        [SMEM, VMEM, VMEM, ANY],
        [VMEM, VMEM, VMEM, ANY],
        [sds((W, W), F32), sds((TW, 2 * TW), F32), sds((8, TW), F32), FILED],
        "unpack",
        aliases={3: 3},
    )(me, mine, other, pin(filed))


def unit():
    r = lax.broadcasted_iota(jnp.int32, (TW, TW), 0)
    c = lax.broadcasted_iota(jnp.int32, (TW, TW), 1)
    return jnp.where(r == c, 1.0, 0.0).astype(F32)


def eliminate(m_rows, v_rows, start, stop):
    groups = len(m_rows)
    full = (8, m_rows[0].shape[1])
    sub = lax.broadcasted_iota(jnp.int32, full, 0)

    def row(x, r):
        return jnp.broadcast_to(x[r : r + 1, :], full)

    for g in range(start, stop):
        lanes = [8 * g + k for k in range(8)]
        columns = [jnp.broadcast_to(m_rows[g][:, lane : lane + 1], full) for lane in lanes]
        a = {(r, k): row(columns[k], r) for k in range(8) for r in range(k, 8)}
        rm = [row(m_rows[g], r) for r in range(8)]
        rv = [row(v_rows[g], r) for r in range(8)]
        inverse = []
        for k in range(8):
            scale = lax.rsqrt(a[k, k])
            inverse.append(scale)
            for r in range(k + 1, 8):
                a[r, k] = a[r, k] * scale
            for c in range(k + 1, 8):
                for r in range(c, 8):
                    a[r, c] = a[r, c] - a[r, k] * a[c, k]
            rm[k] = rm[k] * scale
            rv[k] = rv[k] * scale
            for r in range(k + 1, 8):
                rm[r] = rm[r] - a[r, k] * rm[k]
                rv[r] = rv[r] - a[r, k] * rv[k]
        for i in range(g + 1, groups):
            factor = [jnp.broadcast_to(m_rows[i][:, lane : lane + 1], full) for lane in lanes]
            new_m, new_v = m_rows[i], v_rows[i]
            for k in range(8):
                factor[k] = factor[k] * inverse[k]
                for r in range(k + 1, 8):
                    factor[r] = factor[r] - factor[k] * a[r, k]
                new_m = new_m - factor[k] * rm[k]
                new_v = new_v - factor[k] * rv[k]
            m_rows[i], v_rows[i] = new_m, new_v
        top_m, top_v = rm[0], rv[0]
        for r in range(1, 8):
            top_m = jnp.where(sub == r, rm[r], top_m)
            top_v = jnp.where(sub == r, rv[r], top_v)
        m_rows[g], v_rows[g] = top_m, top_v
    return m_rows, v_rows


def eliminate_body(e_in, _, e_out, __):
    groups = range(TW // 8)
    m_rows = [e_in[8 * g : 8 * g + 8, :TW] for g in groups]
    v_rows = [e_in[8 * g : 8 * g + 8, TW:] for g in groups]
    m_rows, v_rows = eliminate(m_rows, v_rows, 0, TW // 8)
    r = lax.broadcasted_iota(jnp.int32, (8, TW), 0)
    c = lax.broadcasted_iota(jnp.int32, (8, TW), 1)
    for g in groups:
        e_out[8 * g : 8 * g + 8, :TW] = jnp.where(r + 8 * g <= c, m_rows[g], 0.0)
        e_out[8 * g : 8 * g + 8, TW:] = v_rows[g]


def eliminate_block(e, filed):
    return call(
        eliminate_body, [VMEM, ANY], [VMEM, ANY], [sds((TW, 2 * TW), F32), FILED], "eliminate", aliases={1: 1}
    )(e, pin(filed))


def eliminate_last(e, before):
    body = lambda e_in, _, e_out: eliminate_body(e_in, None, e_out, None)
    return call(body, [VMEM, ANY], VMEM, sds((TW, 2 * TW), F32), "eliminate", flops=RELAY_COST)(e, before)


def spread_body(b, e_in, s_in, v_in, s_ref, v_ref, e_out):
    lo, hi = b * TW, (b + 1) * TW
    s_ref[...] = s_in[...]
    if b == 0:
        v_ref[...] = jnp.zeros_like(v_ref)
    else:
        v_ref[...] = v_in[...]
    inv = e_in[:, TW:]
    s_ref[lo:hi, lo:hi] = e_in[:, :TW]
    v_ref[lo:hi, lo:hi] = inv
    if b > 0:
        v_ref[lo:hi, :lo] = hdot(inv, v_in[lo:hi, :lo], ((1,), (0,)))
    if hi < W:
        right = hdot(inv, s_in[lo:hi, hi:], ((1,), (0,)))
        s_ref[lo:hi, hi:] = right
        s_ref[hi:, hi:] -= hdot(right, right, ((0,), (0,)))
        s_ref[hi:, lo:hi] = jnp.zeros((W - hi, TW), F32)
        v_ref[hi:, :hi] -= hdot(right, v_ref[lo:hi, :hi], ((0,), (0,)))
        e_out[:, :TW] = s_ref[hi : hi + TW, hi : hi + TW]
        e_out[:, TW:] = unit()
    else:
        e_out[0] = s_ref[: W // 2, : W // 2]
        e_out[1] = s_ref[W // 2 :, W // 2 :]


def spread(b, e, s, v):
    return call(
        functools.partial(spread_body, b),
        [VMEM] * 3,
        [VMEM] * 3,
        [sds((W, W), F32), sds((W, W), F32), sds((TW, 2 * TW) if b < TJ - 1 else (2, W // 2, W // 2), F32)],
        "spread",
    )(e, s, v)


def masked(ref, flags, i, r):
    parts = []
    for j in range(TJ):
        block = ref[r * TH : (r + 1) * TH, j * TW : (j + 1) * TW]
        parts.append(jnp.where(flags[i * DEEP + r, j] > 0, block, jnp.zeros_like(block)))
    return jnp.concatenate(parts, 1)


def occupied(flags, row):
    count, starts = jnp.int32(0), [jnp.int32(0)] * TJ
    for j in range(TJ):
        for q in range(j + 1):
            starts[q] += jnp.where((flags[row, j] > 0) & (count == q), j * TW, 0)
        count += jnp.where(flags[row, j] > 0, 1, 0)
    return count, [pl.ds(pl.multiple_of(v, TW), TW) for v in starts]


DEEP = 2


def project_body(me, occ, panel, x_ref, a_ref, keep, give, c_ref):
    i = pl.program_id(0)

    @pl.when(i == 0)
    def _():
        c_ref[...] = jnp.zeros_like(c_ref)

    for r in range(DEEP):
        count, at = occupied(panel, i * DEEP + r)
        for k in range(1, TJ + 1):

            @pl.when((me[ROOT] == 0) & (count == k))
            def _(r=r, at=at[:k]):
                ah, al = split(jnp.concatenate([a_ref[r * TH : (r + 1) * TH, v] for v in at], 1))
                bh, bl = split(masked(x_ref, occ, i, r))
                ah_t, al_t = ah.T, al.T
                part = dot(jnp.concatenate([ah_t, al_t, ah_t], 1), jnp.concatenate([bh, bh, bl], 0))
                for q, v in enumerate(at):
                    c_ref[v, :] += part[q * TW : (q + 1) * TW]

    @pl.when(i == TI // DEEP - 1)
    def _():
        half = W // 2
        mine = pl.multiple_of(me[CORE] * half, half)
        keep[...] = c_ref[pl.ds(mine, half), :]
        give[...] = c_ref[pl.ds(half - mine, half), :]


def project(me, occ, panel, x, filed):
    block = pl.BlockSpec((DEEP * TH, W), lambda i, *_: (i, 0))
    whole = pl.BlockSpec((W // 2, W), lambda i, *_: (0, 0))
    return pl.pallas_call(
        project_body,
        grid_spec=pltpu.PrefetchScalarGridSpec(
            num_scalar_prefetch=3,
            grid=(TI // DEEP,),
            in_specs=[block, block],
            out_specs=[whole, whole],
            scratch_shapes=[pltpu.VMEM((W, W), F32)],
        ),
        out_shape=[sds((W // 2, W), F32)] * 2,
        compiler_params=params(40),
        cost_estimate=cost(0),
        name="project",
    )(me, occ, panel, in_hbm(x), in_hbm(filed))


def halve_body(me, a, b, own, one, two, three, total):
    total[...] = a[...] + b[...]
    h = W // 8
    for k, out in enumerate((own, one, two, three)):
        at = lax.rem(me[YPOS] + k, 4) * h
        out[...] = total[pl.ds(pl.multiple_of(at, h), h), :]


def add_and_cut(me, a, b):
    return call(
        halve_body,
        [SMEM, VMEM, VMEM],
        [VMEM] * 4,
        [sds((W // 8, W), F32)] * 4,
        "add_and_cut",
        [pltpu.VMEM((W // 2, W), F32)],
    )(me, a, b)


def solve_body(scale, me, v_ref, c_ref, high_ref, low_ref):
    v, h = v_ref[...], W // 2
    rows, cols = ((1,), (0,)), ((0,), (0,))
    top = hdot(v[:h, :h], c_ref[:h, :], rows)
    low = hdot(v[h:, :], c_ref[...], rows)
    coef = jnp.concatenate([hdot(v[:h, :h], top, cols) + hdot(v[h:, :h], low, cols), hdot(v[h:, h:], low, cols)], 0)
    coef = jnp.where(me[ROOT] > 0, -scale * v.T, coef)
    high_ref[...], low_ref[...] = split(coef)


def solve(scale, me, inv, proj):
    return call(
        functools.partial(solve_body, scale),
        [SMEM, VMEM, VMEM],
        [VMEM, VMEM],
        [sds((W, W), BF16)] * 2,
        "solve",
    )(me, inv, proj)


def finish_body(me, occ, panel, x_ref, a_ref, xh, xl, out_ref):
    i = pl.program_id(0)
    keep = 1 - me[ROOT]
    for r in range(DEEP):
        rows = slice(r * TH, (r + 1) * TH)
        count, at = occupied(panel, i * DEEP + r)
        for k in range(TJ + 1):

            @pl.when(count == k)
            def _(r=r, rows=rows, at=at[:k]):
                if at:
                    ah, al = split(jnp.concatenate([a_ref[rows, v] for v in at], 1))
                    high, low = [xh[v, :] for v in at], [xl[v, :] for v in at]
                    taken = dot(jnp.concatenate([ah, al, ah], 1), jnp.concatenate(high + high + low, 0))
                else:
                    taken = jnp.zeros((TH, W), F32)
                for j in range(TJ):
                    cols = slice(j * TW, (j + 1) * TW)
                    keep_tile = (occ[i * DEEP + r, j] * keep).astype(F32)
                    out_ref[rows, cols] = x_ref[rows, cols] * keep_tile - taken[:, cols]


def finish(me, occ, panel, x, filed, xh, xl):
    rows = TI * TH
    block = pl.BlockSpec((DEEP * TH, W), lambda i, *_: (i, 0))
    whole = pl.BlockSpec((W, W), lambda i, *_: (0, 0))
    return pl.pallas_call(
        finish_body,
        grid_spec=pltpu.PrefetchScalarGridSpec(
            num_scalar_prefetch=3,
            grid=(TI // DEEP,),
            in_specs=[block, block, whole, whole],
            out_specs=block,
        ),
        out_shape=sds((rows, W), F32),
        compiler_params=params(40),
        cost_estimate=cost(0),
        name="finish",
    )(me, occ, panel, in_hbm(x), in_hbm(filed), xh, xl)


def shards(snapshots, tiles):
    col = lax.axis_index("col")
    _, y, core = site(lax.axis_index("row"))
    root = col == 0
    hop = jnp.where(core == 0, col, (4 - col) % 4)
    scale = math.sqrt(snapshots.shape[0] * lax.axis_size("row"))
    me = jnp.stack([root.astype(jnp.int32), hop, core, y, col]).astype(jnp.int32)
    state = {"x": snapshots, "panel": tiles}
    flags = shifted(tiles, "col")

    def ring(start, stop, filed, beside=None):
        got = [None] * LAG
        steps = stop - start + 3 * LAG
        for s in range(steps):
            last = s >= steps - LAG
            others = flags if start == 0 and s == 1 else []
            filed, send, seen = relay(s, start, stop, last, me, state["panel"], others, state["x"], got[s % LAG], filed)
            if others:
                state["panel"] = seen
            if not last:
                got[s % LAG] = ring_step(send)
            if beside is not None:
                filed = beside(s, filed)
        return filed

    def gram_stage(name, filed):
        if name == "load":
            state["x"] = load(snapshots, filed)
        elif name == "parts":
            keep, give, filed = gram_part(me, tiles, state["x"], filed)
            state["v"] = [keep, lax.ppermute(give, "row", SWAP)]
        elif name == "core":
            own, one, two, three, filed = add_cut(me, state["v"], filed)
            sent = [lax.ppermute(p, "row", SHIFT["y"][d]) for d, p in ((1, one), (2, two), (3, three))]
            state["v"] = [own] + sent
        elif name == "y":
            v, filed = add_parts(state["v"], filed)
            state["v"] = [v] + shifted(v, "z")
        elif name == "z":
            v, filed = add_parts(state["v"], filed)
            state["v"] = [v] + shifted(v, "col")
        elif name == "col":
            v, filed = choose(me, state["v"], filed)
            state["v"] = [v] + shifted(v, "y")
        elif name == "stack":
            v, filed = stack(me, state["v"], filed)
            state["v"] = [v, lax.ppermute(v, "row", SWAP)]
        elif name == "unpack":
            state["s"], state["e"], state["over"], filed = unpack(me, *state["v"], filed)
            state["inv"] = state["s"]
        elif name[0] == "e":
            state["e"], filed = eliminate_block(state["e"], filed)
        else:
            state["s"], state["inv"], state["e"] = spread(int(name[1]), state["e"], state["s"], state["inv"])
        return filed

    plan = {1: ["load"], 3: ["parts"], 4: ["core"], 6: ["y"], 7: ["z"], 9: ["col"], 10: ["stack"], 11: ["unpack", "e0", "s0"]}
    plan.update({12: ["e1", "s1"], 13: ["e2", "s2"]})

    def beside(s, filed):
        for name in plan.get(s, []):
            filed = gram_stage(name, filed)
        return filed

    filed = ring(0, SHORT, None, beside)
    filed = lax.cond(state["over"][0, 0] > 0.5, lambda f: ring(SHORT, CHUNKS, f), lambda f: f, filed)
    panel = state["panel"]
    keep, give = project(me, tiles, panel, snapshots, filed)
    state["e"] = eliminate_last(state["e"], keep)
    proj = row_sum(me, keep, give, state["e"])
    gram_stage("s3", filed)
    xh, xl = solve(scale, me, state["inv"], proj)
    out = finish(me, tiles, panel, snapshots, filed, xh, xl)
    return state["e"], out


def solution(mesh):
    placed = (P("row", "col"), P("row", "col"))
    return jax.shard_map(shards, mesh=mesh, in_specs=placed, out_specs=(P(), P("row", "col")), check_vma=False)
```
